32 devices in a mesh: ctx: 8 (over y, x, core), tp: 4 (over z).
Axes of the slice: x: 2, y: 2, z: 4, core: 2. Of those that a mesh axis runs over, the one named last changes fastest.
Arguments:
- residual_in: bfloat16 [2, 2048, 4096], P(None, 'ctx', 'tp'), may hold values from -6 to 6
- mr_qkv: bfloat16 [2, 2048, 3, 4096], P(None, 'ctx', None, 'tp'), may hold values from -6 to 6
- mr_short_w: float32 [3, 3, 4096], P(None, None, 'tp'), may hold values from -3.5 to 3.5
- mr_filter: bfloat16 [128, 4096], P(None, 'tp'), may hold values from -0.5 to 0.5
- mr_skip: float32 [4096], P('tp'), may hold values from -4 to 4
- mr_out_w: bfloat16 [4096, 4096], P('tp', 'ctx'), may hold values from -0.09375 to 0.09375
- lr_gain: float32 [4096], replicated, may hold values from 0.1 to 1.9
- lr_in_w: bfloat16 [4096, 3, 4096], P(None, None, 'tp'), may hold values from -0.09375 to 0.09375
- lr_short_w: float32 [3, 3, 4096], P(None, None, 'tp'), may hold values from -3.5 to 3.5
- lr_rate: float32 [16, 4096], P(None, 'tp'), may hold values from 0 to 1, as said below
- lr_res: float32 [16, 4096], P(None, 'tp'), may hold values from -3 to 3
- lr_skip: float32 [4096], P('tp'), may hold values from -4 to 4
- lr_out_w: bfloat16 [4096, 4096], P('tp', 'ctx'), may hold values from -0.09375 to 0.09375
Outputs:
- residual_out: bfloat16 [2, 2048, 4096], P(None, 'ctx', 'tp')
The draws below stay inside these ranges and needn't reach their ends.
Inputs may be any that keep to these rules, and one draw needn't show every extreme that they name: `lr_rate`: each rate lies between 0.1 / 2048 and 1 / 20.
All inputs are finite; a program needn't handle non-finite values.
Results may differ from the reference program's by a relative error of at most 0.034.
Values may be sent and summed in bfloat16 or wider, within the bound.
No kernel may reach another device: no remote copies, remote signals or barrier semaphores. Data moves between devices by JAX's collectives and lax.ppermute only.
A program may use at most 192 MiB of HBM per device.

```python
import math
import jax
import jax.numpy as jnp
from jax import lax

D = 4096
MR_TAPS = 128
STATE = 16
SHORT = 3
SEQS = 2
LENGTH = 2048
N_TP = 4


def draw_lr_rate(key, part):
    lowest = math.log(0.1 / LENGTH)
    return jnp.exp(jax.random.uniform(key, (STATE, D), jnp.float32, lowest, math.log(1.0 / 30.0))).astype(jnp.float32)


def level_of(rng, dims, cuts, smallest, largest):
    def one(position, parts):
        heights = jax.random.uniform(jax.random.fold_in(jax.random.fold_in(rng, 6), position), (parts,), jnp.float32, smallest / len(cuts), largest / len(cuts))
        return jnp.repeat(jnp.exp(heights), dims[position] // parts).reshape((-1,) + (1,) * (len(dims) - position - 1))

    level = one(*cuts[0])
    for cut in cuts[1:]:
        level = level * one(*cut)
    return level


def noise(own_key, dims, scale, bound, cuts=(), held_as=jnp.bfloat16):
    gain = level_of(own_key, dims, cuts, -0.22, 0.18) if cuts else 1.0
    values = jax.random.normal(own_key, dims, jnp.float32) * scale * gain
    return jnp.minimum(jnp.maximum(values, -bound), bound).astype(held_as)


def setup_inputs(seed: int = 0) -> dict:
    arg_keys = jax.random.split(jax.random.key(seed), 14)
    return {
        "residual_in": noise(arg_keys[0], (SEQS, LENGTH, D), 1.0, 6.0, ((1, 8), (2, 4))),
        "mr_qkv": noise(arg_keys[1], (SEQS, LENGTH, 3, D), 1.0, 6.0, ((1, 8), (3, 4))),
        "mr_short_w": noise(arg_keys[2], (SHORT, 3, D), SHORT ** -0.5, 3.5, ((2, 4),), jnp.float32),
        "mr_filter": noise(arg_keys[3], (MR_TAPS, D), MR_TAPS ** -0.5, 0.5, ((1, 4),)),
        "mr_skip": noise(arg_keys[4], (D,), 1.0, 4.0, ((0, 4),), jnp.float32),
        "mr_out_w": noise(arg_keys[5], (D, D), D ** -0.5, 0.09375, ((0, 4), (1, 8))),
        "lr_gain": jnp.clip(1.0 + 0.18 * jax.random.normal(arg_keys[6], (D,), jnp.float32), 0.1, 1.9),
        "lr_in_w": noise(arg_keys[7], (D, 3, D), D ** -0.5, 0.09375, ((2, 4),)),
        "lr_short_w": noise(arg_keys[8], (SHORT, 3, D), SHORT ** -0.5, 3.5, ((2, 4),), jnp.float32),
        "lr_rate": draw_lr_rate(jax.random.fold_in(arg_keys[13], 71), 0),
        "lr_res": noise(arg_keys[10], (STATE, D), 0.5, 3.0, ((1, 4),), jnp.float32),
        "lr_skip": noise(arg_keys[11], (D,), 1.0, 4.0, ((0, 4),), jnp.float32),
        "lr_out_w": noise(arg_keys[12], (D, D), D ** -0.5, 0.09375, ((0, 4), (1, 8))),
    }


def causal_short(inputs, weights):
    prior = weights.shape[0] - 1
    padded = jnp.pad(inputs, ((0, 0), (prior, 0), (0, 0), (0, 0)))
    total = jnp.zeros(inputs.shape, jnp.float32)
    for lag in range(weights.shape[0]):
        total = total + weights[lag] * padded[:, prior - lag:prior - lag + LENGTH].astype(jnp.float32)
    return total

def long_taps(values, taps):
    padded = jnp.pad(values.astype(jnp.float32), ((0, 0), (MR_TAPS - 1, 0), (0, 0)))

    def accumulate(index, total):
        offset = (MR_TAPS - 1 - index).astype(jnp.int32)
        window = lax.dynamic_slice_in_dim(padded, offset, LENGTH, 1)
        return total + taps[index].astype(jnp.float32) * window
    return lax.fori_loop(0, MR_TAPS, accumulate, jnp.zeros(values.shape, jnp.float32))

def modal(values, rate, residue):
    decay = jnp.exp(-rate)
    weight = residue * jnp.sqrt(1.0 - jnp.exp(-2.0 * rate))

    def advance(state, row):
        state = decay * state + row[:, None, :]
        return (state, lax.optimization_barrier(jnp.sum(weight * state, axis=1)))
    start = jnp.zeros((SEQS, STATE, D), jnp.float32)
    _, result = lax.scan(advance, start, jnp.moveaxis(values, 1, 0))
    return jnp.moveaxis(result, 0, 1)

def split_sum(mixed, weight):
    group = D // N_TP
    flat = mixed.reshape(SEQS * LENGTH, D)
    total = jnp.zeros((SEQS * LENGTH, D), jnp.float32)
    for index in range(N_TP):
        partial_sum = jnp.dot(flat[:, index * group:(index + 1) * group], weight[index * group:(index + 1) * group], preferred_element_type=jnp.float32)
        total = total + partial_sum.astype(jnp.bfloat16).astype(jnp.float32)
    return total.reshape(SEQS, LENGTH, D)

def reference(residual_in, mr_qkv, mr_short_w, mr_filter, mr_skip, mr_out_w, lr_gain, lr_in_w, lr_short_w, lr_rate, lr_res, lr_skip, lr_out_w):
    mr_mixed = causal_short(mr_qkv, mr_short_w)
    mr_u = (mr_mixed[:, :, 1] * mr_mixed[:, :, 2]).astype(jnp.bfloat16)
    mr_conv = long_taps(mr_u, mr_filter)
    mr_z = (mr_mixed[:, :, 0] * (mr_conv + mr_skip * mr_u.astype(jnp.float32))).astype(jnp.bfloat16)
    residual_mid = (residual_in.astype(jnp.float32) + split_sum(mr_z, mr_out_w)).astype(jnp.bfloat16)
    widened = residual_mid.astype(jnp.float32)
    meansq = lax.optimization_barrier(jnp.mean(widened * widened, axis=-1, keepdims=True))
    normed = (widened * lax.rsqrt(meansq + 1e-06) * lr_gain).astype(jnp.bfloat16)
    lr_qkv = jnp.dot(normed.reshape(SEQS * LENGTH, D), lr_in_w.reshape(D, 3 * D), preferred_element_type=jnp.float32)
    lr_qkv = lr_qkv.astype(jnp.bfloat16).reshape(SEQS, LENGTH, 3, D)
    lr_mixed = causal_short(lr_qkv, lr_short_w)
    lr_u = lr_mixed[:, :, 1] * lr_mixed[:, :, 2]
    lr_conv = modal(lr_u, lr_rate, lr_res)
    lr_z = (lr_mixed[:, :, 0] * (lr_conv + lr_skip * lr_u)).astype(jnp.bfloat16)
    return (residual_mid.astype(jnp.float32) + split_sum(lr_z, lr_out_w)).astype(jnp.bfloat16)
```

```python
import functools

import jax
import jax.numpy as jnp
from jax import lax
from jax.experimental import pallas as pl
from jax.experimental.pallas import tpu as pltpu
from jax.sharding import PartitionSpec as P

F32 = jnp.float32
BF16 = jnp.bfloat16
LANES = 128
SUB = 8
HALO = 16
STEP = 8


def params(mebibytes, **more):
    return pltpu.CompilerParams(vmem_limit_bytes=mebibytes * 2**20, **more)


def vmem(count):
    return [pl.BlockSpec(memory_space=pltpu.VMEM)] * count


def cost(flops, moved):
    return pl.CostEstimate(flops=int(flops), bytes_accessed=int(moved), transcendentals=0)


def tiles(value):
    width = value.shape[-1]
    room = SUB * LANES
    if width < room:
        value = jnp.pad(value, [(0, 0)] * (value.ndim - 1) + [(0, room - width)])
    return value.reshape(value.shape[:-1] + (SUB, LANES)).astype(F32)


def put_rows(flat_ref, first, rows, lane_tile, value):
    flat_ref[pl.ds(first * SUB + lane_tile, rows, stride=SUB), :] = value


def get_rows(flat_ref, first, rows, lane_tile):
    return flat_ref[pl.ds(first * SUB + lane_tile, rows, stride=SUB), :]


def mr_kernel(x_ref, halo_ref, short_ref, filter_ref, skip_ref, z_ref, raw, u, zs):
    _, _, tokens, width = x_ref.shape
    taps = filter_ref.shape[0]
    lags = short_ref.shape[0]
    prior = lags - 1
    for tile in range(width // LANES):
        lanes = slice(tile * LANES, (tile + 1) * LANES)
        put_rows(u, 0, taps, tile, halo_ref[0, :taps, lanes].astype(F32))
        tail = halo_ref[0, taps : taps + HALO, lanes].astype(F32)
        for p in range(3):
            put_rows(raw.at[p], 0, prior, tile, tail[prior * p : prior * (p + 1)])
            put_rows(raw.at[p], prior, tokens, tile, x_ref[0, p, :, lanes].astype(F32))
    raw3 = raw.reshape(3, tokens + prior, SUB, LANES)
    u3 = u.reshape(taps + tokens, SUB, LANES)
    zs3 = zs.reshape(tokens, SUB, LANES)

    def mix(p, first, rows):
        total = short_ref[0, p] * raw3[p, pl.ds(first + prior, rows)]
        for lag in range(1, lags):
            total = total + short_ref[lag, p] * raw3[p, pl.ds(first + prior - lag, rows)]
        return total

    @pl.loop(0, tokens // STEP)
    def _(block):
        first = block * STEP
        product = mix(1, first, STEP) * mix(2, first, STEP)
        u3[pl.ds(taps + first, STEP)] = product.astype(BF16).astype(F32)

    @pl.loop(0, tokens // STEP)
    def _(block):
        first = block * STEP

        def chunk(index, totals):
            tap = index * STEP
            base = first + taps - tap - (STEP - 1)
            window = [u3[base + j] for j in range(2 * STEP - 1)]
            totals = list(totals)
            for k in range(STEP):
                weight = filter_ref[tap + k]
                for t in range(STEP):
                    totals[t] = totals[t] + weight * window[t - k + STEP - 1]
            return tuple(totals)

        nothing = jnp.zeros((SUB, LANES), F32)
        totals = lax.fori_loop(0, taps // STEP, chunk, (nothing,) * STEP)
        queries = mix(0, first, STEP)
        for t in range(STEP):
            zs3[first + t] = queries[t] * (totals[t] + skip_ref[...] * u3[taps + first + t])

    for tile in range(width // LANES):
        lanes = slice(tile * LANES, (tile + 1) * LANES)
        z_ref[:, lanes] = get_rows(zs, 0, tokens, tile).astype(BF16)


def mr_filtered(x, halo, short_w, taps_w, skip, seq):
    _, _, tokens, width = x.shape
    taps = taps_w.shape[0]
    prior = short_w.shape[0] - 1
    rows = halo.shape[1]
    return pl.pallas_call(
        mr_kernel,
        grid=(1,),
        out_shape=jax.ShapeDtypeStruct((tokens, width), BF16),
        in_specs=[
            pl.BlockSpec((1, 3, tokens, width), lambda i: (seq, 0, 0, 0)),
            pl.BlockSpec((1, rows, width), lambda i: (seq, 0, 0)),
            *vmem(3),
        ],
        out_specs=pl.BlockSpec((tokens, width), lambda i: (0, 0)),
        scratch_shapes=[
            pltpu.VMEM((3, (tokens + prior) * SUB, LANES), F32),
            pltpu.VMEM(((taps + tokens) * SUB, LANES), F32),
            pltpu.VMEM((tokens * SUB, LANES), F32),
        ],
        compiler_params=params(32),
        cost_estimate=cost(2.0e10, 4e6),
        name="mr_filtered",
    )(x, halo, short_w, taps_w, skip)


def project_kernel(places, scalar_ref, z_ref, *refs):
    weights, out_ref = refs[:-1], refs[-1]
    width = out_ref.shape[2]
    z = z_ref[...]
    for (offset, piece, whole), weight in zip(places, weights, strict=True):
        columns = weight.shape[1]
        owner = lax.bitwise_xor(scalar_ref[0], offset)
        start = owner * whole + piece * columns
        share = lax.div(start, width)
        lanes = pl.ds(pl.multiple_of(lax.rem(start, width), columns), columns)
        out_ref[share, :, lanes] = jnp.dot(z, weight[...], preferred_element_type=F32).astype(BF16)


def project(z, position, places, weights, shares):
    tokens, width = z.shape
    total = sum(w.shape[1] for w in weights)
    return pl.pallas_call(
        functools.partial(project_kernel, places),
        out_shape=jax.ShapeDtypeStruct((shares, tokens, total // shares), BF16),
        in_specs=[pl.BlockSpec(memory_space=pltpu.SMEM), *vmem(1 + len(weights))],
        out_specs=pl.BlockSpec(memory_space=pltpu.VMEM),
        compiler_params=params(40),
        cost_estimate=cost(2 * tokens * width * total, 2 * total * (width + tokens)),
        name="project",
    )(position, z, *weights)


def swap_gather(block, axis, pieces):
    count = lax.axis_size(axis)
    bits = [1 << k for k in range(count.bit_length() - 1)]
    whole = block.shape[1]
    columns = whole // pieces
    places, arrays = [], []
    for piece in range(pieces):
        far = bits[:0:-1]
        turn = piece % max(1, len(far))
        held = [(0, block[:, piece * columns : (piece + 1) * columns])]
        for bit in far[turn:] + far[:turn] + bits[:1]:
            pairs = [(i, i ^ bit) for i in range(count)]
            held = held + [(offset ^ bit, lax.ppermute(v, axis, pairs)) for offset, v in held]
        places += [(offset, piece, whole) for offset, _ in held]
        arrays += [v for _, v in held]
    return tuple(places), arrays


def add(a, b):
    return (a.astype(F32) + b.astype(F32)).astype(BF16)


def line_scatter(parts, axis):
    count = lax.axis_size(axis)
    place = lax.axis_index(axis)

    def part(share):
        return lax.dynamic_index_in_dim(parts, jnp.clip(share, 0, count - 1), 0, False)

    from_low = from_high = None
    for step in range(1, count):
        up = [(p, p + 1) for p in range(step)]
        down = [(p, p - 1) for p in range(count - step, count)]
        up_share = count - step + place
        down_share = step - count + place
        if step < count - 1 - step:
            value = part(jnp.where(place < step, up_share, down_share))
            if from_low is not None:
                value = add(value, from_low)
            from_low = from_high = lax.ppermute(value, axis, up + down)
        else:
            low, high = part(up_share), part(down_share)
            if from_low is not None:
                low, high = add(low, from_low), add(high, from_high)
            from_low = lax.ppermute(low, axis, up)
            from_high = lax.ppermute(high, axis, down)
    return part(place), from_low, from_high


def line_gather(value, axis):
    count = lax.axis_size(axis)
    place = lax.axis_index(axis)
    low, high = [], []
    up_value = down_value = value
    for step in range(1, count):
        up = [(p, p + 1) for p in range(step - 1, count - 1)]
        down = [(p, p - 1) for p in range(1, count - step + 1)]
        if step - 1 > count - step:
            both = lax.ppermute(jnp.where(place >= step - 1, up_value, down_value), axis, up + down)
            up_value = down_value = both
        else:
            up_value = lax.ppermute(up_value, axis, up)
            down_value = lax.ppermute(down_value, axis, down)
        low.append(up_value)
        high.append(down_value)
    return [value, *low, *high]


def lr_in_kernel(count, scalar_ref, halo_ref, gain_ref, *refs):
    blocks, (w_ref, out_ref, mid, normed) = refs[: 2 * count - 1], refs[2 * count - 1 :]
    tokens, width = blocks[0].shape
    own, low, high = blocks[0], blocks[1:count], blocks[count:]

    @pl.when((pl.program_id(0) == 0) & (pl.program_id(1) == 0))
    def _():
        for share in range(count):
            lanes = pl.ds(share * width, width)
            mid[:HALO, lanes] = halo_ref[share]
            for place in range(count):
                source = own if place == share else (low[place - share - 1] if share < place else high[share - place - 1])

                @pl.when(scalar_ref[0] == place)
                def _(source=source, lanes=lanes):
                    mid[HALO:, lanes] = source[...]

        rows = HALO

        @pl.loop(0, (tokens + HALO) // rows)
        def _(block):
            where = pl.ds(pl.multiple_of(block * rows, rows), rows)
            wide = mid[where, :].astype(F32)
            scale = lax.rsqrt(jnp.mean(wide * wide, axis=-1, keepdims=True) + 1e-6)
            normed[where, :] = (wide * scale * gain_ref[...]).astype(BF16)

    out_ref[0] = jnp.dot(normed[...], w_ref[0], preferred_element_type=F32).astype(BF16)


def lr_in(place, halo, gain, blocks, weight):
    count = halo.shape[0]
    tokens, width = blocks[0].shape
    _, model, out_width = weight.shape
    columns = min(512, out_width)
    rows = tokens + HALO
    return pl.pallas_call(
        functools.partial(lr_in_kernel, count),
        grid=(3, out_width // columns),
        out_shape=jax.ShapeDtypeStruct((3, rows, out_width), BF16),
        in_specs=[
            pl.BlockSpec(memory_space=pltpu.SMEM),
            *vmem(2 + len(blocks)),
            pl.BlockSpec((1, model, columns), lambda p, j: (p, 0, j)),
        ],
        out_specs=pl.BlockSpec((1, rows, columns), lambda p, j: (p, 0, j)),
        scratch_shapes=[pltpu.VMEM((rows, model), BF16), pltpu.VMEM((rows, model), BF16)],
        compiler_params=params(48),
        cost_estimate=cost(6 * rows * model * out_width, 6 * model * out_width),
        name="lr_in",
    )(place, halo, gain, *blocks, weight)


def lr_mix_kernel(x_ref, short_ref, rate_ref, q_ref, u_ref, end_ref, raw):
    _, rows, width = x_ref.shape
    tokens = rows - HALO
    lags = short_ref.shape[0]
    prior = lags - 1
    poles = rate_ref.shape[0]
    for tile in range(width // LANES):
        lanes = slice(tile * LANES, (tile + 1) * LANES)
        for p in range(3):
            wide = x_ref[p, :, lanes].astype(F32)
            put_rows(raw.at[p], 0, rows, tile, wide)
    raw3 = raw.reshape(3, rows, SUB, LANES)
    decay = [jnp.exp(-rate_ref[n]) for n in range(poles)]

    def mix(p, first):
        total = short_ref[0, p] * raw3[p, pl.ds(first + HALO, STEP)]
        for lag in range(1, lags):
            total = total + short_ref[lag, p] * raw3[p, pl.ds(first + HALO - lag, STEP)]
        return total

    def block(index, states):
        first = index * STEP
        q_ref[pl.ds(first, STEP)] = mix(0, first)
        product = mix(1, first) * mix(2, first)
        u_ref[pl.ds(first, STEP)] = product
        states = list(states)
        for t in range(STEP):
            for n in range(poles):
                states[n] = decay[n] * states[n] + product[t]
        return tuple(states)

    nothing = jnp.zeros((SUB, LANES), F32)
    states = lax.fori_loop(0, tokens // STEP, block, (nothing,) * poles)
    for n in range(poles):
        end_ref[n] = states[n].astype(BF16)


def lr_mix(x, short_w, rate):
    _, rows, width = x.shape
    tokens = rows - HALO
    poles = rate.shape[0]
    return pl.pallas_call(
        lr_mix_kernel,
        out_shape=(
            jax.ShapeDtypeStruct((tokens, SUB, LANES), F32),
            jax.ShapeDtypeStruct((tokens, SUB, LANES), F32),
            jax.ShapeDtypeStruct((poles, SUB, LANES), BF16),
        ),
        in_specs=vmem(3),
        out_specs=tuple(vmem(3)),
        scratch_shapes=[pltpu.VMEM((3, rows * SUB, LANES), F32)],
        compiler_params=params(32),
        cost_estimate=cost(4e9, 5e6),
        name="lr_mix",
    )(x, short_w, rate)


def lr_modal_kernel(scalar_ref, q_ref, u_ref, ends_ref, rate_ref, res_ref, skip_ref, z_ref, zs):
    tokens = q_ref.shape[0]
    width = z_ref.shape[1]
    count, poles = ends_ref.shape[:2]
    position = scalar_ref[0]
    decay, weight, enter = [], [], []
    for n in range(poles):
        rate = rate_ref[n]
        decay.append(jnp.exp(-rate))
        weight.append(res_ref[n] * jnp.sqrt(1.0 - jnp.exp(-2.0 * rate)))

        def arrive(index, total, n=n, rate=rate):
            distance = (position - 1 - index).astype(F32)
            return total + jnp.exp(-rate * tokens * distance) * ends_ref[index, n].astype(F32)

        enter.append(lax.fori_loop(0, position, arrive, jnp.zeros((SUB, LANES), F32)))
    zs3 = zs.reshape(tokens, SUB, LANES)

    def block(index, states):
        first = index * STEP
        states = list(states)
        for t in range(STEP):
            value = u_ref[first + t]
            total = skip_ref[...] * value
            for n in range(poles):
                states[n] = decay[n] * states[n] + value
                total = total + weight[n] * states[n]
            zs3[first + t] = q_ref[first + t] * total
        return tuple(states)

    lax.fori_loop(0, tokens // STEP, block, tuple(enter))
    for tile in range(width // LANES):
        lanes = slice(tile * LANES, (tile + 1) * LANES)
        z_ref[:, lanes] = get_rows(zs, 0, tokens, tile).astype(BF16)


def lr_modal(position, q, u, ends, rate, res, skip, width):
    tokens = q.shape[0]
    return pl.pallas_call(
        lr_modal_kernel,
        out_shape=jax.ShapeDtypeStruct((tokens, width), BF16),
        in_specs=[pl.BlockSpec(memory_space=pltpu.SMEM), *vmem(6)],
        out_specs=pl.BlockSpec(memory_space=pltpu.VMEM),
        scratch_shapes=[pltpu.VMEM((tokens * SUB, LANES), F32)],
        compiler_params=params(32),
        cost_estimate=cost(8e9, 4e6),
        name="lr_modal",
    )(position, q, u, ends, rate, res, skip)


def local(
    residual_in,
    mr_qkv,
    mr_short_w,
    mr_filter,
    mr_skip,
    mr_out_w,
    lr_gain,
    lr_in_w,
    lr_short_w,
    lr_rate,
    lr_res,
    lr_skip,
    lr_out_w,
):
    sequences, tokens, _, width = mr_qkv.shape
    taps = mr_filter.shape[0]
    prior = mr_short_w.shape[0] - 1
    ctx, tp = lax.axis_size("ctx"), lax.axis_size("tp")
    position = lax.axis_index("ctx").astype(jnp.int32).reshape(1)
    place = lax.axis_index("tp").astype(jnp.int32).reshape(1)
    onward = [(i, i + 1) for i in range(ctx - 1)]

    tail = mr_qkv[:, tokens - taps - prior :].astype(F32)
    mixed = sum(mr_short_w[lag, 1:] * tail[:, prior - lag : prior - lag + taps, 1:] for lag in range(prior + 1))
    tail_u = (mixed[:, :, 0] * mixed[:, :, 1]).astype(BF16)
    last = jnp.swapaxes(mr_qkv[:, tokens - prior :], 1, 2).reshape(sequences, 3 * prior, width)
    last = jnp.pad(last, ((0, 0), (0, HALO - 3 * prior), (0, 0)))
    halo = lax.ppermute(jnp.concatenate([tail_u, last], axis=1), "ctx", onward)

    places, mr_weights = swap_gather(mr_out_w, "ctx", 2)
    x = jnp.swapaxes(mr_qkv, 1, 2)
    mr_short, lr_short = tiles(mr_short_w), tiles(lr_short_w)
    mr_taps, mr_direct = tiles(mr_filter), tiles(mr_skip)
    rate, res, lr_direct = tiles(lr_rate), tiles(lr_res), tiles(lr_skip)
    in_w = jnp.swapaxes(lr_in_w, 0, 1)
    gain = lr_gain.reshape(1, -1)

    lr_weights = lax.all_gather(lr_out_w, "ctx", axis=0)
    lr_weights = [lr_weights[i] for i in range(ctx)]
    lr_places = tuple((i, 0, lr_out_w.shape[1]) for i in range(ctx))
    zero = jnp.zeros((1,), jnp.int32)

    mids, outs = [], []
    zs = [mr_filtered(x, halo, mr_short, mr_taps, mr_direct, s) for s in range(sequences)]
    for s in range(sequences):
        parts = project(zs[s], position, places, mr_weights, tp)
        own, low, high = line_scatter(parts, "tp")
        total = own.astype(F32) + low.astype(F32) + high.astype(F32)
        mids.append((residual_in[s].astype(F32) + total).astype(BF16))
    xs = []
    for s in range(sequences):
        edge = lax.ppermute(mids[s][tokens - HALO :], "ctx", onward)
        edge = lax.all_gather(edge, "tp", axis=0)
        blocks = line_gather(mids[s], "tp")
        xs.append(lr_in(place, edge, gain, blocks, in_w))
    for s in range(sequences):
        q, u, end = lr_mix(xs[s], lr_short, rate)
        ends = lax.all_gather(end, "ctx", axis=0)
        z = lr_modal(position, q, u, ends, rate, res, lr_direct, width)
        parts = project(z, zero, lr_places, lr_weights, tp)
        own, low, high = line_scatter(parts, "tp")
        total = own.astype(F32) + low.astype(F32) + high.astype(F32)
        outs.append((mids[s].astype(F32) + total).astype(BF16))
    return jnp.stack(outs)


def solution(mesh):
    in_specs = (
        P(None, "ctx", "tp"),
        P(None, "ctx", None, "tp"),
        P(None, None, "tp"),
        P(None, "tp"),
        P("tp"),
        P("tp", "ctx"),
        P(),
        P(None, None, "tp"),
        P(None, None, "tp"),
        P(None, "tp"),
        P(None, "tp"),
        P("tp"),
        P("tp", "ctx"),
    )
    out_specs = P(None, "ctx", "tp")
    return jax.shard_map(local, mesh=mesh, in_specs=in_specs, out_specs=out_specs, check_vma=False)
```

```python
import functools

import jax
import jax.numpy as jnp
from jax import lax
from jax.experimental import pallas as pl
from jax.experimental.pallas import tpu as pltpu
from jax.sharding import PartitionSpec as P

F32 = jnp.float32
BF16 = jnp.bfloat16
LANES = 128
SUB = 8
HALO = 16
STEP = 8


def params(mebibytes, **more):
    return pltpu.CompilerParams(vmem_limit_bytes=mebibytes * 2**20, **more)


def vmem(count):
    return [pl.BlockSpec(memory_space=pltpu.VMEM)] * count


def cost(flops, moved):
    return pl.CostEstimate(flops=int(flops), bytes_accessed=int(moved), transcendentals=0)


def tiles(value):
    width = value.shape[-1]
    room = SUB * LANES
    if width < room:
        value = jnp.pad(value, [(0, 0)] * (value.ndim - 1) + [(0, room - width)])
    return value.reshape(value.shape[:-1] + (SUB, LANES)).astype(F32)


def put_rows(flat_ref, first, rows, lane_tile, value):
    flat_ref[pl.ds(first * SUB + lane_tile, rows, stride=SUB), :] = value


def get_rows(flat_ref, first, rows, lane_tile):
    return flat_ref[pl.ds(first * SUB + lane_tile, rows, stride=SUB), :]


def window_sum(filter_ref, source3, base, chunks, totals):
    def chunk(index, totals):
        tap = index * STEP
        window = [source3[base - tap - (STEP - 1) + j] for j in range(2 * STEP - 1)]
        totals = list(totals)
        for k in range(STEP):
            weight = filter_ref[tap + k]
            for t in range(STEP):
                totals[t] = totals[t] + weight * window[t - k + STEP - 1]
        return tuple(totals)

    return lax.fori_loop(*chunks, chunk, tuple(totals))


def mr_local_kernel(x_ref, short_ref, filter_ref, skip_ref, q_ref, conv_ref, raw, u):
    _, _, tokens, width = x_ref.shape
    taps = filter_ref.shape[0]
    lags = short_ref.shape[0]
    prior = lags - 1
    for tile in range(width // LANES):
        lanes = slice(tile * LANES, (tile + 1) * LANES)
        for p in range(3):
            put_rows(raw.at[p], prior, tokens, tile, x_ref[0, p, :, lanes].astype(F32))
    raw3 = raw.reshape(3, tokens + prior, SUB, LANES)
    u3 = u.reshape(taps + tokens, SUB, LANES)
    for p in range(3):
        raw3[p, :prior] = jnp.zeros((prior, SUB, LANES), F32)

    @pl.loop(0, taps // STEP)
    def _(block):
        u3[pl.ds(block * STEP, STEP)] = jnp.zeros((STEP, SUB, LANES), F32)

    def mix(p, first, rows):
        total = short_ref[0, p] * raw3[p, pl.ds(first + prior, rows)]
        for lag in range(1, lags):
            total = total + short_ref[lag, p] * raw3[p, pl.ds(first + prior - lag, rows)]
        return total

    @pl.loop(0, tokens // STEP)
    def _(block):
        first = block * STEP
        q_ref[pl.ds(first, STEP)] = mix(0, first, STEP)
        product = mix(1, first, STEP) * mix(2, first, STEP)
        u3[pl.ds(taps + first, STEP)] = product.astype(BF16).astype(F32)

    @pl.loop(0, tokens // STEP)
    def _(block):
        first = block * STEP
        totals = [skip_ref[...] * u3[taps + first + t] for t in range(STEP)]
        chunks = (0, lax.min(block + 1, taps // STEP))
        totals = window_sum(filter_ref, u3, taps + first, chunks, totals)
        for t in range(STEP):
            conv_ref[first + t] = totals[t]


def mr_local(x, short_w, taps_w, skip, seq):
    _, _, tokens, width = x.shape
    taps = taps_w.shape[0]
    prior = short_w.shape[0] - 1
    rows = jax.ShapeDtypeStruct((tokens, SUB, LANES), F32)
    return pl.pallas_call(
        mr_local_kernel,
        grid=(1,),
        out_shape=(rows, rows),
        in_specs=[pl.BlockSpec((1, 3, tokens, width), lambda i: (seq, 0, 0, 0)), *vmem(3)],
        out_specs=(pl.BlockSpec((tokens, SUB, LANES), lambda i: (0, 0, 0)),) * 2,
        scratch_shapes=[
            pltpu.VMEM((3, (tokens + prior) * SUB, LANES), F32),
            pltpu.VMEM(((taps + tokens) * SUB, LANES), F32),
        ],
        compiler_params=params(20),
        cost_estimate=cost(1e9, 1e6),
        name="mr_local",
    )(x, short_w, taps_w, skip)


def mr_finish_kernel(x_ref, halo_ref, q_ref, conv_ref, short_ref, filter_ref, skip_ref, z_ref, raw, extra, zs):
    tokens, _, _ = q_ref.shape
    width = z_ref.shape[1]
    taps = filter_ref.shape[0]
    lags = short_ref.shape[0]
    prior = lags - 1
    for tile in range(width // LANES):
        lanes = slice(tile * LANES, (tile + 1) * LANES)
        put_rows(extra, 0, taps, tile, halo_ref[0, :taps, lanes].astype(F32))
        tail = halo_ref[0, taps : taps + HALO, lanes].astype(F32)
        for p in range(3):
            put_rows(raw.at[p], 0, prior, tile, tail[prior * p : prior * (p + 1)])
            put_rows(raw.at[p], prior, prior, tile, x_ref[0, p, :, lanes].astype(F32)[:prior])
    raw3 = raw.reshape(3, 2 * prior, SUB, LANES)
    extra3 = extra.reshape(taps + 2 * STEP, SUB, LANES)
    zs3 = zs.reshape(tokens, SUB, LANES)

    def mix(p, t, lowest):
        total = short_ref[0, p] * raw3[p, prior + t]
        for lag in range(1, lags):
            if prior + t - lag >= lowest:
                total = total + short_ref[lag, p] * raw3[p, prior + t - lag]
        return total

    extra3[taps:] = jnp.zeros((2 * STEP, SUB, LANES), F32)
    for t in range(prior):
        whole = (mix(1, t, 0) * mix(2, t, 0)).astype(BF16).astype(F32)
        alone = (mix(1, t, prior) * mix(2, t, prior)).astype(BF16).astype(F32)
        extra3[taps + t] = whole - alone

    def sums(block):
        first = block * STEP
        chunks = (lax.max(block - 1, 0), taps // STEP)
        totals = [conv_ref[first + t] for t in range(STEP)]
        return first, window_sum(filter_ref, extra3, taps + first, chunks, totals)

    first, totals = sums(0)
    for t in range(STEP):
        if t < prior:
            zs3[t] = mix(0, t, 0) * (totals[t] + skip_ref[...] * extra3[taps + t])
        else:
            zs3[t] = q_ref[t] * totals[t]

    @pl.loop(1, taps // STEP + 1)
    def _(block):
        first, totals = sums(block)
        for t in range(STEP):
            zs3[first + t] = q_ref[first + t] * totals[t]

    @pl.loop(taps // STEP + 1, tokens // STEP)
    def _(block):
        where = pl.ds(block * STEP, STEP)
        zs3[where] = q_ref[where] * conv_ref[where]

    for tile in range(width // LANES):
        lanes = slice(tile * LANES, (tile + 1) * LANES)
        z_ref[:, lanes] = get_rows(zs, 0, tokens, tile).astype(BF16)


def mr_finish(x, halo, q, conv, short_w, taps_w, skip, seq):
    _, _, tokens, width = x.shape
    taps = taps_w.shape[0]
    prior = short_w.shape[0] - 1
    rows = pl.BlockSpec((tokens, SUB, LANES), lambda i: (0, 0, 0))
    return pl.pallas_call(
        mr_finish_kernel,
        grid=(1,),
        out_shape=jax.ShapeDtypeStruct((tokens, width), BF16),
        in_specs=[
            pl.BlockSpec((1, 3, HALO, width), lambda i: (seq, 0, 0, 0)),
            pl.BlockSpec((1, halo.shape[1], width), lambda i: (seq, 0, 0)),
            rows,
            rows,
            *vmem(3),
        ],
        out_specs=pl.BlockSpec((tokens, width), lambda i: (0, 0)),
        scratch_shapes=[
            pltpu.VMEM((3, 2 * prior * SUB, LANES), F32),
            pltpu.VMEM(((taps + 2 * STEP) * SUB, LANES), F32),
            pltpu.VMEM((tokens * SUB, LANES), F32),
        ],
        compiler_params=params(20),
        cost_estimate=cost(1e9, 1e6),
        name="mr_finish",
    )(x, halo, q, conv, short_w, taps_w, skip)


def project_kernel(places, scalar_ref, z_ref, *refs):
    count = len(places)
    weights = refs[:count]
    out_ref, result = refs[-4 - count], refs[-3 - count]
    held, in_sems, out_sems = refs[-2 - count : -2], refs[-2], refs[-1]
    width = out_ref.shape[2]
    copies = [pltpu.make_async_copy(weights[k], held[k], in_sems.at[k]) for k in range(count)]
    for copy in copies:
        copy.start()
    z = z_ref[...]
    sent = []
    begun = 0
    for k, (offset, begin, whole) in enumerate(places):
        columns = held[k].shape[1]
        start = lax.bitwise_xor(scalar_ref[0], offset) * whole + begin
        share = lax.div(start, width)
        lanes = pl.ds(pl.multiple_of(lax.rem(start, width), columns), columns)
        mine = slice(begun, begun + columns)
        begun += columns
        copies[k].wait()
        result[:, mine] = jnp.dot(z, held[k][...], preferred_element_type=F32).astype(BF16)
        sent.append(pltpu.make_async_copy(result.at[:, mine], out_ref.at[share, :, lanes], out_sems.at[k]))
        sent[-1].start()
    for copy in sent:
        copy.wait()


def project(z, position, places, weights, shares, given=None):
    tokens, width = z.shape
    total = sum(w.shape[1] for w in weights)
    model = places[0][2] * lax.axis_size("ctx")
    extra = [] if given is None else [given]
    anywhere = pl.BlockSpec(memory_space=pl.ANY)
    return pl.pallas_call(
        functools.partial(project_kernel, places),
        out_shape=jax.ShapeDtypeStruct((shares, tokens, model // shares), BF16),
        in_specs=[
            pl.BlockSpec(memory_space=pltpu.SMEM),
            *vmem(1),
            *[anywhere] * (len(weights) + len(extra)),
        ],
        out_specs=anywhere,
        scratch_shapes=[
            pltpu.VMEM((tokens, total), BF16),
            *[pltpu.VMEM(w.shape, w.dtype) for w in weights],
            pltpu.SemaphoreType.DMA((len(weights),)),
            pltpu.SemaphoreType.DMA((len(weights),)),
        ],
        input_output_aliases={2 + len(weights): 0} if extra else {},
        compiler_params=params(16),
        cost_estimate=cost(2 * tokens * width * total, 2 * total * (width + tokens)),
        name="project",
    )(position, z, *weights, *extra)


def after(value, *others):
    return lax.optimization_barrier((value, *others))[0]


def swap_pairs(axis, bit):
    return [(i, i ^ bit) for i in range(lax.axis_size(axis))]


def swap_gather(block, axis, middle=None, late=None):
    count = lax.axis_size(axis)
    far = [1 << k for k in range(count.bit_length() - 1, 0, -1) if 1 << k < count]
    whole = block.shape[1]
    have = {(0, 0): block}
    for bit in far:
        have[bit, 0] = lax.ppermute(block, axis, swap_pairs(axis, bit))
    near = dict(have)
    pieces = 1 << max(1, len(far)).bit_length() - 1
    columns = whole // pieces
    for piece in range(pieces if far else 0):
        begin = piece * columns
        part = {bit: have[bit, 0][:, begin : begin + columns] for bit in far}
        order = far[piece:] + far[:piece]
        known = [order[0]]
        for bit in order[1:]:
            for offset in list(known):
                value = part[offset] if middle is None else after(part[offset], middle)
                part[offset ^ bit] = lax.ppermute(value, axis, swap_pairs(axis, bit))
                have[offset ^ bit, begin] = part[offset ^ bit]
                known.append(offset ^ bit)
            known.append(bit)
    for key in list(have):
        value = have[key]
        if key in near:
            value = value if middle is None else after(value, middle)
        else:
            value = value if late is None else after(value, late)
        have[key[0] ^ 1, key[1]] = lax.ppermute(value, axis, swap_pairs(axis, 1))
    return tuple((offset, begin, whole) for offset, begin in have), list(have.values())


def add(a, b):
    return (a.astype(F32) + b.astype(F32)).astype(BF16)


def line_scatter(parts, axis):
    count = lax.axis_size(axis)
    place = lax.axis_index(axis)

    def part(share):
        return lax.dynamic_index_in_dim(parts, jnp.clip(share, 0, count - 1), 0, False)

    from_low = from_high = None
    for step in range(1, count):
        up = [(p, p + 1) for p in range(step)]
        down = [(p, p - 1) for p in range(count - step, count)]
        up_share = count - step + place
        down_share = step - count + place
        if step < count - 1 - step:
            value = part(jnp.where(place < step, up_share, down_share))
            if from_low is not None:
                value = add(value, from_low)
            from_low = from_high = lax.ppermute(value, axis, up + down)
        else:
            low, high = part(up_share), part(down_share)
            if from_low is not None:
                low, high = add(low, from_low), add(high, from_high)
            from_low = lax.ppermute(low, axis, up)
            from_high = lax.ppermute(high, axis, down)
    return part(place), from_low, from_high


def line_gather(value, axis):
    count = lax.axis_size(axis)

    def move(what, *pairs):
        return lax.ppermute(what, axis, pairs)

    if count == 4:
        outer = move(value, (0, 1), (1, 0), (2, 3), (3, 2))
        inner = move(value, (1, 2), (2, 1))
        crossed = move(outer, (1, 2), (2, 1))
        outward = move(inner, (1, 0), (2, 3))
        last = move(crossed, (1, 0), (2, 3))
        table = ((0, 1, 4, 5), (1, 0, 2, 3), (3, 2, 0, 1), (5, 4, 1, 0))
        return [value, outer, inner, crossed, outward, last], table
    low, high = [value], [value]
    for step in range(1, count):
        low.append(move(low[-1], *[(p, p + 1) for p in range(step - 1, count - 1)]))
        high.append(move(high[-1], *[(p, p - 1) for p in range(1, count - step + 1)]))
    table = tuple(
        tuple(place - share if share <= place else count - 1 + share - place for share in range(count))
        for place in range(count)
    )
    return low + high[1:], table


def lr_in_kernel(table, scalar_ref, gain_ref, *refs):
    count = len(table)
    *blocks, w_ref, out_ref, mid, normed, held, sems = refs
    tokens, width = blocks[0].shape
    parts, _, _, columns = held.shape
    copies = []
    for k in range(parts):
        p, begin = divmod(k * columns, width)
        copies.append(pltpu.make_async_copy(w_ref.at[p, :, pl.ds(begin, columns)], held.at[k, 0], sems.at[k]))
        copies[-1].start()
    for share in range(count):
        lanes = pl.ds(share * width, width)
        for place in range(count):

            @pl.when(scalar_ref[0] == place)
            def _(source=blocks[table[place][share]], lanes=lanes):
                mid[:, lanes] = source[...]

    @pl.loop(0, tokens // HALO)
    def _(block):
        where = pl.ds(pl.multiple_of(block * HALO, HALO), HALO)
        wide = mid[where, :].astype(F32)
        scale = lax.rsqrt(jnp.mean(wide * wide, axis=-1, keepdims=True) + 1e-6)
        normed[where, :] = (wide * scale * gain_ref[...]).astype(BF16)

    for k in range(parts):
        p, begin = divmod(k * columns, width)
        copies[k].wait()
        total = jnp.dot(normed[...], held[k, 0], preferred_element_type=F32)
        out_ref[p, :, begin : begin + columns] = total.astype(BF16)


def lr_in(place, gain, blocks, table, weight):
    tokens, width = blocks[0].shape
    _, model, _ = weight.shape
    columns = min(512, width)
    parts = 3 * width // columns
    return pl.pallas_call(
        functools.partial(lr_in_kernel, table),
        out_shape=jax.ShapeDtypeStruct((3, tokens, width), BF16),
        in_specs=[
            pl.BlockSpec(memory_space=pltpu.SMEM),
            *vmem(1 + len(blocks)),
            pl.BlockSpec(memory_space=pl.ANY),
        ],
        out_specs=pl.BlockSpec(memory_space=pltpu.VMEM),
        scratch_shapes=[
            pltpu.VMEM((tokens, model), BF16),
            pltpu.VMEM((tokens, model), BF16),
            pltpu.VMEM((parts, 1, model, columns), BF16),
            pltpu.SemaphoreType.DMA((parts,)),
        ],
        compiler_params=params(40),
        cost_estimate=cost(6 * tokens * model * width, 6 * model * width),
        name="lr_in",
    )(place, gain, *blocks, weight)


def lr_mix_kernel(x_ref, short_ref, rate_ref, q_ref, u_ref, send_ref, raw):
    _, tokens, width = x_ref.shape
    lags = short_ref.shape[0]
    prior = lags - 1
    poles = rate_ref.shape[0]
    for tile in range(width // LANES):
        lanes = slice(tile * LANES, (tile + 1) * LANES)
        for p in range(3):
            put_rows(raw.at[p], prior, tokens, tile, x_ref[p, :, lanes].astype(F32))
    raw3 = raw.reshape(3, tokens + prior, SUB, LANES)
    for p in range(3):
        raw3[p, :prior] = jnp.zeros((prior, SUB, LANES), F32)
    decay = [jnp.exp(-rate_ref[n]) for n in range(poles)]

    def mix(p, first):
        total = short_ref[0, p] * raw3[p, pl.ds(first + prior, STEP)]
        for lag in range(1, lags):
            total = total + short_ref[lag, p] * raw3[p, pl.ds(first + prior - lag, STEP)]
        return total

    def block(index, states):
        first = index * STEP
        q_ref[pl.ds(first, STEP)] = mix(0, first)
        product = mix(1, first) * mix(2, first)
        u_ref[pl.ds(first, STEP)] = product
        states = list(states)
        for t in range(STEP):
            for n in range(poles):
                states[n] = decay[n] * states[n] + product[t]
        return tuple(states)

    nothing = jnp.zeros((SUB, LANES), F32)
    states = lax.fori_loop(0, tokens // STEP, block, (nothing,) * poles)
    rows = [*states]
    rows += [raw3[p, prior + j] for p in (1, 2) for j in range(prior)]
    rows += [raw3[p, tokens + j] for p in range(3) for j in range(prior)]
    for n, row in enumerate(rows):
        send_ref[n] = row.astype(BF16)
    for n in range(len(rows), send_ref.shape[0]):
        send_ref[n] = jnp.zeros((SUB, LANES), BF16)


def lr_mix(x, short_w, rate):
    _, tokens, width = x.shape
    poles = rate.shape[0]
    prior = short_w.shape[0] - 1
    sent = -(-(poles + 5 * prior) // HALO) * HALO
    return pl.pallas_call(
        lr_mix_kernel,
        out_shape=(
            jax.ShapeDtypeStruct((tokens, SUB, LANES), F32),
            jax.ShapeDtypeStruct((tokens, SUB, LANES), F32),
            jax.ShapeDtypeStruct((sent, SUB, LANES), BF16),
        ),
        in_specs=vmem(3),
        out_specs=tuple(vmem(3)),
        scratch_shapes=[pltpu.VMEM((3, (tokens + prior) * SUB, LANES), F32)],
        compiler_params=params(16),
        cost_estimate=cost(1e9, 1e6),
        name="lr_mix",
    )(x, short_w, rate)


def lr_modal_kernel(scalar_ref, q_ref, u_ref, sent_ref, short_ref, rate_ref, res_ref, skip_ref, z_ref, zs, change):
    tokens = q_ref.shape[0]
    width = z_ref.shape[1]
    lags = short_ref.shape[0]
    prior = lags - 1
    poles = rate_ref.shape[0]
    position = scalar_ref[0]
    zs3 = zs.reshape(tokens, SUB, LANES)

    def head(index, p, j):
        return sent_ref[index, poles + (p - 1) * prior + j].astype(F32)

    def tail(index, p, j):
        return sent_ref[index, poles + 2 * prior + p * prior + j].astype(F32)

    def missed(index, p, t):
        total = short_ref[t + 1, p] * tail(index - 1, p, prior - 1)
        for lag in range(t + 2, lags):
            total = total + short_ref[lag, p] * tail(index - 1, p, prior + t - lag)
        return total

    def had(index, p, t):
        total = short_ref[0, p] * head(index, p, t)
        for lag in range(1, t + 1):
            total = total + short_ref[lag, p] * head(index, p, t - lag)
        return total

    def change_of_u(index, t):
        key, value = had(index, 1, t), had(index, 2, t)
        more_key, more_value = missed(index, 1, t), missed(index, 2, t)
        return key * more_value + more_key * value + more_key * more_value

    nothing = jnp.zeros((SUB, LANES), F32)
    change[0] = jnp.zeros((prior, SUB, LANES), F32)

    @pl.loop(1, position + 1)
    def _(index):
        for t in range(prior):
            change[index, t] = change_of_u(index, t)

    decay, weight, enter = [], [], []
    for n in range(poles):
        rate = rate_ref[n]
        decay.append(jnp.exp(-rate))
        weight.append(res_ref[n] * jnp.sqrt(1.0 - jnp.exp(-2.0 * rate)))

        def arrive(index, total, n=n, rate=rate):
            distance = (position - 1 - index).astype(F32)
            end = sent_ref[index, n].astype(F32)
            for t in range(prior):
                end = end + jnp.exp(-rate * (tokens - 1 - t)) * change[index, t]
            return total + jnp.exp(-rate * tokens * distance) * end

        enter.append(lax.fori_loop(0, position, arrive, nothing))

    first_u, first_q = [], []
    for t in range(prior):
        first_u.append(u_ref[t] + change[position, t])
        before = lax.max(position, 1)
        first_q.append(q_ref[t] + jnp.where(position > 0, missed(before, 0, t), 0.0))

    def row(states, value, query):
        total = skip_ref[...] * value
        for n in range(poles):
            states[n] = decay[n] * states[n] + value
            total = total + weight[n] * states[n]
        return query * total

    states = list(enter)
    for t in range(STEP):
        value, query = (first_u[t], first_q[t]) if t < prior else (u_ref[t], q_ref[t])
        zs3[t] = row(states, value, query)

    def block(index, states):
        first = index * STEP
        states = list(states)
        for t in range(STEP):
            zs3[first + t] = row(states, u_ref[first + t], q_ref[first + t])
        return tuple(states)

    lax.fori_loop(1, tokens // STEP, block, tuple(states))
    for tile in range(width // LANES):
        lanes = slice(tile * LANES, (tile + 1) * LANES)
        z_ref[:, lanes] = get_rows(zs, 0, tokens, tile).astype(BF16)


def lr_modal(position, q, u, sent, short_w, rate, res, skip, width):
    tokens = q.shape[0]
    prior = short_w.shape[0] - 1
    return pl.pallas_call(
        lr_modal_kernel,
        out_shape=jax.ShapeDtypeStruct((tokens, width), BF16),
        in_specs=[pl.BlockSpec(memory_space=pltpu.SMEM), *vmem(7)],
        out_specs=pl.BlockSpec(memory_space=pltpu.VMEM),
        scratch_shapes=[
            pltpu.VMEM((tokens * SUB, LANES), F32),
            pltpu.VMEM((sent.shape[0], prior, SUB, LANES), F32),
        ],
        compiler_params=params(16),
        cost_estimate=cost(1e9, 1e6),
        name="lr_modal",
    )(position, q, u, sent, short_w, rate, res, skip)


def local(
    residual_in,
    mr_qkv,
    mr_short_w,
    mr_filter,
    mr_skip,
    mr_out_w,
    lr_gain,
    lr_in_w,
    lr_short_w,
    lr_rate,
    lr_res,
    lr_skip,
    lr_out_w,
):
    sequences, tokens, _, width = mr_qkv.shape
    taps = mr_filter.shape[0]
    prior = mr_short_w.shape[0] - 1
    ctx, tp = lax.axis_size("ctx"), lax.axis_size("tp")
    position = lax.axis_index("ctx").astype(jnp.int32).reshape(1)
    place = lax.axis_index("tp").astype(jnp.int32).reshape(1)
    onward = [(i, i + 1) for i in range(ctx - 1)]

    tail = mr_qkv[:, tokens - taps - prior :].astype(F32)
    mixed = sum(mr_short_w[lag, 1:] * tail[:, prior - lag : prior - lag + taps, 1:] for lag in range(prior + 1))
    tail_u = (mixed[:, :, 0] * mixed[:, :, 1]).astype(BF16)
    last = jnp.swapaxes(mr_qkv[:, tokens - prior :], 1, 2).reshape(sequences, 3 * prior, width)
    last = jnp.pad(last, ((0, 0), (0, HALO - 3 * prior), (0, 0)))
    halo = lax.ppermute(jnp.concatenate([tail_u, last], axis=1), "ctx", onward)

    x = jnp.swapaxes(mr_qkv, 1, 2)
    mr_short, lr_short = tiles(mr_short_w), tiles(lr_short_w)
    mr_taps, mr_direct = tiles(mr_filter), tiles(mr_skip)
    rate, res, lr_direct = tiles(lr_rate), tiles(lr_res), tiles(lr_skip)
    in_w = jnp.swapaxes(lr_in_w, 0, 1)
    gain = lr_gain.reshape(1, -1)

    own = [mr_local(x, mr_short, mr_taps, mr_direct, s) for s in range(sequences)]
    zs = [mr_finish(x, halo, *own[s], mr_short, mr_taps, mr_direct, s) for s in range(sequences)]
    places, mr_weights = swap_gather(mr_out_w, "ctx", own[-1][0], zs[-1])
    early = [k for k, (offset, _, whole) in enumerate(places) if mr_weights[k].shape[1] == whole]
    late = [k for k in range(len(places)) if k not in early]

    def project_pieces(z):
        terms = None
        for ks in (early, late):
            if ks:
                terms = project(z, position, tuple(places[k] for k in ks), [mr_weights[k] for k in ks], tp, terms)
        return terms

    parts = [project_pieces(z) for z in zs]
    lr_places, lr_weights = swap_gather(after(lr_out_w, parts[-1]), "ctx")

    mids, blocks, outs = [], [], []
    before = lr_weights[: -len(late) // 2]
    for s in range(sequences):
        share = lax.psum_scatter(after(parts[s], *parts[:s]), "tp", scatter_dimension=0)
        mid = (residual_in[s].astype(F32) + after(share, *before).astype(F32)).astype(BF16)
        mid = lax.optimization_barrier(mid)
        mids.append(mid)
        arrays, table = line_gather(mid, "tp")
        blocks.append(arrays)
        before = [*lr_weights, *arrays]
    for s in range(sequences):
        more = blocks[s + 1] if s + 1 < sequences else None
        x = lr_in(place, gain, blocks[s], table, in_w)
        if more:
            x = after(x, *more[1:3])
        q, u, send = lr_mix(x, lr_short, rate)
        sent = lax.all_gather(send, "ctx", axis=0)
        if more:
            sent = after(sent, *more[3:5])
        z = lr_modal(position, q, u, sent, lr_short, rate, res, lr_direct, width)
        share = lax.psum_scatter(project(z, position, lr_places, lr_weights, tp), "tp", scatter_dimension=0)
        outs.append((mids[s].astype(F32) + share.astype(F32)).astype(BF16))
    return jnp.stack(outs)


def solution(mesh):
    in_specs = (
        P(None, "ctx", "tp"),
        P(None, "ctx", None, "tp"),
        P(None, None, "tp"),
        P(None, "tp"),
        P("tp"),
        P("tp", "ctx"),
        P(),
        P(None, None, "tp"),
        P(None, None, "tp"),
        P(None, "tp"),
        P(None, "tp"),
        P("tp"),
        P("tp", "ctx"),
    )
    out_specs = P(None, "ctx", "tp")
    return jax.shard_map(local, mesh=mesh, in_specs=in_specs, out_specs=out_specs, check_vma=False)
```

```python
import functools

import jax
import jax.numpy as jnp
from jax import lax
from jax.experimental import pallas as pl
from jax.experimental.pallas import tpu as pltpu
from jax.sharding import PartitionSpec as P

F32 = jnp.float32
BF16 = jnp.bfloat16
LANES = 128
SUB = 8
HALO = 16
STEP = 8
VMEM_MIB = 56


def params(mebibytes, **more):
    return pltpu.CompilerParams(vmem_limit_bytes=mebibytes * 2**20, **more)


def vmem(count):
    return [pl.BlockSpec(memory_space=pltpu.VMEM)] * count


def in_hbm(count):
    return [pl.BlockSpec(memory_space=pltpu.HBM)] * count


def cost(flops, moved):
    return pl.CostEstimate(flops=int(flops), bytes_accessed=int(moved), transcendentals=0)


def tiles(value):
    width = value.shape[-1]
    room = SUB * LANES
    if width < room:
        value = jnp.pad(value, [(0, 0)] * (value.ndim - 1) + [(0, room - width)])
    return value.reshape(value.shape[:-1] + (SUB, LANES)).astype(F32)


def put_rows(flat_ref, first, rows, lane_tile, value):
    flat_ref[pl.ds(first * SUB + lane_tile, rows, stride=SUB), :] = value


def get_rows(flat_ref, first, rows, lane_tile):
    return flat_ref[pl.ds(first * SUB + lane_tile, rows, stride=SUB), :]


def window_sum(filter_ref, source3, base, chunks, totals):
    def chunk(index, totals):
        tap = index * STEP
        window = [source3[base - tap - (STEP - 1) + j] for j in range(2 * STEP - 1)]
        totals = list(totals)
        for k in range(STEP):
            weight = filter_ref[tap + k]
            for t in range(STEP):
                totals[t] = totals[t] + weight * window[t - k + STEP - 1]
        return tuple(totals)

    return lax.fori_loop(*chunks, chunk, tuple(totals))


def mr_local_kernel(x_ref, short_ref, filter_ref, skip_ref, z_ref, q_ref, conv_ref, raw, u, zs):
    _, _, tokens, width = x_ref.shape
    head = q_ref.shape[1]
    taps = filter_ref.shape[0]
    lags = short_ref.shape[0]
    prior = lags - 1
    for tile in range(width // LANES):
        lanes = slice(tile * LANES, (tile + 1) * LANES)
        for p in range(3):
            put_rows(raw.at[p], prior, tokens, tile, x_ref[0, p, :, lanes].astype(F32))
    raw3 = raw.reshape(3, tokens + prior, SUB, LANES)
    u3 = u.reshape(taps + tokens, SUB, LANES)
    zs3 = zs.reshape(tokens, SUB, LANES)
    for p in range(3):
        raw3[p, :prior] = jnp.zeros((prior, SUB, LANES), F32)

    @pl.loop(0, taps // STEP)
    def _(block):
        u3[pl.ds(block * STEP, STEP)] = jnp.zeros((STEP, SUB, LANES), F32)

    def mix(p, first, rows):
        total = short_ref[0, p] * raw3[p, pl.ds(first + prior, rows)]
        for lag in range(1, lags):
            total = total + short_ref[lag, p] * raw3[p, pl.ds(first + prior - lag, rows)]
        return total

    @pl.loop(0, tokens // STEP)
    def _(block):
        first = block * STEP
        product = mix(1, first, STEP) * mix(2, first, STEP)
        u3[pl.ds(taps + first, STEP)] = product.astype(BF16).astype(F32)

    def sums(block):
        first = block * STEP
        totals = [skip_ref[...] * u3[taps + first + t] for t in range(STEP)]
        chunks = (0, lax.min(block + 1, taps // STEP))
        return first, mix(0, first, STEP), window_sum(filter_ref, u3, taps + first, chunks, totals)

    @pl.loop(0, head // STEP)
    def _(block):
        first, queries, totals = sums(block)
        q_ref[0, pl.ds(first, STEP)] = queries
        for t in range(STEP):
            conv_ref[0, first + t] = totals[t]

    @pl.loop(head // STEP, tokens // STEP)
    def _(block):
        first, queries, totals = sums(block)
        for t in range(STEP):
            zs3[first + t] = queries[t] * totals[t]

    for tile in range(width // LANES):
        lanes = slice(tile * LANES, (tile + 1) * LANES)
        z_ref[0, head:, lanes] = get_rows(zs, head, tokens - head, tile).astype(BF16)


def mr_local(x, short_w, taps_w, skip):
    sequences, _, tokens, width = x.shape
    taps = taps_w.shape[0]
    prior = short_w.shape[0] - 1
    head = taps + HALO
    rows = jax.ShapeDtypeStruct((sequences, head, SUB, LANES), F32)
    return pl.pallas_call(
        mr_local_kernel,
        grid=(sequences,),
        out_shape=(jax.ShapeDtypeStruct((sequences, tokens, width), BF16), rows, rows),
        in_specs=[pl.BlockSpec((1, 3, tokens, width), lambda i: (i, 0, 0, 0)), *vmem(3)],
        out_specs=(
            pl.BlockSpec((1, tokens, width), lambda i: (i, 0, 0)),
            *(pl.BlockSpec((1, head, SUB, LANES), lambda i: (i, 0, 0, 0)),) * 2,
        ),
        scratch_shapes=[
            pltpu.VMEM((3, (tokens + prior) * SUB, LANES), F32),
            pltpu.VMEM(((taps + tokens) * SUB, LANES), F32),
            pltpu.VMEM((tokens * SUB, LANES), F32),
        ],
        compiler_params=params(VMEM_MIB),
        cost_estimate=cost(1e9, 1e6),
        name="mr_local",
    )(x, short_w, taps_w, skip)


def mr_finish_kernel(x_ref, halo_ref, q_ref, conv_ref, short_ref, filter_ref, skip_ref, gate_ref, z_ref, raw, extra, zs):
    tokens = q_ref.shape[1]
    width = z_ref.shape[1]
    taps = filter_ref.shape[0]
    lags = short_ref.shape[0]
    prior = lags - 1
    for tile in range(width // LANES):
        lanes = slice(tile * LANES, (tile + 1) * LANES)
        put_rows(extra, 0, taps, tile, halo_ref[0, :taps, lanes].astype(F32))
        tail = halo_ref[0, taps : taps + HALO, lanes].astype(F32)
        for p in range(3):
            put_rows(raw.at[p], 0, prior, tile, tail[prior * p : prior * (p + 1)])
            put_rows(raw.at[p], prior, prior, tile, x_ref[0, p, :, lanes].astype(F32)[:prior])
    raw3 = raw.reshape(3, 2 * prior, SUB, LANES)
    extra3 = extra.reshape(taps + 2 * STEP, SUB, LANES)
    zs3 = zs.reshape(tokens, SUB, LANES)

    def mix(p, t, lowest):
        total = short_ref[0, p] * raw3[p, prior + t]
        for lag in range(1, lags):
            if prior + t - lag >= lowest:
                total = total + short_ref[lag, p] * raw3[p, prior + t - lag]
        return total

    extra3[taps:] = jnp.zeros((2 * STEP, SUB, LANES), F32)
    for t in range(prior):
        whole = (mix(1, t, 0) * mix(2, t, 0)).astype(BF16).astype(F32)
        alone = (mix(1, t, prior) * mix(2, t, prior)).astype(BF16).astype(F32)
        extra3[taps + t] = whole - alone

    def sums(block):
        first = block * STEP
        chunks = (lax.max(block - 1, 0), taps // STEP)
        totals = [conv_ref[0, first + t] for t in range(STEP)]
        return first, window_sum(filter_ref, extra3, taps + first, chunks, totals)

    first, totals = sums(0)
    for t in range(STEP):
        if t < prior:
            zs3[t] = mix(0, t, 0) * (totals[t] + skip_ref[...] * extra3[taps + t])
        else:
            zs3[t] = q_ref[0, t] * totals[t]

    @pl.loop(1, taps // STEP + 1)
    def _(block):
        first, totals = sums(block)
        for t in range(STEP):
            zs3[first + t] = q_ref[0, first + t] * totals[t]

    @pl.loop(taps // STEP + 1, tokens // STEP)
    def _(block):
        where = pl.ds(block * STEP, STEP)
        zs3[where] = q_ref[0, where] * conv_ref[0, where]

    for tile in range(width // LANES):
        lanes = slice(tile * LANES, (tile + 1) * LANES)
        z_ref[:, lanes] = get_rows(zs, 0, tokens, tile).astype(BF16)


def mr_finish(x, halo, q, conv, short_w, taps_w, skip, seq, gate):
    width = x.shape[3]
    head = q.shape[1]
    taps = taps_w.shape[0]
    prior = short_w.shape[0] - 1
    rows = pl.BlockSpec((1, head, SUB, LANES), lambda i: (seq, 0, 0, 0))
    return pl.pallas_call(
        mr_finish_kernel,
        grid=(1,),
        out_shape=jax.ShapeDtypeStruct((head, width), BF16),
        in_specs=[
            pl.BlockSpec((1, 3, HALO, width), lambda i: (seq, 0, 0, 0)),
            pl.BlockSpec((1, halo.shape[1], width), lambda i: (seq, 0, 0)),
            rows,
            rows,
            *vmem(3),
            *in_hbm(1),
        ],
        out_specs=pl.BlockSpec((head, width), lambda i: (0, 0)),
        scratch_shapes=[
            pltpu.VMEM((3, 2 * prior * SUB, LANES), F32),
            pltpu.VMEM(((taps + 2 * STEP) * SUB, LANES), F32),
            pltpu.VMEM((head * SUB, LANES), F32),
        ],
        compiler_params=params(VMEM_MIB),
        cost_estimate=cost(4e10, 1e6),
        name="mr_finish",
    )(x, halo, q, conv, short_w, taps_w, skip, gate)


def place_blocks(places, position, z, copies, held, result, out_ref, out_sems):
    width = out_ref.shape[2]
    sent = []
    begun = 0
    for k, (offset, begin, whole) in enumerate(places):
        columns = held[k].shape[1]
        start = lax.bitwise_xor(position, offset) * whole + begin
        share = lax.div(start, width)
        lanes = pl.ds(pl.multiple_of(lax.rem(start, width), columns), columns)
        mine = slice(begun, begun + columns)
        begun += columns
        copies.get(k)
        result[:, mine] = jnp.dot(z, held[k][...], preferred_element_type=F32).astype(BF16)
        sent.append(pltpu.make_async_copy(result.at[:, mine], out_ref.at[share, :, lanes], out_sems.at[k]))
        sent[-1].start()
    for copy in sent:
        copy.wait()


class Fetch:
    def __init__(self, copies, ahead=3):
        self.copies, self.ahead = copies, ahead

    def begin(self):
        for copies in self.copies[: self.ahead]:
            for copy in copies:
                copy.start()

    def get(self, k):
        for copy in self.copies[k]:
            copy.wait()
        if k + self.ahead < len(self.copies):
            for copy in self.copies[k + self.ahead]:
                copy.start()


def fetch(sources, held, sems):
    return Fetch([(pltpu.make_async_copy(sources[k], held[k], sems.at[k]),) for k in range(len(held))])


def project_kernel(places, seq, scalar_ref, head_ref, body_ref, *refs):
    count = len(places)
    weights = refs[:count]
    out_ref, z_ref, z_sems, result = refs[-6 - count], refs[-5 - count], refs[-4 - count], refs[-3 - count]
    held, in_sems, out_sems = refs[-2 - count : -2], refs[-2], refs[-1]
    head = head_ref.shape[0]
    rest = z_ref.shape[0] - head
    first = pltpu.make_async_copy(head_ref, z_ref.at[pl.ds(0, head)], z_sems.at[0])
    second = pltpu.make_async_copy(body_ref.at[seq, pl.ds(head, rest)], z_ref.at[pl.ds(head, rest)], z_sems.at[1])
    first.start()
    second.start()
    copies = fetch(weights, held, in_sems)
    copies.begin()
    first.wait()
    second.wait()
    place_blocks(places, scalar_ref[0], z_ref[...], copies, held, result, out_ref, out_sems)


def project(z, position, places, weights, shares, given=None):
    head, body, seq = z
    _, tokens, width = body.shape
    total = sum(w.shape[1] for w in weights)
    model = places[0][2] * lax.axis_size("ctx")
    extra = [] if given is None else [given]
    return pl.pallas_call(
        functools.partial(project_kernel, places, seq),
        out_shape=jax.ShapeDtypeStruct((shares, tokens, model // shares), BF16),
        in_specs=[pl.BlockSpec(memory_space=pltpu.SMEM), *in_hbm(2 + len(weights) + len(extra))],
        out_specs=in_hbm(1)[0],
        scratch_shapes=[
            pltpu.VMEM((tokens, width), BF16),
            pltpu.SemaphoreType.DMA((2,)),
            pltpu.VMEM((tokens, total), BF16),
            *[pltpu.VMEM(w.shape, w.dtype) for w in weights],
            pltpu.SemaphoreType.DMA((len(weights),)),
            pltpu.SemaphoreType.DMA((len(weights),)),
        ],
        input_output_aliases={3 + len(weights): 0} if extra else {},
        compiler_params=params(VMEM_MIB),
        cost_estimate=cost(2 * tokens * width * total, 2 * total * (width + tokens)),
        name="project",
    )(position, head, body, *weights, *extra)


def after(value, *others):
    return lax.optimization_barrier((value, *others))[0]


def swap_pairs(axis, bit):
    return [(i, i ^ bit) for i in range(lax.axis_size(axis))]


def together(*values):
    return lax.optimization_barrier(values)


class SwapGather:
    def __init__(self, block, axis):
        count = lax.axis_size(axis)
        self.axis, self.whole = axis, block.shape[1]
        self.far = [1 << k for k in range(count.bit_length() - 1, 0, -1) if 1 << k < count]
        self.arrays = {(0, 0): block}

    def swap(self, value, bit):
        return lax.ppermute(value, self.axis, swap_pairs(self.axis, bit))

    def near(self, keys):
        for offset, begin in keys:
            self.arrays[offset ^ 1, begin] = self.swap(self.arrays[offset, begin], 1)

    def first(self):
        block = self.arrays[0, 0]
        for bit in self.far:
            self.arrays[bit, 0] = self.swap(block, bit)
        self.near([(0, 0)])

    def second(self):
        pieces = 1 << max(1, len(self.far)).bit_length() - 1
        columns = self.whole // pieces
        for piece in range(pieces if len(self.far) > 1 else 0):
            begin = piece * columns
            part = {bit: self.arrays[bit, 0][:, begin : begin + columns] for bit in self.far}
            order = self.far[piece:] + self.far[:piece]
            known = [order[0]]
            for bit in order[1:]:
                for offset in list(known):
                    part[offset ^ bit] = self.swap(part[offset], bit)
                    self.arrays[offset ^ bit, begin] = part[offset ^ bit]
                    known.append(offset ^ bit)
                known.append(bit)
        self.near([(bit, 0) for bit in self.far])

    def third(self):
        self.near([key for key in self.arrays if (key[0] ^ 1, key[1]) not in self.arrays])

    def places(self, keys):
        return tuple((offset, begin, self.whole) for offset, begin in keys)


def add(a, b):
    return (a.astype(F32) + b.astype(F32)).astype(BF16)


def line_part(parts, axis, share):
    return lax.dynamic_index_in_dim(parts, jnp.clip(share, 0, lax.axis_size(axis) - 1), 0, False)


def line_scatter(parts, axis, step, arrived):
    count = lax.axis_size(axis)
    place = lax.axis_index(axis)
    up = [(p, p + 1) for p in range(step)]
    down = [(p, p - 1) for p in range(count - step, count)]
    up_share = count - step + place
    down_share = step - count + place
    if step < count - 1 - step:
        value = line_part(parts, axis, jnp.where(place < step, up_share, down_share))
        if arrived:
            value = add(value, arrived[0])
        return [lax.ppermute(value, axis, up + down)] * 2
    low, high = line_part(parts, axis, up_share), line_part(parts, axis, down_share)
    if arrived:
        low, high = add(low, arrived[0]), add(high, arrived[1])
    return [lax.ppermute(low, axis, up), lax.ppermute(high, axis, down)]


def line_gather(value, axis, step, arrays):
    count = lax.axis_size(axis)

    def move(what, *pairs):
        return lax.ppermute(what, axis, pairs)

    if count == 4:
        if step == 1:
            return [value, move(value, (0, 1), (1, 0), (2, 3), (3, 2)), move(value, (1, 2), (2, 1))]
        if step == 2:
            return arrays + [move(arrays[1], (1, 2), (2, 1)), move(arrays[2], (1, 0), (2, 3))]
        return arrays + [move(arrays[3], (1, 0), (2, 3))]
    if step > 1:
        return arrays
    low, high = [value], [value]
    for hop in range(1, count):
        low.append(move(low[-1], *[(p, p + 1) for p in range(hop - 1, count - 1)]))
        high.append(move(high[-1], *[(p, p - 1) for p in range(1, count - hop + 1)]))
    return low + high[1:]


def line_table(count):
    if count == 4:
        return ((0, 1, 4, 5), (1, 0, 2, 3), (3, 2, 0, 1), (5, 4, 1, 0))
    return tuple(
        tuple(place - share if share <= place else count - 1 + share - place for share in range(count))
        for place in range(count)
    )


def lr_in_start_kernel(table, scalar_ref, gain_ref, *refs):
    count = len(table)
    *blocks, w_ref, total_ref, square_ref, scaled, held, total, sems, out_sems = refs
    tokens, width = blocks[0].shape
    parts, rows, columns = held.shape
    begin = jnp.where(scalar_ref[0] < count // 2, 0, width)
    copies = []
    for k in range(parts):
        p, first = divmod(k * columns, width)
        source = w_ref.at[p, pl.ds(pl.multiple_of(begin, width), rows), pl.ds(first, columns)]
        copies.append((pltpu.make_async_copy(source, held.at[k], sems.at[k]),))
    copies = Fetch(copies, 2)
    copies.begin()
    for place in range(count):
        shares = [share + (place >= count // 2) for share in range(count - 1)]
        sources = [blocks[table[place][share]] for share in shares]

        @pl.when(scalar_ref[0] == place)
        def _(shares=shares, sources=sources):
            @pl.loop(0, tokens // HALO)
            def _(block):
                where = pl.ds(pl.multiple_of(block * HALO, HALO), HALO)
                squares = jnp.zeros((HALO, LANES), F32)
                for k, source in enumerate(sources):
                    wide = source[where, :].astype(F32)
                    for lane in range(0, width, LANES):
                        squares = squares + wide[:, lane : lane + LANES] * wide[:, lane : lane + LANES]
                    gain = gain_ref[:, shares[k] * width : (shares[k] + 1) * width]
                    scaled[where, k * width : (k + 1) * width] = (wide * gain).astype(BF16)
                square_ref[where, :] = squares

    sent = []
    for k in range(parts):
        p, first = divmod(k * columns, width)
        copies.get(k)
        total[k] = jnp.dot(scaled[...], held[k], preferred_element_type=F32)
        sent.append(pltpu.make_async_copy(total.at[k], total_ref.at[k], out_sems.at[k]))
        sent[-1].start()
    for copy in sent:
        copy.wait()


def lr_in_start(place, gain, blocks, table, weight):
    count = len(table)
    tokens, width = blocks[0].shape
    rows = (count - 1) * width
    columns = min(512, width)
    parts = 3 * width // columns
    return pl.pallas_call(
        functools.partial(lr_in_start_kernel, table),
        out_shape=(
            jax.ShapeDtypeStruct((parts, tokens, columns), F32),
            jax.ShapeDtypeStruct((tokens, LANES), F32),
        ),
        in_specs=[pl.BlockSpec(memory_space=pltpu.SMEM), *vmem(1 + len(blocks)), *in_hbm(1)],
        out_specs=(*in_hbm(1), *vmem(1)),
        scratch_shapes=[
            pltpu.VMEM((tokens, rows), BF16),
            pltpu.VMEM((parts, rows, columns), BF16),
            pltpu.VMEM((parts, tokens, columns), F32),
            pltpu.SemaphoreType.DMA((parts,)),
            pltpu.SemaphoreType.DMA((parts,)),
        ],
        compiler_params=params(VMEM_MIB),
        cost_estimate=cost(6 * tokens * rows * width, 6 * rows * width),
        name="lr_in_start",
    )(place, gain, *blocks, weight)


SEGMENTS = 4


def lr_mix_kernel(table, scalar_ref, gain_ref, square_ref, short_ref, rate_ref, total_ref, *refs):
    count = len(table)
    blocks, w_ref, q_out, u_out, send_ref = refs[: len(refs) - 15], *refs[len(refs) - 15 : len(refs) - 11]
    source, scaled, scale, held, begun, raw, q_ref, u_ref, sems, begun_sems, out_sems = refs[len(refs) - 11 :]
    tokens, width = blocks[0].shape
    model = count * width
    parts, _, columns = held.shape
    lags = short_ref.shape[0]
    prior = lags - 1
    poles = rate_ref.shape[0]
    begin = jnp.where(scalar_ref[0] < count // 2, model - width, 0)
    for place in range(count):
        share = count - 1 if place < count // 2 else 0

        @pl.when(scalar_ref[0] == place)
        def _(block=blocks[table[place][share]]):
            pltpu.make_async_copy(block, source, out_sems.at[0, 0]).start()

    copies = []
    for k in range(parts):
        p, first = divmod(k * columns, width)
        weight = w_ref.at[p, pl.ds(pl.multiple_of(begin, width), width), pl.ds(first, columns)]
        both = (
            pltpu.make_async_copy(weight, held.at[k], sems.at[k]),
            pltpu.make_async_copy(total_ref.at[k], begun.at[k], begun_sems.at[k]),
        )
        copies.append(both)
    copies = Fetch(copies)
    copies.begin()
    pltpu.make_async_copy(blocks[0], source, out_sems.at[0, 0]).wait()

    @pl.loop(0, tokens // HALO)
    def _(block):
        where = pl.ds(pl.multiple_of(block * HALO, HALO), HALO)
        wide = source[where, :].astype(F32)
        squares = square_ref[where, :]
        for lane in range(0, width, LANES):
            squares = squares + wide[:, lane : lane + LANES] * wide[:, lane : lane + LANES]
        mean = jnp.sum(squares, axis=-1, keepdims=True) * (1.0 / model)
        scale[where, :] = jnp.broadcast_to(lax.rsqrt(mean + 1e-6), (HALO, LANES))
        gain = gain_ref[:, pl.ds(pl.multiple_of(begin, width), width)]
        scaled[where, :] = (wide * gain).astype(BF16)

    for k in range(parts):
        p, first = divmod(k * columns, width)
        copies.get(k)
        total = jnp.dot(scaled[...], held[k], preferred_element_type=F32)
        for lane in range(0, columns, LANES):
            whole = (total[:, lane : lane + LANES] + begun[k, :, lane : lane + LANES]) * scale[...]
            put_rows(raw.at[p], prior, tokens, (first + lane) // LANES, whole.astype(BF16).astype(F32))

    raw3 = raw.reshape(3, tokens + prior, SUB, LANES)
    for p in range(3):
        raw3[p, :prior] = jnp.zeros((prior, SUB, LANES), F32)
    decay = [jnp.exp(-rate_ref[n]) for n in range(poles)]

    def mix(p, first):
        total = short_ref[0, p] * raw3[p, pl.ds(first + prior, STEP)]
        for lag in range(1, lags):
            total = total + short_ref[lag, p] * raw3[p, pl.ds(first + prior - lag, STEP)]
        return total

    def block(index, states):
        first = index * STEP
        q_ref[pl.ds(first, STEP)] = mix(0, first)
        product = mix(1, first) * mix(2, first)
        u_ref[pl.ds(first, STEP)] = product
        states = list(states)
        for t in range(STEP):
            for n in range(poles):
                states[n] = decay[n] * states[n] + product[t]
        return tuple(states)

    rows = tokens // SEGMENTS

    def moved(segment):
        where = pl.ds(pl.multiple_of(segment * rows, rows), rows)
        return (
            pltpu.make_async_copy(q_ref.at[where], q_out.at[where], out_sems.at[0, segment]),
            pltpu.make_async_copy(u_ref.at[where], u_out.at[where], out_sems.at[1, segment]),
        )

    def segment(index, states):
        steps = rows // STEP
        states = lax.fori_loop(index * steps, (index + 1) * steps, block, states)
        for copy in moved(index):
            copy.start()
        return states

    nothing = jnp.zeros((SUB, LANES), F32)
    states = lax.fori_loop(0, SEGMENTS, segment, (nothing,) * poles)
    lines = [*states]
    lines += [raw3[p, prior + j] for p in (1, 2) for j in range(prior)]
    lines += [raw3[p, tokens + j] for p in range(3) for j in range(prior)]
    for n, line in enumerate(lines):
        send_ref[n] = line.astype(BF16)
    for n in range(len(lines), send_ref.shape[0]):
        send_ref[n] = jnp.zeros((SUB, LANES), BF16)
    for index in range(SEGMENTS):
        for copy in moved(index):
            copy.wait()


def lr_mix(place, gain, begun, blocks, table, weight, short_w, rate):
    tokens, width = blocks[0].shape
    columns = min(512, width)
    parts = 3 * width // columns
    poles = rate.shape[0]
    prior = short_w.shape[0] - 1
    lines = -(-(poles + 5 * prior) // HALO) * HALO
    total, squares = begun
    rows = jax.ShapeDtypeStruct((tokens, SUB, LANES), F32)
    return pl.pallas_call(
        functools.partial(lr_mix_kernel, table),
        out_shape=(rows, rows, jax.ShapeDtypeStruct((lines, SUB, LANES), BF16)),
        in_specs=[pl.BlockSpec(memory_space=pltpu.SMEM), *vmem(4), *in_hbm(2 + len(blocks))],
        out_specs=(*in_hbm(2), *vmem(1)),
        scratch_shapes=[
            pltpu.VMEM((tokens, width), BF16),
            pltpu.VMEM((tokens, width), BF16),
            pltpu.VMEM((tokens, LANES), F32),
            pltpu.VMEM((parts, width, columns), BF16),
            pltpu.VMEM((parts, tokens, columns), F32),
            pltpu.VMEM((3, (tokens + prior) * SUB, LANES), F32),
            pltpu.VMEM((tokens, SUB, LANES), F32),
            pltpu.VMEM((tokens, SUB, LANES), F32),
            pltpu.SemaphoreType.DMA((parts,)),
            pltpu.SemaphoreType.DMA((parts,)),
            pltpu.SemaphoreType.DMA((2, SEGMENTS)),
        ],
        compiler_params=params(VMEM_MIB),
        cost_estimate=cost(6 * tokens * width * width, 6 * width * width),
        name="lr_mix",
    )(place, gain, squares, short_w, rate, total, *blocks, weight)


def lr_modal_kernel(places, scalar_ref, sent_ref, short_ref, rate_ref, res_ref, skip_ref, q_in, u_in, *refs):
    blocks = len(places)
    weights, out_ref, zs, change, z_ref, result = refs[:blocks], *refs[blocks : blocks + 5]
    q_ref, u_ref, row_sems = refs[blocks + 5 : blocks + 8]
    held, in_sems, out_sems = refs[blocks + 8 : -2], refs[-2], refs[-1]
    rows = q_ref.shape[0] // SEGMENTS

    def moved(segment):
        where = pl.ds(pl.multiple_of(segment * rows, rows), rows)
        return (
            pltpu.make_async_copy(q_in.at[where], q_ref.at[where], row_sems.at[0, segment]),
            pltpu.make_async_copy(u_in.at[where], u_ref.at[where], row_sems.at[1, segment]),
        )

    for index in range(SEGMENTS):
        for copy in moved(index):
            copy.start()
    copies = Fetch(fetch(weights, held, in_sems).copies, blocks)
    tokens = q_ref.shape[0]
    width = z_ref.shape[1]
    lags = short_ref.shape[0]
    prior = lags - 1
    poles = rate_ref.shape[0]
    position = scalar_ref[0]
    zs3 = zs.reshape(tokens, SUB, LANES)

    def head(index, p, j):
        return sent_ref[index, poles + (p - 1) * prior + j].astype(F32)

    def tail(index, p, j):
        return sent_ref[index, poles + 2 * prior + p * prior + j].astype(F32)

    def missed(index, p, t):
        total = short_ref[t + 1, p] * tail(index - 1, p, prior - 1)
        for lag in range(t + 2, lags):
            total = total + short_ref[lag, p] * tail(index - 1, p, prior + t - lag)
        return total

    def had(index, p, t):
        total = short_ref[0, p] * head(index, p, t)
        for lag in range(1, t + 1):
            total = total + short_ref[lag, p] * head(index, p, t - lag)
        return total

    def change_of_u(index, t):
        key, value = had(index, 1, t), had(index, 2, t)
        more_key, more_value = missed(index, 1, t), missed(index, 2, t)
        return key * more_value + more_key * value + more_key * more_value

    nothing = jnp.zeros((SUB, LANES), F32)
    change[0] = jnp.zeros((prior, SUB, LANES), F32)

    @pl.loop(1, position + 1)
    def _(index):
        for t in range(prior):
            change[index, t] = change_of_u(index, t)

    decay, weight, enter = [], [], []
    for n in range(poles):
        rate = rate_ref[n]
        decay.append(jnp.exp(-rate))
        weight.append(res_ref[n] * jnp.sqrt(1.0 - jnp.exp(-2.0 * rate)))

        def arrive(index, total, n=n, rate=rate):
            distance = (position - 1 - index).astype(F32)
            end = sent_ref[index, n].astype(F32)
            for t in range(prior):
                end = end + jnp.exp(-rate * (tokens - 1 - t)) * change[index, t]
            return total + jnp.exp(-rate * tokens * distance) * end

        enter.append(lax.fori_loop(0, position, arrive, nothing))

    for copy in moved(0):
        copy.wait()
    copies.begin()
    first_u, first_q = [], []
    for t in range(prior):
        first_u.append(u_ref[t] + change[position, t])
        before = lax.max(position, 1)
        first_q.append(q_ref[t] + jnp.where(position > 0, missed(before, 0, t), 0.0))

    def row(states, value, query):
        total = skip_ref[...] * value
        for n in range(poles):
            states[n] = decay[n] * states[n] + value
            total = total + weight[n] * states[n]
        return query * total

    states = list(enter)
    for t in range(STEP):
        value, query = (first_u[t], first_q[t]) if t < prior else (u_ref[t], q_ref[t])
        zs3[t] = row(states, value, query)

    def block(index, states):
        first = index * STEP
        states = list(states)
        for t in range(STEP):
            zs3[first + t] = row(states, u_ref[first + t], q_ref[first + t])
        return tuple(states)

    steps = rows // STEP
    states = lax.fori_loop(1, steps, block, tuple(states))

    def segment(index, states):
        for copy in moved(index):
            copy.wait()
        return lax.fori_loop(index * steps, (index + 1) * steps, block, states)

    lax.fori_loop(1, SEGMENTS, segment, states)
    for tile in range(width // LANES):
        lanes = slice(tile * LANES, (tile + 1) * LANES)
        z_ref[:, lanes] = get_rows(zs, 0, tokens, tile).astype(BF16)
    place_blocks(places, position, z_ref[...], copies, held, result, out_ref, out_sems)


def lr_modal(position, q, u, sent, short_w, rate, res, skip, width, places, weights, shares):
    tokens = q.shape[0]
    prior = short_w.shape[0] - 1
    total = sum(w.shape[1] for w in weights)
    return pl.pallas_call(
        functools.partial(lr_modal_kernel, places),
        out_shape=jax.ShapeDtypeStruct((shares, tokens, total // shares), BF16),
        in_specs=[pl.BlockSpec(memory_space=pltpu.SMEM), *vmem(5), *in_hbm(2 + len(weights))],
        out_specs=in_hbm(1)[0],
        scratch_shapes=[
            pltpu.VMEM((tokens * SUB, LANES), F32),
            pltpu.VMEM((sent.shape[0], prior, SUB, LANES), F32),
            pltpu.VMEM((tokens, width), BF16),
            pltpu.VMEM((tokens, total), BF16),
            pltpu.VMEM((tokens, SUB, LANES), F32),
            pltpu.VMEM((tokens, SUB, LANES), F32),
            pltpu.SemaphoreType.DMA((2, SEGMENTS)),
            *[pltpu.VMEM(w.shape, w.dtype) for w in weights],
            pltpu.SemaphoreType.DMA((len(weights),)),
            pltpu.SemaphoreType.DMA((len(weights),)),
        ],
        compiler_params=params(VMEM_MIB),
        cost_estimate=cost(2 * tokens * width * total, 2 * total * (width + tokens)),
        name="lr_modal",
    )(position, sent, short_w, rate, res, skip, q, u, *weights)


def local(
    residual_in,
    mr_qkv,
    mr_short_w,
    mr_filter,
    mr_skip,
    mr_out_w,
    lr_gain,
    lr_in_w,
    lr_short_w,
    lr_rate,
    lr_res,
    lr_skip,
    lr_out_w,
):
    sequences, tokens, _, width = mr_qkv.shape
    taps = mr_filter.shape[0]
    prior = mr_short_w.shape[0] - 1
    ctx, tp = lax.axis_size("ctx"), lax.axis_size("tp")
    position = lax.axis_index("ctx").astype(jnp.int32).reshape(1)
    place = lax.axis_index("tp").astype(jnp.int32).reshape(1)
    onward = [(i, i + 1) for i in range(ctx - 1)]

    tail = mr_qkv[:, tokens - taps - prior :].astype(F32)
    mixed = sum(mr_short_w[lag, 1:] * tail[:, prior - lag : prior - lag + taps, 1:] for lag in range(prior + 1))
    tail_u = (mixed[:, :, 0] * mixed[:, :, 1]).astype(BF16)
    last = jnp.swapaxes(mr_qkv[:, tokens - prior :], 1, 2).reshape(sequences, 3 * prior, width)
    last = jnp.pad(last, ((0, 0), (0, HALO - 3 * prior), (0, 0)))
    halo = lax.ppermute(jnp.concatenate([tail_u, last], axis=1), "ctx", onward)

    x = jnp.swapaxes(mr_qkv, 1, 2)
    mr_short, lr_short = tiles(mr_short_w), tiles(lr_short_w)
    mr_taps, mr_direct = tiles(mr_filter), tiles(mr_skip)
    rate, res, lr_direct = tiles(lr_rate), tiles(lr_res), tiles(lr_skip)
    in_w = jnp.swapaxes(lr_in_w, 0, 1)
    gain = lr_gain.reshape(1, -1)

    def scattered(parts):
        return lax.psum_scatter(parts, "tp", scatter_dimension=0)

    def as_mid(s, *terms):
        total = residual_in[s].astype(F32)
        for term in terms:
            total = total + term.astype(F32)
        return lax.optimization_barrier(total.astype(BF16))

    table = line_table(tp)
    assert sequences == 2

    mr_w = SwapGather(mr_out_w, "ctx")
    mr_w.first()
    body, q, conv = mr_local(x, mr_short, mr_taps, mr_direct)
    mr_w.arrays, halo = together(mr_w.arrays, halo)

    early = list(mr_w.arrays)
    mr_w.second()
    early = [k for k in mr_w.arrays if k in early or (k[0] ^ 1, k[1]) in early]
    head = mr_finish(x, halo, q, conv, mr_short, mr_taps, mr_direct, 0, conv)
    z = head, body, 0
    first = project(z, position, mr_w.places(early), [mr_w.arrays[k] for k in early], tp)
    mr_w.arrays, first = together(mr_w.arrays, first)

    mr_w.third()
    late = [k for k in mr_w.arrays if k not in early]
    if late:
        first = project(z, position, mr_w.places(late), [mr_w.arrays[k] for k in late], tp, first)
    share = scattered(first)

    lr_w = SwapGather(after(lr_out_w, first), "ctx")
    lr_w.first()
    head = mr_finish(x, halo, q, conv, mr_short, mr_taps, mr_direct, 1, first)
    second = project((head, body, 1), position, mr_w.places(mr_w.arrays), list(mr_w.arrays.values()), tp)
    lr_w.arrays, second = together(lr_w.arrays, second)
    lr_w.second()
    lr_w.arrays, share = together(lr_w.arrays, share)

    def near(blocks):
        return blocks[:5] if tp == 4 else blocks

    def scatter_all(parts, steps, arrived):
        for step in steps:
            arrived = line_scatter(parts, "tp", step, arrived)
        return arrived

    mids = [as_mid(0, share)]
    blocks = line_gather(mids[0], "tp", 1, None)
    lr_w.third()
    blocks, second, lr_w.arrays = together(blocks, second, lr_w.arrays)
    blocks = line_gather(mids[0], "tp", 2, blocks)
    arrived = line_scatter(second, "tp", 1, None)
    blocks, arrived = together(blocks, arrived)
    blocks = line_gather(mids[0], "tp", 3, blocks)
    arrived = line_scatter(second, "tp", 2, arrived)
    begun = lr_in_start(place, gain, near(blocks), table, in_w)
    blocks, arrived, begun = together(blocks, arrived, begun)
    arrived = scatter_all(second, range(3, tp), arrived)
    q, u, send = lr_mix(place, gain, begun, blocks, table, in_w, lr_short, rate)
    arrived, q, u, send = together(arrived, q, u, send)
    mids.append(as_mid(1, line_part(second, "tp", lax.axis_index("tp")), *arrived))
    blocks = line_gather(mids[1], "tp", 1, None)
    sent = lax.all_gather(send, "ctx", axis=0)
    blocks, sent, q, u = together(blocks, sent, q, u)
    blocks = line_gather(mids[1], "tp", 2, blocks)
    lr_places, lr_weights = lr_w.places(lr_w.arrays), list(lr_w.arrays.values())
    modal_w = (lr_short, rate, res, lr_direct, width, lr_places, lr_weights, tp)
    first = lr_modal(position, q, u, sent, *modal_w)
    blocks, first = together(blocks, first)
    begun = lr_in_start(place, gain, near(blocks), table, in_w)
    blocks = line_gather(mids[1], "tp", 3, blocks)
    blocks, begun, first = together(blocks, begun, first)
    share = scattered(first)
    q, u, send = lr_mix(place, gain, begun, blocks, table, in_w, lr_short, rate)
    sent = lax.all_gather(send, "ctx", axis=0)
    second = lr_modal(position, q, u, sent, *modal_w)
    out = (mids[0].astype(F32) + share.astype(F32)).astype(BF16)
    out, second = together(jnp.stack([out, mids[1]]), second)
    last = (out[1].astype(F32) + scattered(second).astype(F32)).astype(BF16)
    return out.at[1].set(last)


def solution(mesh):
    in_specs = (
        P(None, "ctx", "tp"),
        P(None, "ctx", None, "tp"),
        P(None, None, "tp"),
        P(None, "tp"),
        P("tp"),
        P("tp", "ctx"),
        P(),
        P(None, None, "tp"),
        P(None, None, "tp"),
        P(None, "tp"),
        P(None, "tp"),
        P("tp"),
        P("tp", "ctx"),
    )
    out_specs = P(None, "ctx", "tp")
    return jax.shard_map(local, mesh=mesh, in_specs=in_specs, out_specs=out_specs, check_vma=False)
```

```python
import functools

import jax
import jax.numpy as jnp
from jax import lax
from jax.experimental import pallas as pl
from jax.experimental.pallas import tpu as pltpu
from jax.sharding import PartitionSpec as P

F32 = jnp.float32
BF16 = jnp.bfloat16
LANES = 128
SUB = 8
HALO = 16
STEP = 8
VMEM_MIB = 56


def params(mebibytes, **more):
    return pltpu.CompilerParams(vmem_limit_bytes=mebibytes * 2**20, **more)


def vmem(count):
    return [pl.BlockSpec(memory_space=pltpu.VMEM)] * count


def in_hbm(count):
    return [pl.BlockSpec(memory_space=pltpu.HBM)] * count


def cost(flops, moved):
    return pl.CostEstimate(flops=int(flops), bytes_accessed=int(moved), transcendentals=0)


def tiles(value):
    width = value.shape[-1]
    room = SUB * LANES
    if width < room:
        value = jnp.pad(value, [(0, 0)] * (value.ndim - 1) + [(0, room - width)])
    return value.reshape(value.shape[:-1] + (SUB, LANES)).astype(F32)


def put_rows(flat_ref, first, rows, lane_tile, value):
    flat_ref[pl.ds(first * SUB + lane_tile, rows, stride=SUB), :] = value


def get_rows(flat_ref, first, rows, lane_tile):
    return flat_ref[pl.ds(first * SUB + lane_tile, rows, stride=SUB), :]


def window_sum(filter_ref, source3, base, chunks, totals):
    def chunk(index, totals):
        tap = index * STEP
        window = [source3[base - tap - (STEP - 1) + j] for j in range(2 * STEP - 1)]
        totals = list(totals)
        for k in range(STEP):
            weight = filter_ref[tap + k]
            for t in range(STEP):
                totals[t] = totals[t] + weight * window[t - k + STEP - 1]
        return tuple(totals)

    return lax.fori_loop(*chunks, chunk, tuple(totals))


def mr_local_kernel(x_ref, short_ref, filter_ref, skip_ref, z_ref, q_ref, conv_ref, raw, u, zs):
    _, _, tokens, width = x_ref.shape
    head = q_ref.shape[1]
    taps = filter_ref.shape[0]
    lags = short_ref.shape[0]
    prior = lags - 1
    for tile in range(width // LANES):
        lanes = slice(tile * LANES, (tile + 1) * LANES)
        for p in range(3):
            put_rows(raw.at[p], prior, tokens, tile, x_ref[0, p, :, lanes].astype(F32))
    raw3 = raw.reshape(3, tokens + prior, SUB, LANES)
    u3 = u.reshape(taps + tokens, SUB, LANES)
    zs3 = zs.reshape(tokens, SUB, LANES)
    for p in range(3):
        raw3[p, :prior] = jnp.zeros((prior, SUB, LANES), F32)

    @pl.loop(0, taps // STEP)
    def _(block):
        u3[pl.ds(block * STEP, STEP)] = jnp.zeros((STEP, SUB, LANES), F32)

    def mix(p, first, rows):
        total = short_ref[0, p] * raw3[p, pl.ds(first + prior, rows)]
        for lag in range(1, lags):
            total = total + short_ref[lag, p] * raw3[p, pl.ds(first + prior - lag, rows)]
        return total

    @pl.loop(0, tokens // STEP)
    def _(block):
        first = block * STEP
        product = mix(1, first, STEP) * mix(2, first, STEP)
        u3[pl.ds(taps + first, STEP)] = product.astype(BF16).astype(F32)

    def sums(block):
        first = block * STEP
        totals = [skip_ref[...] * u3[taps + first + t] for t in range(STEP)]
        chunks = (0, lax.min(block + 1, taps // STEP))
        return first, mix(0, first, STEP), window_sum(filter_ref, u3, taps + first, chunks, totals)

    @pl.loop(0, head // STEP)
    def _(block):
        first, queries, totals = sums(block)
        q_ref[0, pl.ds(first, STEP)] = queries
        for t in range(STEP):
            conv_ref[0, first + t] = totals[t]

    @pl.loop(head // STEP, tokens // STEP)
    def _(block):
        first, queries, totals = sums(block)
        for t in range(STEP):
            zs3[first + t] = queries[t] * totals[t]

    for tile in range(width // LANES):
        lanes = slice(tile * LANES, (tile + 1) * LANES)
        z_ref[0, head:, lanes] = get_rows(zs, head, tokens - head, tile).astype(BF16)


def mr_local(x, short_w, taps_w, skip):
    sequences, _, tokens, width = x.shape
    taps = taps_w.shape[0]
    prior = short_w.shape[0] - 1
    head = taps + HALO
    rows = jax.ShapeDtypeStruct((sequences, head, SUB, LANES), F32)
    return pl.pallas_call(
        mr_local_kernel,
        grid=(sequences,),
        out_shape=(jax.ShapeDtypeStruct((sequences, tokens, width), BF16), rows, rows),
        in_specs=[pl.BlockSpec((1, 3, tokens, width), lambda i: (i, 0, 0, 0)), *vmem(3)],
        out_specs=(
            pl.BlockSpec((1, tokens, width), lambda i: (i, 0, 0)),
            *(pl.BlockSpec((1, head, SUB, LANES), lambda i: (i, 0, 0, 0)),) * 2,
        ),
        scratch_shapes=[
            pltpu.VMEM((3, (tokens + prior) * SUB, LANES), F32),
            pltpu.VMEM(((taps + tokens) * SUB, LANES), F32),
            pltpu.VMEM((tokens * SUB, LANES), F32),
        ],
        compiler_params=params(VMEM_MIB),
        cost_estimate=cost(1e9, 1e6),
        name="mr_local",
    )(x, short_w, taps_w, skip)


def mr_finish_kernel(x_ref, halo_ref, q_ref, conv_ref, short_ref, filter_ref, skip_ref, gate_ref, z_ref, raw, extra, zs):
    tokens = q_ref.shape[1]
    width = z_ref.shape[1]
    taps = filter_ref.shape[0]
    lags = short_ref.shape[0]
    prior = lags - 1
    for tile in range(width // LANES):
        lanes = slice(tile * LANES, (tile + 1) * LANES)
        put_rows(extra, 0, taps, tile, halo_ref[0, :taps, lanes].astype(F32))
        tail = halo_ref[0, taps : taps + HALO, lanes].astype(F32)
        for p in range(3):
            put_rows(raw.at[p], 0, prior, tile, tail[prior * p : prior * (p + 1)])
            put_rows(raw.at[p], prior, prior, tile, x_ref[0, p, :, lanes].astype(F32)[:prior])
    raw3 = raw.reshape(3, 2 * prior, SUB, LANES)
    extra3 = extra.reshape(taps + 2 * STEP, SUB, LANES)
    zs3 = zs.reshape(tokens, SUB, LANES)

    def mix(p, t, lowest):
        total = short_ref[0, p] * raw3[p, prior + t]
        for lag in range(1, lags):
            if prior + t - lag >= lowest:
                total = total + short_ref[lag, p] * raw3[p, prior + t - lag]
        return total

    extra3[taps:] = jnp.zeros((2 * STEP, SUB, LANES), F32)
    for t in range(prior):
        whole = (mix(1, t, 0) * mix(2, t, 0)).astype(BF16).astype(F32)
        alone = (mix(1, t, prior) * mix(2, t, prior)).astype(BF16).astype(F32)
        extra3[taps + t] = whole - alone

    def sums(block):
        first = block * STEP
        chunks = (lax.max(block - 1, 0), taps // STEP)
        totals = [conv_ref[0, first + t] for t in range(STEP)]
        return first, window_sum(filter_ref, extra3, taps + first, chunks, totals)

    first, totals = sums(0)
    for t in range(STEP):
        if t < prior:
            zs3[t] = mix(0, t, 0) * (totals[t] + skip_ref[...] * extra3[taps + t])
        else:
            zs3[t] = q_ref[0, t] * totals[t]

    @pl.loop(1, taps // STEP + 1)
    def _(block):
        first, totals = sums(block)
        for t in range(STEP):
            zs3[first + t] = q_ref[0, first + t] * totals[t]

    @pl.loop(taps // STEP + 1, tokens // STEP)
    def _(block):
        where = pl.ds(block * STEP, STEP)
        zs3[where] = q_ref[0, where] * conv_ref[0, where]

    for tile in range(width // LANES):
        lanes = slice(tile * LANES, (tile + 1) * LANES)
        z_ref[:, lanes] = get_rows(zs, 0, tokens, tile).astype(BF16)


def mr_finish(x, halo, q, conv, short_w, taps_w, skip, seq, gate):
    width = x.shape[3]
    head = q.shape[1]
    taps = taps_w.shape[0]
    prior = short_w.shape[0] - 1
    rows = pl.BlockSpec((1, head, SUB, LANES), lambda i: (seq, 0, 0, 0))
    return pl.pallas_call(
        mr_finish_kernel,
        grid=(1,),
        out_shape=jax.ShapeDtypeStruct((head, width), BF16),
        in_specs=[
            pl.BlockSpec((1, 3, HALO, width), lambda i: (seq, 0, 0, 0)),
            pl.BlockSpec((1, halo.shape[1], width), lambda i: (seq, 0, 0)),
            rows,
            rows,
            *vmem(3),
            *in_hbm(1),
        ],
        out_specs=pl.BlockSpec((head, width), lambda i: (0, 0)),
        scratch_shapes=[
            pltpu.VMEM((3, 2 * prior * SUB, LANES), F32),
            pltpu.VMEM(((taps + 2 * STEP) * SUB, LANES), F32),
            pltpu.VMEM((head * SUB, LANES), F32),
        ],
        compiler_params=params(VMEM_MIB),
        cost_estimate=cost(4e10, 1e6),
        name="mr_finish",
    )(x, halo, q, conv, short_w, taps_w, skip, gate)


def place_blocks(places, position, z, copies, held, result, out_ref, out_sems):
    width = out_ref.shape[2]
    sent = []
    begun = 0
    for k, (offset, begin, whole) in enumerate(places):
        columns = held[k].shape[1]
        start = lax.bitwise_xor(position, offset) * whole + begin
        share = lax.div(start, width)
        lanes = pl.ds(pl.multiple_of(lax.rem(start, width), columns), columns)
        mine = slice(begun, begun + columns)
        begun += columns
        copies.get(k)
        result[:, mine] = jnp.dot(z, held[k][...], preferred_element_type=F32).astype(BF16)
        sent.append(pltpu.make_async_copy(result.at[:, mine], out_ref.at[share, :, lanes], out_sems.at[k]))
        sent[-1].start()
    for copy in sent:
        copy.wait()


class Fetch:
    def __init__(self, copies, ahead=3):
        self.copies, self.ahead = copies, ahead

    def begin(self):
        for copies in self.copies[: self.ahead]:
            for copy in copies:
                copy.start()

    def get(self, k):
        for copy in self.copies[k]:
            copy.wait()
        if k + self.ahead < len(self.copies):
            for copy in self.copies[k + self.ahead]:
                copy.start()


def fetch(sources, held, sems):
    return Fetch([(pltpu.make_async_copy(sources[k], held[k], sems.at[k]),) for k in range(len(held))])


def project_kernel(places, seq, scalar_ref, head_ref, body_ref, *refs):
    count = len(places)
    weights = refs[:count]
    out_ref, z_ref, z_sems, result = refs[-6 - count], refs[-5 - count], refs[-4 - count], refs[-3 - count]
    held, in_sems, out_sems = refs[-2 - count : -2], refs[-2], refs[-1]
    head = head_ref.shape[0]
    rest = z_ref.shape[0] - head
    first = pltpu.make_async_copy(head_ref, z_ref.at[pl.ds(0, head)], z_sems.at[0])
    second = pltpu.make_async_copy(body_ref.at[seq, pl.ds(head, rest)], z_ref.at[pl.ds(head, rest)], z_sems.at[1])
    first.start()
    second.start()
    copies = fetch(weights, held, in_sems)
    copies.begin()
    first.wait()
    second.wait()
    place_blocks(places, scalar_ref[0], z_ref[...], copies, held, result, out_ref, out_sems)


def project(z, position, places, weights, shares, given=None):
    head, body, seq = z
    _, tokens, width = body.shape
    total = sum(w.shape[1] for w in weights)
    model = places[0][2] * lax.axis_size("ctx")
    extra = [] if given is None else [given]
    return pl.pallas_call(
        functools.partial(project_kernel, places, seq),
        out_shape=jax.ShapeDtypeStruct((shares, tokens, model // shares), BF16),
        in_specs=[pl.BlockSpec(memory_space=pltpu.SMEM), *in_hbm(2 + len(weights) + len(extra))],
        out_specs=in_hbm(1)[0],
        scratch_shapes=[
            pltpu.VMEM((tokens, width), BF16),
            pltpu.SemaphoreType.DMA((2,)),
            pltpu.VMEM((tokens, total), BF16),
            *[pltpu.VMEM(w.shape, w.dtype) for w in weights],
            pltpu.SemaphoreType.DMA((len(weights),)),
            pltpu.SemaphoreType.DMA((len(weights),)),
        ],
        input_output_aliases={3 + len(weights): 0} if extra else {},
        compiler_params=params(VMEM_MIB),
        cost_estimate=cost(2 * tokens * width * total, 2 * total * (width + tokens)),
        name="project",
    )(position, head, body, *weights, *extra)


def after(value, *others):
    return lax.optimization_barrier((value, *others))[0]


def swap_pairs(axis, bit):
    return [(i, i ^ bit) for i in range(lax.axis_size(axis))]


def together(*values):
    return lax.optimization_barrier(values)


class SwapGather:
    def __init__(self, block, axis):
        count = lax.axis_size(axis)
        self.axis, self.whole = axis, block.shape[1]
        self.far = [1 << k for k in range(count.bit_length() - 1, 0, -1) if 1 << k < count]
        self.arrays = {(0, 0): block}

    def swap(self, value, bit):
        return lax.ppermute(value, self.axis, swap_pairs(self.axis, bit))

    def near(self, keys):
        for offset, begin in keys:
            self.arrays[offset ^ 1, begin] = self.swap(self.arrays[offset, begin], 1)

    def first(self):
        block = self.arrays[0, 0]
        for bit in self.far:
            self.arrays[bit, 0] = self.swap(block, bit)
        self.near([(0, 0)])

    def second(self):
        pieces = 1 << max(1, len(self.far)).bit_length() - 1
        columns = self.whole // pieces
        for piece in range(pieces if len(self.far) > 1 else 0):
            begin = piece * columns
            part = {bit: self.arrays[bit, 0][:, begin : begin + columns] for bit in self.far}
            order = self.far[piece:] + self.far[:piece]
            known = [order[0]]
            for bit in order[1:]:
                for offset in list(known):
                    part[offset ^ bit] = self.swap(part[offset], bit)
                    self.arrays[offset ^ bit, begin] = part[offset ^ bit]
                    known.append(offset ^ bit)
                known.append(bit)
        self.near([(bit, 0) for bit in self.far])

    def third(self):
        self.near([key for key in self.arrays if (key[0] ^ 1, key[1]) not in self.arrays])

    def places(self, keys):
        return tuple((offset, begin, self.whole) for offset, begin in keys)


def add(a, b):
    return (a.astype(F32) + b.astype(F32)).astype(BF16)


def line_part(parts, axis, share):
    return lax.dynamic_index_in_dim(parts, jnp.clip(share, 0, lax.axis_size(axis) - 1), 0, False)


def line_scatter(parts, axis, step, arrived):
    count = lax.axis_size(axis)
    place = lax.axis_index(axis)
    up = [(p, p + 1) for p in range(step)]
    down = [(p, p - 1) for p in range(count - step, count)]
    up_share = count - step + place
    down_share = step - count + place
    if step < count - 1 - step:
        value = line_part(parts, axis, jnp.where(place < step, up_share, down_share))
        if arrived:
            value = add(value, arrived[0])
        return [lax.ppermute(value, axis, up + down)] * 2
    if step <= count - step:
        value = line_part(parts, axis, jnp.where(place < step, up_share, down_share))
        if arrived:
            value = add(value, arrived[0] if arrived[0] is arrived[1] else jnp.where(place < step, *arrived))
        return [lax.ppermute(value, axis, up), lax.ppermute(value, axis, down)]
    low, high = line_part(parts, axis, up_share), line_part(parts, axis, down_share)
    if arrived:
        low, high = add(low, arrived[0]), add(high, arrived[1])
    return [lax.ppermute(low, axis, up), lax.ppermute(high, axis, down)]


def line_gather(value, axis, step, arrays):
    count = lax.axis_size(axis)

    def move(what, *pairs):
        return lax.ppermute(what, axis, pairs)

    if count == 4:
        if step == 1:
            return [value, move(value, (0, 1), (1, 0), (2, 3), (3, 2)), move(value, (1, 2), (2, 1))]
        if step == 2:
            return arrays + [move(arrays[1], (1, 2), (2, 1)), move(arrays[2], (1, 0), (2, 3))]
        return arrays + [move(arrays[3], (1, 0), (2, 3))]
    if step > 1:
        return arrays
    low, high = [value], [value]
    for hop in range(1, count):
        low.append(move(low[-1], *[(p, p + 1) for p in range(hop - 1, count - 1)]))
        high.append(move(high[-1], *[(p, p - 1) for p in range(1, count - hop + 1)]))
    return low + high[1:]


def line_table(count):
    if count == 4:
        return ((0, 1, 4, 5), (1, 0, 2, 3), (3, 2, 0, 1), (5, 4, 1, 0))
    return tuple(
        tuple(place - share if share <= place else count - 1 + share - place for share in range(count))
        for place in range(count)
    )


def lr_in_start_kernel(table, scalar_ref, gain_ref, *refs):
    count = len(table)
    *blocks, w_ref, total_ref, square_ref, scaled, held, total, sems, out_sems = refs
    tokens, width = blocks[0].shape
    parts, rows, columns = held.shape
    begin = jnp.where(scalar_ref[0] < count // 2, 0, width)
    copies = []
    for k in range(parts):
        p, first = divmod(k * columns, width)
        source = w_ref.at[p, pl.ds(pl.multiple_of(begin, width), rows), pl.ds(first, columns)]
        copies.append((pltpu.make_async_copy(source, held.at[k], sems.at[k]),))
    copies = Fetch(copies, 2)
    copies.begin()
    for place in range(count):
        shares = [share + (place >= count // 2) for share in range(count - 1)]
        sources = [blocks[table[place][share]] for share in shares]

        @pl.when(scalar_ref[0] == place)
        def _(shares=shares, sources=sources):
            @pl.loop(0, tokens // HALO)
            def _(block):
                where = pl.ds(pl.multiple_of(block * HALO, HALO), HALO)
                squares = jnp.zeros((HALO, LANES), F32)
                for k, source in enumerate(sources):
                    wide = source[where, :].astype(F32)
                    for lane in range(0, width, LANES):
                        squares = squares + wide[:, lane : lane + LANES] * wide[:, lane : lane + LANES]
                    gain = gain_ref[:, shares[k] * width : (shares[k] + 1) * width]
                    scaled[where, k * width : (k + 1) * width] = (wide * gain).astype(BF16)
                square_ref[where, :] = squares

    sent = []
    for k in range(parts):
        p, first = divmod(k * columns, width)
        copies.get(k)
        total[k] = jnp.dot(scaled[...], held[k], preferred_element_type=F32)
        sent.append(pltpu.make_async_copy(total.at[k], total_ref.at[k], out_sems.at[k]))
        sent[-1].start()
    for copy in sent:
        copy.wait()


def lr_in_start(place, gain, blocks, table, weight):
    count = len(table)
    tokens, width = blocks[0].shape
    rows = (count - 1) * width
    columns = min(512, width)
    parts = 3 * width // columns
    return pl.pallas_call(
        functools.partial(lr_in_start_kernel, table),
        out_shape=(
            jax.ShapeDtypeStruct((parts, tokens, columns), F32),
            jax.ShapeDtypeStruct((tokens, LANES), F32),
        ),
        in_specs=[pl.BlockSpec(memory_space=pltpu.SMEM), *vmem(1 + len(blocks)), *in_hbm(1)],
        out_specs=(*in_hbm(1), *vmem(1)),
        scratch_shapes=[
            pltpu.VMEM((tokens, rows), BF16),
            pltpu.VMEM((parts, rows, columns), BF16),
            pltpu.VMEM((parts, tokens, columns), F32),
            pltpu.SemaphoreType.DMA((parts,)),
            pltpu.SemaphoreType.DMA((parts,)),
        ],
        compiler_params=params(VMEM_MIB),
        cost_estimate=cost(6 * tokens * rows * width, 6 * rows * width),
        name="lr_in_start",
    )(place, gain, *blocks, weight)


SEGMENTS = 4


def lr_mix_kernel(table, scalar_ref, gain_ref, square_ref, short_ref, rate_ref, total_ref, *refs):
    count = len(table)
    blocks, w_ref, q_out, u_out, send_ref = refs[: len(refs) - 15], *refs[len(refs) - 15 : len(refs) - 11]
    source, scaled, scale, held, begun, raw, q_ref, u_ref, sems, begun_sems, out_sems = refs[len(refs) - 11 :]
    tokens, width = blocks[0].shape
    model = count * width
    parts, _, columns = held.shape
    lags = short_ref.shape[0]
    prior = lags - 1
    poles = rate_ref.shape[0]
    begin = jnp.where(scalar_ref[0] < count // 2, model - width, 0)
    for place in range(count):
        share = count - 1 if place < count // 2 else 0

        @pl.when(scalar_ref[0] == place)
        def _(block=blocks[table[place][share]]):
            pltpu.make_async_copy(block, source, out_sems.at[0, 0]).start()

    copies = []
    for k in range(parts):
        p, first = divmod(k * columns, width)
        weight = w_ref.at[p, pl.ds(pl.multiple_of(begin, width), width), pl.ds(first, columns)]
        both = (
            pltpu.make_async_copy(weight, held.at[k], sems.at[k]),
            pltpu.make_async_copy(total_ref.at[k], begun.at[k], begun_sems.at[k]),
        )
        copies.append(both)
    copies = Fetch(copies)
    copies.begin()
    pltpu.make_async_copy(blocks[0], source, out_sems.at[0, 0]).wait()

    @pl.loop(0, tokens // HALO)
    def _(block):
        where = pl.ds(pl.multiple_of(block * HALO, HALO), HALO)
        wide = source[where, :].astype(F32)
        squares = square_ref[where, :]
        for lane in range(0, width, LANES):
            squares = squares + wide[:, lane : lane + LANES] * wide[:, lane : lane + LANES]
        mean = jnp.sum(squares, axis=-1, keepdims=True) * (1.0 / model)
        scale[where, :] = jnp.broadcast_to(lax.rsqrt(mean + 1e-6), (HALO, LANES))
        gain = gain_ref[:, pl.ds(pl.multiple_of(begin, width), width)]
        scaled[where, :] = (wide * gain).astype(BF16)

    for k in range(parts):
        p, first = divmod(k * columns, width)
        copies.get(k)
        total = jnp.dot(scaled[...], held[k], preferred_element_type=F32)
        for lane in range(0, columns, LANES):
            whole = (total[:, lane : lane + LANES] + begun[k, :, lane : lane + LANES]) * scale[...]
            put_rows(raw.at[p], prior, tokens, (first + lane) // LANES, whole.astype(BF16).astype(F32))

    raw3 = raw.reshape(3, tokens + prior, SUB, LANES)
    for p in range(3):
        raw3[p, :prior] = jnp.zeros((prior, SUB, LANES), F32)
    decay = [jnp.exp(-rate_ref[n]) for n in range(poles)]

    def mix(p, first):
        total = short_ref[0, p] * raw3[p, pl.ds(first + prior, STEP)]
        for lag in range(1, lags):
            total = total + short_ref[lag, p] * raw3[p, pl.ds(first + prior - lag, STEP)]
        return total

    def block(index, states):
        first = index * STEP
        q_ref[pl.ds(first, STEP)] = mix(0, first)
        product = mix(1, first) * mix(2, first)
        u_ref[pl.ds(first, STEP)] = product
        states = list(states)
        for t in range(STEP):
            for n in range(poles):
                states[n] = decay[n] * states[n] + product[t]
        return tuple(states)

    rows = tokens // SEGMENTS

    def moved(segment):
        where = pl.ds(pl.multiple_of(segment * rows, rows), rows)
        return (
            pltpu.make_async_copy(q_ref.at[where], q_out.at[where], out_sems.at[0, segment]),
            pltpu.make_async_copy(u_ref.at[where], u_out.at[where], out_sems.at[1, segment]),
        )

    def segment(index, states):
        steps = rows // STEP
        states = lax.fori_loop(index * steps, (index + 1) * steps, block, states)
        for copy in moved(index):
            copy.start()
        return states

    nothing = jnp.zeros((SUB, LANES), F32)
    states = lax.fori_loop(0, SEGMENTS, segment, (nothing,) * poles)
    lines = [*states]
    lines += [raw3[p, prior + j] for p in (1, 2) for j in range(prior)]
    lines += [raw3[p, tokens + j] for p in range(3) for j in range(prior)]
    for n, line in enumerate(lines):
        send_ref[n] = line.astype(BF16)
    for n in range(len(lines), send_ref.shape[0]):
        send_ref[n] = jnp.zeros((SUB, LANES), BF16)
    for index in range(SEGMENTS):
        for copy in moved(index):
            copy.wait()


def lr_mix(place, gain, begun, blocks, table, weight, short_w, rate):
    tokens, width = blocks[0].shape
    columns = min(512, width)
    parts = 3 * width // columns
    poles = rate.shape[0]
    prior = short_w.shape[0] - 1
    lines = -(-(poles + 5 * prior) // HALO) * HALO
    total, squares = begun
    rows = jax.ShapeDtypeStruct((tokens, SUB, LANES), F32)
    return pl.pallas_call(
        functools.partial(lr_mix_kernel, table),
        out_shape=(rows, rows, jax.ShapeDtypeStruct((lines, SUB, LANES), BF16)),
        in_specs=[pl.BlockSpec(memory_space=pltpu.SMEM), *vmem(4), *in_hbm(2 + len(blocks))],
        out_specs=(*in_hbm(2), *vmem(1)),
        scratch_shapes=[
            pltpu.VMEM((tokens, width), BF16),
            pltpu.VMEM((tokens, width), BF16),
            pltpu.VMEM((tokens, LANES), F32),
            pltpu.VMEM((parts, width, columns), BF16),
            pltpu.VMEM((parts, tokens, columns), F32),
            pltpu.VMEM((3, (tokens + prior) * SUB, LANES), F32),
            pltpu.VMEM((tokens, SUB, LANES), F32),
            pltpu.VMEM((tokens, SUB, LANES), F32),
            pltpu.SemaphoreType.DMA((parts,)),
            pltpu.SemaphoreType.DMA((parts,)),
            pltpu.SemaphoreType.DMA((2, SEGMENTS)),
        ],
        compiler_params=params(VMEM_MIB),
        cost_estimate=cost(6 * tokens * width * width, 6 * width * width),
        name="lr_mix",
    )(place, gain, squares, short_w, rate, total, *blocks, weight)


def lr_modal_kernel(places, scalar_ref, sent_ref, short_ref, rate_ref, res_ref, skip_ref, q_in, u_in, *refs):
    blocks = len(places)
    weights, out_ref, zs, change, z_ref, result = refs[:blocks], *refs[blocks : blocks + 5]
    q_ref, u_ref, row_sems, powers = refs[blocks + 5 : blocks + 9]
    held, in_sems, out_sems = refs[blocks + 9 : -2], refs[-2], refs[-1]
    rows = q_ref.shape[0] // SEGMENTS

    def moved(segment):
        where = pl.ds(pl.multiple_of(segment * rows, rows), rows)
        return (
            pltpu.make_async_copy(q_in.at[where], q_ref.at[where], row_sems.at[0, segment]),
            pltpu.make_async_copy(u_in.at[where], u_ref.at[where], row_sems.at[1, segment]),
        )

    for index in range(SEGMENTS):
        for copy in moved(index):
            copy.start()
    copies = Fetch(fetch(weights, held, in_sems).copies, blocks)
    tokens = q_ref.shape[0]
    width = z_ref.shape[1]
    lags = short_ref.shape[0]
    prior = lags - 1
    poles = rate_ref.shape[0]
    position = scalar_ref[0]
    zs3 = zs.reshape(tokens, SUB, LANES)

    def head(index, p, j):
        return sent_ref[index, poles + (p - 1) * prior + j].astype(F32)

    def tail(index, p, j):
        return sent_ref[index, poles + 2 * prior + p * prior + j].astype(F32)

    def missed(index, p, t):
        total = short_ref[t + 1, p] * tail(index - 1, p, prior - 1)
        for lag in range(t + 2, lags):
            total = total + short_ref[lag, p] * tail(index - 1, p, prior + t - lag)
        return total

    def had(index, p, t):
        total = short_ref[0, p] * head(index, p, t)
        for lag in range(1, t + 1):
            total = total + short_ref[lag, p] * head(index, p, t - lag)
        return total

    def change_of_u(index, t):
        key, value = had(index, 1, t), had(index, 2, t)
        more_key, more_value = missed(index, 1, t), missed(index, 2, t)
        return key * more_value + more_key * value + more_key * more_value

    nothing = jnp.zeros((SUB, LANES), F32)
    change[0] = jnp.zeros((prior, SUB, LANES), F32)

    @pl.loop(1, position + 1)
    def _(index):
        for t in range(prior):
            change[index, t] = change_of_u(index, t)

    decay, weight = [], []
    for n in range(poles):
        rate = rate_ref[n]
        decay.append(jnp.exp(-rate))
        weight.append(res_ref[n] * jnp.sqrt(1.0 - jnp.exp(-2.0 * rate)))
        powers[0, n] = jnp.exp(-rate * tokens)
        for t in range(prior):
            powers[1 + t, n] = jnp.exp(-rate * (tokens - 1 - t))

    def arrive(index, totals):
        totals = list(totals)
        changes = [change[index, t] for t in range(prior)]
        for n in range(poles):
            end = sent_ref[index, n].astype(F32)
            for t in range(prior):
                end = end + powers[1 + t, n] * changes[t]
            totals[n] = powers[0, n] * totals[n] + end
        return tuple(totals)

    enter = lax.fori_loop(0, position, arrive, (nothing,) * poles)

    for copy in moved(0):
        copy.wait()
    copies.begin()
    first_u, first_q = [], []
    for t in range(prior):
        first_u.append(u_ref[t] + change[position, t])
        before = lax.max(position, 1)
        first_q.append(q_ref[t] + jnp.where(position > 0, missed(before, 0, t), 0.0))

    def row(states, value, query):
        total = skip_ref[...] * value
        for n in range(poles):
            states[n] = decay[n] * states[n] + value
            total = total + weight[n] * states[n]
        return query * total

    states = list(enter)
    for t in range(STEP):
        value, query = (first_u[t], first_q[t]) if t < prior else (u_ref[t], q_ref[t])
        zs3[t] = row(states, value, query)

    def block(index, states):
        first = index * STEP
        states = list(states)
        for t in range(STEP):
            zs3[first + t] = row(states, u_ref[first + t], q_ref[first + t])
        return tuple(states)

    steps = rows // STEP
    states = lax.fori_loop(1, steps, block, tuple(states))

    def segment(index, states):
        for copy in moved(index):
            copy.wait()
        return lax.fori_loop(index * steps, (index + 1) * steps, block, states)

    lax.fori_loop(1, SEGMENTS, segment, states)
    for tile in range(width // LANES):
        lanes = slice(tile * LANES, (tile + 1) * LANES)
        z_ref[:, lanes] = get_rows(zs, 0, tokens, tile).astype(BF16)
    place_blocks(places, position, z_ref[...], copies, held, result, out_ref, out_sems)


def lr_modal(position, q, u, sent, short_w, rate, res, skip, width, places, weights, shares):
    tokens = q.shape[0]
    prior = short_w.shape[0] - 1
    total = sum(w.shape[1] for w in weights)
    return pl.pallas_call(
        functools.partial(lr_modal_kernel, places),
        out_shape=jax.ShapeDtypeStruct((shares, tokens, total // shares), BF16),
        in_specs=[pl.BlockSpec(memory_space=pltpu.SMEM), *vmem(5), *in_hbm(2 + len(weights))],
        out_specs=in_hbm(1)[0],
        scratch_shapes=[
            pltpu.VMEM((tokens * SUB, LANES), F32),
            pltpu.VMEM((sent.shape[0], prior, SUB, LANES), F32),
            pltpu.VMEM((tokens, width), BF16),
            pltpu.VMEM((tokens, total), BF16),
            pltpu.VMEM((tokens, SUB, LANES), F32),
            pltpu.VMEM((tokens, SUB, LANES), F32),
            pltpu.SemaphoreType.DMA((2, SEGMENTS)),
            pltpu.VMEM((1 + prior, *rate.shape), F32),
            *[pltpu.VMEM(w.shape, w.dtype) for w in weights],
            pltpu.SemaphoreType.DMA((len(weights),)),
            pltpu.SemaphoreType.DMA((len(weights),)),
        ],
        compiler_params=params(VMEM_MIB),
        cost_estimate=cost(2 * tokens * width * total, 2 * total * (width + tokens)),
        name="lr_modal",
    )(position, sent, short_w, rate, res, skip, q, u, *weights)


def local(
    residual_in,
    mr_qkv,
    mr_short_w,
    mr_filter,
    mr_skip,
    mr_out_w,
    lr_gain,
    lr_in_w,
    lr_short_w,
    lr_rate,
    lr_res,
    lr_skip,
    lr_out_w,
):
    sequences, tokens, _, width = mr_qkv.shape
    taps = mr_filter.shape[0]
    prior = mr_short_w.shape[0] - 1
    ctx, tp = lax.axis_size("ctx"), lax.axis_size("tp")
    position = lax.axis_index("ctx").astype(jnp.int32).reshape(1)
    place = lax.axis_index("tp").astype(jnp.int32).reshape(1)
    onward = [(i, i + 1) for i in range(ctx - 1)]

    tail = mr_qkv[:, tokens - taps - prior :].astype(F32)
    mixed = sum(mr_short_w[lag, 1:] * tail[:, prior - lag : prior - lag + taps, 1:] for lag in range(prior + 1))
    tail_u = (mixed[:, :, 0] * mixed[:, :, 1]).astype(BF16)
    last = jnp.swapaxes(mr_qkv[:, tokens - prior :], 1, 2).reshape(sequences, 3 * prior, width)
    last = jnp.pad(last, ((0, 0), (0, HALO - 3 * prior), (0, 0)))
    halo = lax.ppermute(jnp.concatenate([tail_u, last], axis=1), "ctx", onward)

    x = jnp.swapaxes(mr_qkv, 1, 2)
    mr_short, lr_short = tiles(mr_short_w), tiles(lr_short_w)
    mr_taps, mr_direct = tiles(mr_filter), tiles(mr_skip)
    rate, res, lr_direct = tiles(lr_rate), tiles(lr_res), tiles(lr_skip)
    in_w = jnp.swapaxes(lr_in_w, 0, 1)
    gain = lr_gain.reshape(1, -1)

    def scattered(parts):
        return lax.psum_scatter(parts, "tp", scatter_dimension=0)

    def as_mid(s, *terms):
        total = residual_in[s].astype(F32)
        for term in terms:
            total = total + term.astype(F32)
        return lax.optimization_barrier(total.astype(BF16))

    table = line_table(tp)
    assert sequences == 2

    mr_w = SwapGather(mr_out_w, "ctx")
    mr_w.first()
    body, q, conv = mr_local(x, mr_short, mr_taps, mr_direct)
    mr_w.arrays, halo = together(mr_w.arrays, halo)

    early = list(mr_w.arrays)
    mr_w.second()
    early = [k for k in mr_w.arrays if k in early or (k[0] ^ 1, k[1]) in early]
    head = mr_finish(x, halo, q, conv, mr_short, mr_taps, mr_direct, 0, conv)
    z = head, body, 0
    first = project(z, position, mr_w.places(early), [mr_w.arrays[k] for k in early], tp)
    mr_w.arrays, first = together(mr_w.arrays, first)

    mr_w.third()
    late = [k for k in mr_w.arrays if k not in early]
    if late:
        first = project(z, position, mr_w.places(late), [mr_w.arrays[k] for k in late], tp, first)
    share = scattered(first)

    lr_w = SwapGather(after(lr_out_w, first), "ctx")
    lr_w.first()
    head = mr_finish(x, halo, q, conv, mr_short, mr_taps, mr_direct, 1, first)
    second = project((head, body, 1), position, mr_w.places(mr_w.arrays), list(mr_w.arrays.values()), tp)
    lr_w.arrays, second = together(lr_w.arrays, second)
    lr_w.second()
    lr_w.arrays, share = together(lr_w.arrays, share)

    def near(blocks):
        return blocks[:5] if tp == 4 else blocks

    def scatter_all(parts, steps, arrived):
        for step in steps:
            arrived = line_scatter(parts, "tp", step, arrived)
        return arrived

    mids = [as_mid(0, share)]
    if tp == 4:
        line = lax.axis_index("tp")
        inside = (line == 1) | (line == 2)

        def outer(value):
            return lax.ppermute(value, "tp", [(0, 1), (1, 0), (2, 3), (3, 2)])

        def inner(value):
            return lax.ppermute(value, "tp", [(1, 2), (2, 1)])

        def part(share):
            return line_part(second, "tp", jnp.where(line < 2, share, 3 - share))

        near_0, near_1 = outer(mids[0]), inner(mids[0])
        lr_w.third()
        near_0, near_1, second, lr_w.arrays = together(near_0, near_1, second, lr_w.arrays)
        far_1 = outer(jnp.where(inside, near_1, part(3)))
        far_0 = inner(near_0)
        near_0, near_1, far_0, far_1 = together(near_0, near_1, far_0, far_1)
        far_2 = outer(jnp.where(inside, far_0, part(2)))
        sums_0 = inner(add(part(3), far_1))
        begun = lr_in_start(place, gain, [mids[0], near_0, near_1, far_0, far_1], table, in_w)
        begun, sums_0, far_0, far_1, far_2, near_0, near_1 = together(begun, sums_0, far_0, far_1, far_2, near_0, near_1)
        blocks = [mids[0], near_0, near_1, far_0, far_1, far_2]
        arrived = [outer(add(part(jnp.where(inside, 0, 1)), sums_0)), inner(add(part(2), far_2))]
    else:
        blocks = line_gather(mids[0], "tp", 1, None)
        lr_w.third()
        blocks, second, lr_w.arrays = together(blocks, second, lr_w.arrays)
        blocks = line_gather(mids[0], "tp", 2, blocks)
        arrived = line_scatter(second, "tp", 1, None)
        blocks, arrived[:1] = together(blocks, arrived[:1])
        arrived = arrived[:1] * 2 if tp == 4 else arrived
        blocks = line_gather(mids[0], "tp", 3, blocks)
        arrived = line_scatter(second, "tp", 2, arrived)
        begun = lr_in_start(place, gain, near(blocks), table, in_w)
        blocks, arrived, begun = together(blocks, arrived, begun)
        arrived = scatter_all(second, range(3, tp), arrived)
    q, u, send = lr_mix(place, gain, begun, blocks, table, in_w, lr_short, rate)
    arrived, q, u, send = together(arrived, q, u, send)
    mids.append(as_mid(1, line_part(second, "tp", lax.axis_index("tp")), *arrived))
    blocks = line_gather(mids[1], "tp", 1, None)
    sent = lax.all_gather(send, "ctx", axis=0)
    blocks, sent, q, u = together(blocks, sent, q, u)
    blocks = line_gather(mids[1], "tp", 2, blocks)
    lr_places, lr_weights = lr_w.places(lr_w.arrays), list(lr_w.arrays.values())
    modal_w = (lr_short, rate, res, lr_direct, width, lr_places, lr_weights, tp)
    first = lr_modal(position, q, u, sent, *modal_w)
    blocks, first = together(blocks, first)
    begun = lr_in_start(place, gain, near(blocks), table, in_w)
    blocks = line_gather(mids[1], "tp", 3, blocks)
    blocks, begun, first = together(blocks, begun, first)
    share = scattered(first)
    q, u, send = lr_mix(place, gain, begun, blocks, table, in_w, lr_short, rate)
    sent = lax.all_gather(send, "ctx", axis=0)
    second = lr_modal(position, q, u, sent, *modal_w)
    out = (mids[0].astype(F32) + share.astype(F32)).astype(BF16)
    out, second = together(jnp.stack([out, mids[1]]), second)
    last = (out[1].astype(F32) + scattered(second).astype(F32)).astype(BF16)
    return out.at[1].set(last)


def solution(mesh):
    in_specs = (
        P(None, "ctx", "tp"),
        P(None, "ctx", None, "tp"),
        P(None, None, "tp"),
        P(None, "tp"),
        P("tp"),
        P("tp", "ctx"),
        P(),
        P(None, None, "tp"),
        P(None, None, "tp"),
        P(None, "tp"),
        P(None, "tp"),
        P("tp"),
        P("tp", "ctx"),
    )
    out_specs = P(None, "ctx", "tp")
    return jax.shard_map(local, mesh=mesh, in_specs=in_specs, out_specs=out_specs, check_vma=False)
```

```python
import functools

import jax
import jax.numpy as jnp
from jax import lax
from jax.experimental import pallas as pl
from jax.experimental.pallas import tpu as pltpu
from jax.sharding import PartitionSpec as P

F32 = jnp.float32
BF16 = jnp.bfloat16
LANES = 128
SUB = 8
HALO = 16
STEP = 8
VMEM_MIB = 56


def params(mebibytes, **more):
    return pltpu.CompilerParams(vmem_limit_bytes=mebibytes * 2**20, **more)


def vmem(count):
    return [pl.BlockSpec(memory_space=pltpu.VMEM)] * count


def in_hbm(count):
    return [pl.BlockSpec(memory_space=pltpu.HBM)] * count


def cost(flops, moved):
    return pl.CostEstimate(flops=int(flops), bytes_accessed=int(moved), transcendentals=0)


def tiles(value):
    width = value.shape[-1]
    room = SUB * LANES
    if width < room:
        value = jnp.pad(value, [(0, 0)] * (value.ndim - 1) + [(0, room - width)])
    return value.reshape(value.shape[:-1] + (SUB, LANES)).astype(F32)


def put_rows(flat_ref, first, rows, lane_tile, value):
    flat_ref[pl.ds(first * SUB + lane_tile, rows, stride=SUB), :] = value


def get_rows(flat_ref, first, rows, lane_tile):
    return flat_ref[pl.ds(first * SUB + lane_tile, rows, stride=SUB), :]


def window_sum(filter_ref, source3, base, chunks, totals):
    def chunk(index, totals):
        tap = index * STEP
        window = [source3[base - tap - (STEP - 1) + j] for j in range(2 * STEP - 1)]
        totals = list(totals)
        for k in range(STEP):
            weight = filter_ref[tap + k]
            for t in range(STEP):
                totals[t] = totals[t] + weight * window[t - k + STEP - 1]
        return tuple(totals)

    return lax.fori_loop(*chunks, chunk, tuple(totals))


def mr_local_kernel(x_ref, short_ref, filter_ref, skip_ref, gate_ref, z_ref, q_ref, conv_ref, raw, u, zs):
    _, _, tokens, width = x_ref.shape
    head = q_ref.shape[1]
    taps = filter_ref.shape[0]
    lags = short_ref.shape[0]
    prior = lags - 1
    for tile in range(width // LANES):
        lanes = slice(tile * LANES, (tile + 1) * LANES)
        for p in range(3):
            put_rows(raw.at[p], prior, tokens, tile, x_ref[0, p, :, lanes].astype(F32))
    raw3 = raw.reshape(3, tokens + prior, SUB, LANES)
    u3 = u.reshape(taps + tokens, SUB, LANES)
    zs3 = zs.reshape(tokens, SUB, LANES)
    for p in range(3):
        raw3[p, :prior] = jnp.zeros((prior, SUB, LANES), F32)

    @pl.loop(0, taps // STEP)
    def _(block):
        u3[pl.ds(block * STEP, STEP)] = jnp.zeros((STEP, SUB, LANES), F32)

    def mix(p, first, rows):
        total = short_ref[0, p] * raw3[p, pl.ds(first + prior, rows)]
        for lag in range(1, lags):
            total = total + short_ref[lag, p] * raw3[p, pl.ds(first + prior - lag, rows)]
        return total

    @pl.loop(0, tokens // STEP)
    def _(block):
        first = block * STEP
        product = mix(1, first, STEP) * mix(2, first, STEP)
        u3[pl.ds(taps + first, STEP)] = product.astype(BF16).astype(F32)

    def sums(block):
        first = block * STEP
        totals = [skip_ref[...] * u3[taps + first + t] for t in range(STEP)]
        chunks = (0, lax.min(block + 1, taps // STEP))
        return first, mix(0, first, STEP), window_sum(filter_ref, u3, taps + first, chunks, totals)

    @pl.loop(0, head // STEP)
    def _(block):
        first, queries, totals = sums(block)
        q_ref[0, pl.ds(first, STEP)] = queries
        for t in range(STEP):
            conv_ref[0, first + t] = totals[t]

    @pl.loop(head // STEP, tokens // STEP)
    def _(block):
        first, queries, totals = sums(block)
        for t in range(STEP):
            zs3[first + t] = queries[t] * totals[t]

    for tile in range(width // LANES):
        lanes = slice(tile * LANES, (tile + 1) * LANES)
        z_ref[0, head:, lanes] = get_rows(zs, head, tokens - head, tile).astype(BF16)


def mr_local(x, short_w, taps_w, skip, seq, gate):
    _, _, tokens, width = x.shape
    taps = taps_w.shape[0]
    prior = short_w.shape[0] - 1
    head = taps + HALO
    rows = jax.ShapeDtypeStruct((1, head, SUB, LANES), F32)
    return pl.pallas_call(
        mr_local_kernel,
        grid=(1,),
        out_shape=(jax.ShapeDtypeStruct((1, tokens, width), BF16), rows, rows),
        in_specs=[pl.BlockSpec((1, 3, tokens, width), lambda i: (seq, 0, 0, 0)), *vmem(3), *in_hbm(1)],
        out_specs=(
            pl.BlockSpec((1, tokens, width), lambda i: (0, 0, 0)),
            *(pl.BlockSpec((1, head, SUB, LANES), lambda i: (0, 0, 0, 0)),) * 2,
        ),
        scratch_shapes=[
            pltpu.VMEM((3, (tokens + prior) * SUB, LANES), F32),
            pltpu.VMEM(((taps + tokens) * SUB, LANES), F32),
            pltpu.VMEM((tokens * SUB, LANES), F32),
        ],
        compiler_params=params(VMEM_MIB),
        cost_estimate=cost(1e9, 1e6),
        name="mr_local",
    )(x, short_w, taps_w, skip, gate)


def mr_finish_kernel(x_ref, halo_ref, q_ref, conv_ref, short_ref, filter_ref, skip_ref, gate_ref, z_ref, raw, extra, zs):
    tokens = q_ref.shape[1]
    width = z_ref.shape[1]
    taps = filter_ref.shape[0]
    lags = short_ref.shape[0]
    prior = lags - 1
    for tile in range(width // LANES):
        lanes = slice(tile * LANES, (tile + 1) * LANES)
        put_rows(extra, 0, taps, tile, halo_ref[0, :taps, lanes].astype(F32))
        tail = halo_ref[0, taps : taps + HALO, lanes].astype(F32)
        for p in range(3):
            put_rows(raw.at[p], 0, prior, tile, tail[prior * p : prior * (p + 1)])
            put_rows(raw.at[p], prior, prior, tile, x_ref[0, p, :, lanes].astype(F32)[:prior])
    raw3 = raw.reshape(3, 2 * prior, SUB, LANES)
    extra3 = extra.reshape(taps + 2 * STEP, SUB, LANES)
    zs3 = zs.reshape(tokens, SUB, LANES)

    def mix(p, t, lowest):
        total = short_ref[0, p] * raw3[p, prior + t]
        for lag in range(1, lags):
            if prior + t - lag >= lowest:
                total = total + short_ref[lag, p] * raw3[p, prior + t - lag]
        return total

    extra3[taps:] = jnp.zeros((2 * STEP, SUB, LANES), F32)
    for t in range(prior):
        whole = (mix(1, t, 0) * mix(2, t, 0)).astype(BF16).astype(F32)
        alone = (mix(1, t, prior) * mix(2, t, prior)).astype(BF16).astype(F32)
        extra3[taps + t] = whole - alone

    def sums(block):
        first = block * STEP
        chunks = (lax.max(block - 1, 0), taps // STEP)
        totals = [conv_ref[0, first + t] for t in range(STEP)]
        return first, window_sum(filter_ref, extra3, taps + first, chunks, totals)

    first, totals = sums(0)
    for t in range(STEP):
        if t < prior:
            zs3[t] = mix(0, t, 0) * (totals[t] + skip_ref[...] * extra3[taps + t])
        else:
            zs3[t] = q_ref[0, t] * totals[t]

    @pl.loop(1, taps // STEP + 1)
    def _(block):
        first, totals = sums(block)
        for t in range(STEP):
            zs3[first + t] = q_ref[0, first + t] * totals[t]

    @pl.loop(taps // STEP + 1, tokens // STEP)
    def _(block):
        where = pl.ds(block * STEP, STEP)
        zs3[where] = q_ref[0, where] * conv_ref[0, where]

    for tile in range(width // LANES):
        lanes = slice(tile * LANES, (tile + 1) * LANES)
        z_ref[:, lanes] = get_rows(zs, 0, tokens, tile).astype(BF16)


def mr_finish(x, halo, q, conv, short_w, taps_w, skip, seq, gate):
    width = x.shape[3]
    head = q.shape[1]
    taps = taps_w.shape[0]
    prior = short_w.shape[0] - 1
    rows = pl.BlockSpec((1, head, SUB, LANES), lambda i: (0, 0, 0, 0))
    return pl.pallas_call(
        mr_finish_kernel,
        grid=(1,),
        out_shape=jax.ShapeDtypeStruct((head, width), BF16),
        in_specs=[
            pl.BlockSpec((1, 3, HALO, width), lambda i: (seq, 0, 0, 0)),
            pl.BlockSpec((1, halo.shape[1], width), lambda i: (seq, 0, 0)),
            rows,
            rows,
            *vmem(3),
            *in_hbm(1),
        ],
        out_specs=pl.BlockSpec((head, width), lambda i: (0, 0)),
        scratch_shapes=[
            pltpu.VMEM((3, 2 * prior * SUB, LANES), F32),
            pltpu.VMEM(((taps + 2 * STEP) * SUB, LANES), F32),
            pltpu.VMEM((head * SUB, LANES), F32),
        ],
        compiler_params=params(VMEM_MIB),
        cost_estimate=cost(4e10, 1e6),
        name="mr_finish",
    )(x, halo, q, conv, short_w, taps_w, skip, gate)


def place_blocks(places, position, z, copies, held, result, out_ref, out_sems):
    width = out_ref.shape[2]
    sent = []
    begun = 0
    for k, (offset, begin, whole) in enumerate(places):
        columns = held[k].shape[1]
        start = lax.bitwise_xor(position, offset) * whole + begin
        share = lax.div(start, width)
        lanes = pl.ds(pl.multiple_of(lax.rem(start, width), columns), columns)
        mine = slice(begun, begun + columns)
        begun += columns
        copies.get(k)
        result[:, mine] = jnp.dot(z, held[k][...], preferred_element_type=F32).astype(BF16)
        sent.append(pltpu.make_async_copy(result.at[:, mine], out_ref.at[share, :, lanes], out_sems.at[k]))
        sent[-1].start()
    for copy in sent:
        copy.wait()


class Fetch:
    def __init__(self, copies, ahead=3):
        self.copies, self.ahead = copies, ahead

    def begin(self):
        for copies in self.copies[: self.ahead]:
            for copy in copies:
                copy.start()

    def get(self, k):
        for copy in self.copies[k]:
            copy.wait()
        if k + self.ahead < len(self.copies):
            for copy in self.copies[k + self.ahead]:
                copy.start()


def fetch(sources, held, sems):
    return Fetch([(pltpu.make_async_copy(sources[k], held[k], sems.at[k]),) for k in range(len(held))])


def project_kernel(places, scalar_ref, head_ref, body_ref, *refs):
    count = len(places)
    weights = refs[:count]
    out_ref, z_ref, z_sems, result = refs[-6 - count], refs[-5 - count], refs[-4 - count], refs[-3 - count]
    held, in_sems, out_sems = refs[-2 - count : -2], refs[-2], refs[-1]
    head = head_ref.shape[0]
    rest = z_ref.shape[0] - head
    first = pltpu.make_async_copy(head_ref, z_ref.at[pl.ds(0, head)], z_sems.at[0])
    second = pltpu.make_async_copy(body_ref.at[0, pl.ds(head, rest)], z_ref.at[pl.ds(head, rest)], z_sems.at[1])
    first.start()
    second.start()
    copies = fetch(weights, held, in_sems)
    copies.begin()
    first.wait()
    second.wait()
    place_blocks(places, scalar_ref[0], z_ref[...], copies, held, result, out_ref, out_sems)


def project(z, position, places, weights, shares, given=None):
    head, body = z
    _, tokens, width = body.shape
    total = sum(w.shape[1] for w in weights)
    model = places[0][2] * lax.axis_size("ctx")
    extra = [] if given is None else [given]
    return pl.pallas_call(
        functools.partial(project_kernel, places),
        out_shape=jax.ShapeDtypeStruct((shares, tokens, model // shares), BF16),
        in_specs=[pl.BlockSpec(memory_space=pltpu.SMEM), *in_hbm(2 + len(weights) + len(extra))],
        out_specs=in_hbm(1)[0],
        scratch_shapes=[
            pltpu.VMEM((tokens, width), BF16),
            pltpu.SemaphoreType.DMA((2,)),
            pltpu.VMEM((tokens, total), BF16),
            *[pltpu.VMEM(w.shape, w.dtype) for w in weights],
            pltpu.SemaphoreType.DMA((len(weights),)),
            pltpu.SemaphoreType.DMA((len(weights),)),
        ],
        input_output_aliases={3 + len(weights): 0} if extra else {},
        compiler_params=params(VMEM_MIB),
        cost_estimate=cost(2 * tokens * width * total, 2 * total * (width + tokens)),
        name="project",
    )(position, head, body, *weights, *extra)


def after(value, *others):
    return lax.optimization_barrier((value, *others))[0]


def swap_pairs(axis, bit):
    return [(i, i ^ bit) for i in range(lax.axis_size(axis))]


def together(*values):
    return lax.optimization_barrier(values)


class SwapGather:
    def __init__(self, block, axis):
        count = lax.axis_size(axis)
        self.axis, self.whole = axis, block.shape[1]
        self.far = [1 << k for k in range(count.bit_length() - 1, 0, -1) if 1 << k < count]
        self.arrays = {(0, 0): block}
        self.sent = []

    def swap(self, value, bit):
        return lax.ppermute(value, self.axis, swap_pairs(self.axis, bit))

    def near(self, keys):
        for offset, begin in keys:
            self.arrays[offset ^ 1, begin] = self.swap(self.arrays[offset, begin], 1)

    def first(self):
        block = self.arrays[0, 0]
        for bit in self.far:
            self.arrays[bit, 0] = self.swap(block, bit)
        self.near([(0, 0)])

    def second(self):
        pieces = 1 << max(1, len(self.far)).bit_length() - 1
        columns = self.whole // pieces
        for piece in range(pieces if len(self.far) > 1 else 0):
            begin = piece * columns
            part = {bit: self.arrays[bit, 0][:, begin : begin + columns] for bit in self.far}
            self.sent.append(part[self.far[piece]])
            order = self.far[piece:] + self.far[:piece]
            known = [order[0]]
            for bit in order[1:]:
                for offset in list(known):
                    part[offset ^ bit] = self.swap(part[offset], bit)
                    self.arrays[offset ^ bit, begin] = part[offset ^ bit]
                    known.append(offset ^ bit)
                known.append(bit)
        self.near([(bit, 0) for bit in self.far])

    def third(self):
        self.near([key for key in self.arrays if (key[0] ^ 1, key[1]) not in self.arrays])

    def places(self, keys):
        return tuple((offset, begin, self.whole) for offset, begin in keys)


def add(a, b):
    return (a.astype(F32) + b.astype(F32)).astype(BF16)


def line_part(parts, axis, share):
    return lax.dynamic_index_in_dim(parts, jnp.clip(share, 0, lax.axis_size(axis) - 1), 0, False)


def line_scatter(parts, axis, step, arrived):
    count = lax.axis_size(axis)
    place = lax.axis_index(axis)
    up = [(p, p + 1) for p in range(step)]
    down = [(p, p - 1) for p in range(count - step, count)]
    up_share = count - step + place
    down_share = step - count + place
    if step < count - 1 - step:
        value = line_part(parts, axis, jnp.where(place < step, up_share, down_share))
        if arrived:
            value = add(value, arrived[0])
        return [lax.ppermute(value, axis, up + down)] * 2
    if step <= count - step:
        value = line_part(parts, axis, jnp.where(place < step, up_share, down_share))
        if arrived:
            value = add(value, arrived[0] if arrived[0] is arrived[1] else jnp.where(place < step, *arrived))
        return [lax.ppermute(value, axis, up), lax.ppermute(value, axis, down)]
    low, high = line_part(parts, axis, up_share), line_part(parts, axis, down_share)
    if arrived:
        low, high = add(low, arrived[0]), add(high, arrived[1])
    return [lax.ppermute(low, axis, up), lax.ppermute(high, axis, down)]


def line_gather(value, axis, step, arrays):
    count = lax.axis_size(axis)

    def move(what, *pairs):
        return lax.ppermute(what, axis, pairs)

    if count == 4:
        if step == 1:
            return [value, move(value, (0, 1), (1, 0), (2, 3), (3, 2)), move(value, (1, 2), (2, 1))]
        if step == 2:
            return arrays + [move(arrays[1], (1, 2), (2, 1)), move(arrays[2], (1, 0), (2, 3))]
        return arrays + [move(arrays[3], (1, 0), (2, 3))]
    if step > 1:
        return arrays
    low, high = [value], [value]
    for hop in range(1, count):
        low.append(move(low[-1], *[(p, p + 1) for p in range(hop - 1, count - 1)]))
        high.append(move(high[-1], *[(p, p - 1) for p in range(1, count - hop + 1)]))
    return low + high[1:]


def line_table(count):
    if count == 4:
        return ((0, 1, 4, 5), (1, 0, 2, 3), (3, 2, 0, 1), (5, 4, 1, 0))
    return tuple(
        tuple(place - share if share <= place else count - 1 + share - place for share in range(count))
        for place in range(count)
    )


def lr_in_start_kernel(table, gates, scalar_ref, gain_ref, *refs):
    count = len(table)
    *blocks, w_ref, total_ref, square_ref, scaled, held, total, sems, out_sems = refs[gates:]
    tokens, width = blocks[0].shape
    parts, rows, columns = held.shape
    begin = jnp.where(scalar_ref[0] < count // 2, 0, width)
    copies = []
    for k in range(parts):
        p, first = divmod(k * columns, width)
        source = w_ref.at[p, pl.ds(pl.multiple_of(begin, width), rows), pl.ds(first, columns)]
        copies.append((pltpu.make_async_copy(source, held.at[k], sems.at[k]),))
    copies = Fetch(copies, 2)
    copies.begin()
    for place in range(count):
        shares = [share + (place >= count // 2) for share in range(count - 1)]
        sources = [blocks[table[place][share]] for share in shares]

        @pl.when(scalar_ref[0] == place)
        def _(shares=shares, sources=sources):
            @pl.loop(0, tokens // HALO)
            def _(block):
                where = pl.ds(pl.multiple_of(block * HALO, HALO), HALO)
                squares = jnp.zeros((HALO, LANES), F32)
                for k, source in enumerate(sources):
                    wide = source[where, :].astype(F32)
                    for lane in range(0, width, LANES):
                        squares = squares + wide[:, lane : lane + LANES] * wide[:, lane : lane + LANES]
                    gain = gain_ref[:, shares[k] * width : (shares[k] + 1) * width]
                    scaled[where, k * width : (k + 1) * width] = (wide * gain).astype(BF16)
                square_ref[where, :] = squares

    sent = []
    for k in range(parts):
        p, first = divmod(k * columns, width)
        copies.get(k)
        total[k] = jnp.dot(scaled[...], held[k], preferred_element_type=F32)
        sent.append(pltpu.make_async_copy(total.at[k], total_ref.at[k], out_sems.at[k]))
        sent[-1].start()
    for copy in sent:
        copy.wait()


def lr_in_start(place, gain, blocks, table, weight, gates=()):
    count = len(table)
    tokens, width = blocks[0].shape
    rows = (count - 1) * width
    columns = min(512, width)
    parts = 3 * width // columns
    return pl.pallas_call(
        functools.partial(lr_in_start_kernel, table, len(gates)),
        out_shape=(
            jax.ShapeDtypeStruct((parts, tokens, columns), F32),
            jax.ShapeDtypeStruct((tokens, LANES), F32),
        ),
        in_specs=[pl.BlockSpec(memory_space=pltpu.SMEM), *vmem(1), *in_hbm(len(gates)), *vmem(len(blocks)), *in_hbm(1)],
        out_specs=(*in_hbm(1), *vmem(1)),
        scratch_shapes=[
            pltpu.VMEM((tokens, rows), BF16),
            pltpu.VMEM((parts, rows, columns), BF16),
            pltpu.VMEM((parts, tokens, columns), F32),
            pltpu.SemaphoreType.DMA((parts,)),
            pltpu.SemaphoreType.DMA((parts,)),
        ],
        compiler_params=params(VMEM_MIB),
        cost_estimate=cost(6 * tokens * rows * width, 6 * rows * width),
        name="lr_in_start",
    )(place, gain, *gates, *blocks, weight)


SEGMENTS = 4


def lr_mix_kernel(table, scalar_ref, gain_ref, square_ref, short_ref, rate_ref, total_ref, *refs):
    count = len(table)
    blocks, w_ref, q_out, u_out, send_ref = refs[: len(refs) - 15], *refs[len(refs) - 15 : len(refs) - 11]
    source, scaled, scale, held, begun, raw, q_ref, u_ref, sems, begun_sems, out_sems = refs[len(refs) - 11 :]
    tokens, width = blocks[0].shape
    model = count * width
    parts, _, columns = held.shape
    lags = short_ref.shape[0]
    prior = lags - 1
    poles = rate_ref.shape[0]
    begin = jnp.where(scalar_ref[0] < count // 2, model - width, 0)
    for place in range(count):
        share = count - 1 if place < count // 2 else 0

        @pl.when(scalar_ref[0] == place)
        def _(block=blocks[table[place][share]]):
            pltpu.make_async_copy(block, source, out_sems.at[0, 0]).start()

    copies = []
    for k in range(parts):
        p, first = divmod(k * columns, width)
        weight = w_ref.at[p, pl.ds(pl.multiple_of(begin, width), width), pl.ds(first, columns)]
        both = (
            pltpu.make_async_copy(weight, held.at[k], sems.at[k]),
            pltpu.make_async_copy(total_ref.at[k], begun.at[k], begun_sems.at[k]),
        )
        copies.append(both)
    copies = Fetch(copies)
    copies.begin()
    pltpu.make_async_copy(blocks[0], source, out_sems.at[0, 0]).wait()

    @pl.loop(0, tokens // HALO)
    def _(block):
        where = pl.ds(pl.multiple_of(block * HALO, HALO), HALO)
        wide = source[where, :].astype(F32)
        squares = square_ref[where, :]
        for lane in range(0, width, LANES):
            squares = squares + wide[:, lane : lane + LANES] * wide[:, lane : lane + LANES]
        mean = jnp.sum(squares, axis=-1, keepdims=True) * (1.0 / model)
        scale[where, :] = jnp.broadcast_to(lax.rsqrt(mean + 1e-6), (HALO, LANES))
        gain = gain_ref[:, pl.ds(pl.multiple_of(begin, width), width)]
        scaled[where, :] = (wide * gain).astype(BF16)

    for k in range(parts):
        p, first = divmod(k * columns, width)
        copies.get(k)
        total = jnp.dot(scaled[...], held[k], preferred_element_type=F32)
        for lane in range(0, columns, LANES):
            whole = (total[:, lane : lane + LANES] + begun[k, :, lane : lane + LANES]) * scale[...]
            put_rows(raw.at[p], prior, tokens, (first + lane) // LANES, whole.astype(BF16).astype(F32))

    raw3 = raw.reshape(3, tokens + prior, SUB, LANES)
    for p in range(3):
        raw3[p, :prior] = jnp.zeros((prior, SUB, LANES), F32)
    decay = [jnp.exp(-rate_ref[n]) for n in range(poles)]

    def mix(p, first):
        total = short_ref[0, p] * raw3[p, pl.ds(first + prior, STEP)]
        for lag in range(1, lags):
            total = total + short_ref[lag, p] * raw3[p, pl.ds(first + prior - lag, STEP)]
        return total

    def block(index, states):
        first = index * STEP
        q_ref[pl.ds(first, STEP)] = mix(0, first)
        product = mix(1, first) * mix(2, first)
        u_ref[pl.ds(first, STEP)] = product
        states = list(states)
        for t in range(STEP):
            for n in range(poles):
                states[n] = decay[n] * states[n] + product[t]
        return tuple(states)

    rows = tokens // SEGMENTS

    def moved(segment):
        where = pl.ds(pl.multiple_of(segment * rows, rows), rows)
        return (
            pltpu.make_async_copy(q_ref.at[where], q_out.at[where], out_sems.at[0, segment]),
            pltpu.make_async_copy(u_ref.at[where], u_out.at[where], out_sems.at[1, segment]),
        )

    def segment(index, states):
        steps = rows // STEP
        states = lax.fori_loop(index * steps, (index + 1) * steps, block, states)
        for copy in moved(index):
            copy.start()
        return states

    nothing = jnp.zeros((SUB, LANES), F32)
    states = lax.fori_loop(0, SEGMENTS, segment, (nothing,) * poles)
    lines = [*states]
    lines += [raw3[p, prior + j] for p in (1, 2) for j in range(prior)]
    lines += [raw3[p, tokens + j] for p in range(3) for j in range(prior)]
    for n, line in enumerate(lines):
        send_ref[n] = line.astype(BF16)
    for n in range(len(lines), send_ref.shape[0]):
        send_ref[n] = jnp.zeros((SUB, LANES), BF16)
    for index in range(SEGMENTS):
        for copy in moved(index):
            copy.wait()


def lr_mix(place, gain, begun, blocks, table, weight, short_w, rate):
    tokens, width = blocks[0].shape
    columns = min(512, width)
    parts = 3 * width // columns
    poles = rate.shape[0]
    prior = short_w.shape[0] - 1
    lines = -(-(poles + 5 * prior) // HALO) * HALO
    total, squares = begun
    rows = jax.ShapeDtypeStruct((tokens, SUB, LANES), F32)
    return pl.pallas_call(
        functools.partial(lr_mix_kernel, table),
        out_shape=(rows, rows, jax.ShapeDtypeStruct((lines, SUB, LANES), BF16)),
        in_specs=[pl.BlockSpec(memory_space=pltpu.SMEM), *vmem(4), *in_hbm(2 + len(blocks))],
        out_specs=(*in_hbm(2), *vmem(1)),
        scratch_shapes=[
            pltpu.VMEM((tokens, width), BF16),
            pltpu.VMEM((tokens, width), BF16),
            pltpu.VMEM((tokens, LANES), F32),
            pltpu.VMEM((parts, width, columns), BF16),
            pltpu.VMEM((parts, tokens, columns), F32),
            pltpu.VMEM((3, (tokens + prior) * SUB, LANES), F32),
            pltpu.VMEM((tokens, SUB, LANES), F32),
            pltpu.VMEM((tokens, SUB, LANES), F32),
            pltpu.SemaphoreType.DMA((parts,)),
            pltpu.SemaphoreType.DMA((parts,)),
            pltpu.SemaphoreType.DMA((2, SEGMENTS)),
        ],
        compiler_params=params(VMEM_MIB),
        cost_estimate=cost(6 * tokens * width * width, 6 * width * width),
        name="lr_mix",
    )(place, gain, squares, short_w, rate, total, *blocks, weight)


def lr_modal_kernel(places, scalar_ref, sent_ref, short_ref, rate_ref, res_ref, skip_ref, q_in, u_in, *refs):
    blocks = len(places)
    weights, out_ref, zs, change, z_ref, result = refs[:blocks], *refs[blocks : blocks + 5]
    q_ref, u_ref, row_sems, powers = refs[blocks + 5 : blocks + 9]
    held, in_sems, out_sems = refs[blocks + 9 : -2], refs[-2], refs[-1]
    rows = q_ref.shape[0] // SEGMENTS

    def moved(segment):
        where = pl.ds(pl.multiple_of(segment * rows, rows), rows)
        return (
            pltpu.make_async_copy(q_in.at[where], q_ref.at[where], row_sems.at[0, segment]),
            pltpu.make_async_copy(u_in.at[where], u_ref.at[where], row_sems.at[1, segment]),
        )

    for index in range(SEGMENTS):
        for copy in moved(index):
            copy.start()
    copies = Fetch(fetch(weights, held, in_sems).copies, blocks)
    tokens = q_ref.shape[0]
    width = z_ref.shape[1]
    lags = short_ref.shape[0]
    prior = lags - 1
    poles = rate_ref.shape[0]
    position = scalar_ref[0]
    zs3 = zs.reshape(tokens, SUB, LANES)

    def head(index, p, j):
        return sent_ref[index, poles + (p - 1) * prior + j].astype(F32)

    def tail(index, p, j):
        return sent_ref[index, poles + 2 * prior + p * prior + j].astype(F32)

    def missed(index, p, t):
        total = short_ref[t + 1, p] * tail(index - 1, p, prior - 1)
        for lag in range(t + 2, lags):
            total = total + short_ref[lag, p] * tail(index - 1, p, prior + t - lag)
        return total

    def had(index, p, t):
        total = short_ref[0, p] * head(index, p, t)
        for lag in range(1, t + 1):
            total = total + short_ref[lag, p] * head(index, p, t - lag)
        return total

    def change_of_u(index, t):
        key, value = had(index, 1, t), had(index, 2, t)
        more_key, more_value = missed(index, 1, t), missed(index, 2, t)
        return key * more_value + more_key * value + more_key * more_value

    nothing = jnp.zeros((SUB, LANES), F32)
    change[0] = jnp.zeros((prior, SUB, LANES), F32)

    @pl.loop(1, position + 1)
    def _(index):
        for t in range(prior):
            change[index, t] = change_of_u(index, t)

    decay, weight = [], []
    for n in range(poles):
        rate = rate_ref[n]
        decay.append(jnp.exp(-rate))
        weight.append(res_ref[n] * jnp.sqrt(1.0 - jnp.exp(-2.0 * rate)))
        powers[0, n] = jnp.exp(-rate * tokens)
        for t in range(prior):
            powers[1 + t, n] = jnp.exp(-rate * (tokens - 1 - t))

    def arrive(index, totals):
        totals = list(totals)
        changes = [change[index, t] for t in range(prior)]
        for n in range(poles):
            end = sent_ref[index, n].astype(F32)
            for t in range(prior):
                end = end + powers[1 + t, n] * changes[t]
            totals[n] = powers[0, n] * totals[n] + end
        return tuple(totals)

    enter = lax.fori_loop(0, position, arrive, (nothing,) * poles)

    for copy in moved(0):
        copy.wait()
    copies.begin()
    first_u, first_q = [], []
    for t in range(prior):
        first_u.append(u_ref[t] + change[position, t])
        before = lax.max(position, 1)
        first_q.append(q_ref[t] + jnp.where(position > 0, missed(before, 0, t), 0.0))

    def row(states, value, query):
        total = skip_ref[...] * value
        for n in range(poles):
            states[n] = decay[n] * states[n] + value
            total = total + weight[n] * states[n]
        return query * total

    states = list(enter)
    for t in range(STEP):
        value, query = (first_u[t], first_q[t]) if t < prior else (u_ref[t], q_ref[t])
        zs3[t] = row(states, value, query)

    def block(index, states):
        first = index * STEP
        states = list(states)
        for t in range(STEP):
            zs3[first + t] = row(states, u_ref[first + t], q_ref[first + t])
        return tuple(states)

    steps = rows // STEP
    states = lax.fori_loop(1, steps, block, tuple(states))

    def segment(index, states):
        for copy in moved(index):
            copy.wait()
        return lax.fori_loop(index * steps, (index + 1) * steps, block, states)

    lax.fori_loop(1, SEGMENTS, segment, states)
    for tile in range(width // LANES):
        lanes = slice(tile * LANES, (tile + 1) * LANES)
        z_ref[:, lanes] = get_rows(zs, 0, tokens, tile).astype(BF16)
    place_blocks(places, position, z_ref[...], copies, held, result, out_ref, out_sems)


def lr_modal(position, q, u, sent, short_w, rate, res, skip, width, places, weights, shares):
    tokens = q.shape[0]
    prior = short_w.shape[0] - 1
    total = sum(w.shape[1] for w in weights)
    return pl.pallas_call(
        functools.partial(lr_modal_kernel, places),
        out_shape=jax.ShapeDtypeStruct((shares, tokens, total // shares), BF16),
        in_specs=[pl.BlockSpec(memory_space=pltpu.SMEM), *vmem(5), *in_hbm(2 + len(weights))],
        out_specs=in_hbm(1)[0],
        scratch_shapes=[
            pltpu.VMEM((tokens * SUB, LANES), F32),
            pltpu.VMEM((sent.shape[0], prior, SUB, LANES), F32),
            pltpu.VMEM((tokens, width), BF16),
            pltpu.VMEM((tokens, total), BF16),
            pltpu.VMEM((tokens, SUB, LANES), F32),
            pltpu.VMEM((tokens, SUB, LANES), F32),
            pltpu.SemaphoreType.DMA((2, SEGMENTS)),
            pltpu.VMEM((1 + prior, *rate.shape), F32),
            *[pltpu.VMEM(w.shape, w.dtype) for w in weights],
            pltpu.SemaphoreType.DMA((len(weights),)),
            pltpu.SemaphoreType.DMA((len(weights),)),
        ],
        compiler_params=params(VMEM_MIB),
        cost_estimate=cost(2 * tokens * width * total, 2 * total * (width + tokens)),
        name="lr_modal",
    )(position, sent, short_w, rate, res, skip, q, u, *weights)


def mid_kernel(seq, residual_ref, share_ref, *refs):
    out_ref, residual, share, total, sems = refs[-5:]
    copies = [
        pltpu.make_async_copy(residual_ref.at[seq], residual, sems.at[0]),
        pltpu.make_async_copy(share_ref, share, sems.at[1]),
        pltpu.make_async_copy(total, out_ref, sems.at[2]),
    ]
    copies[0].start()
    copies[1].start()
    copies[0].wait()
    copies[1].wait()

    @pl.loop(0, total.shape[0] // HALO)
    def _(block):
        where = pl.ds(pl.multiple_of(block * HALO, HALO), HALO)
        total[where, :] = (residual[where, :].astype(F32) + share[where, :].astype(F32)).astype(BF16)

    copies[2].start()
    copies[2].wait()


def mid_sum(residual, share, seq, gates):
    tokens, width = share.shape
    rows = pltpu.VMEM((tokens, width), BF16)
    return pl.pallas_call(
        functools.partial(mid_kernel, seq),
        out_shape=jax.ShapeDtypeStruct((tokens, width), BF16),
        in_specs=in_hbm(2 + len(gates)),
        out_specs=in_hbm(1)[0],
        scratch_shapes=[rows, rows, rows, pltpu.SemaphoreType.DMA((3,))],
        compiler_params=params(VMEM_MIB),
        cost_estimate=cost(1e6, 1e6),
        name="mid_sum",
    )(residual, share, *gates)


def local(
    residual_in,
    mr_qkv,
    mr_short_w,
    mr_filter,
    mr_skip,
    mr_out_w,
    lr_gain,
    lr_in_w,
    lr_short_w,
    lr_rate,
    lr_res,
    lr_skip,
    lr_out_w,
):
    sequences, tokens, _, width = mr_qkv.shape
    taps = mr_filter.shape[0]
    prior = mr_short_w.shape[0] - 1
    ctx, tp = lax.axis_size("ctx"), lax.axis_size("tp")
    position = lax.axis_index("ctx").astype(jnp.int32).reshape(1)
    place = lax.axis_index("tp").astype(jnp.int32).reshape(1)
    onward = [(i, i + 1) for i in range(ctx - 1)]

    tail = mr_qkv[:, tokens - taps - prior :].astype(F32)
    mixed = sum(mr_short_w[lag, 1:] * tail[:, prior - lag : prior - lag + taps, 1:] for lag in range(prior + 1))
    tail_u = (mixed[:, :, 0] * mixed[:, :, 1]).astype(BF16)
    last = jnp.swapaxes(mr_qkv[:, tokens - prior :], 1, 2).reshape(sequences, 3 * prior, width)
    last = jnp.pad(last, ((0, 0), (0, HALO - 3 * prior), (0, 0)))
    halo = lax.ppermute(jnp.concatenate([tail_u, last], axis=1), "ctx", onward)

    x = jnp.swapaxes(mr_qkv, 1, 2)
    mr_short, lr_short = tiles(mr_short_w), tiles(lr_short_w)
    mr_taps, mr_direct = tiles(mr_filter), tiles(mr_skip)
    rate, res, lr_direct = tiles(lr_rate), tiles(lr_res), tiles(lr_skip)
    in_w = jnp.swapaxes(lr_in_w, 0, 1)
    gain = lr_gain.reshape(1, -1)

    def scattered(parts):
        return lax.psum_scatter(parts, "tp", scatter_dimension=0)

    def as_mid(s, *terms):
        total = residual_in[s].astype(F32)
        for term in terms:
            total = total + term.astype(F32)
        return lax.optimization_barrier(total.astype(BF16))

    table = line_table(tp)
    assert sequences == 2

    mr_w = SwapGather(mr_out_w, "ctx")
    mr_w.first()
    body, q, conv = mr_local(x, mr_short, mr_taps, mr_direct, 0, x)
    mr_w.arrays, halo = together(mr_w.arrays, halo)

    early = list(mr_w.arrays)
    mr_w.second()
    early = [k for k in mr_w.arrays if k in early or (k[0] ^ 1, k[1]) in early]
    head = mr_finish(x, halo, q, conv, mr_short, mr_taps, mr_direct, 0, conv)
    z = head, body
    first = project(z, position, mr_w.places(early), [mr_w.arrays[k] for k in early], tp)
    mr_w.arrays, first = together(mr_w.arrays, first)

    mr_w.third()
    late = [k for k in mr_w.arrays if k not in early]
    if late:
        first = project(z, position, mr_w.places(late), [mr_w.arrays[k] for k in late], tp, first)
    share = scattered(first)

    lr_w = SwapGather(after(lr_out_w, first), "ctx")
    lr_w.first()
    body, q, conv = mr_local(x, mr_short, mr_taps, mr_direct, 1, first)
    head = mr_finish(x, halo, q, conv, mr_short, mr_taps, mr_direct, 1, first)
    second = project((head, body), position, mr_w.places(mr_w.arrays), list(mr_w.arrays.values()), tp)
    lr_w.arrays, second = together(lr_w.arrays, second)
    lr_w.second()

    def near(blocks):
        return blocks[:5] if tp == 4 else blocks

    def scatter_all(parts, steps, arrived):
        for step in steps:
            arrived = line_scatter(parts, "tp", step, arrived)
        return arrived

    mids = [mid_sum(residual_in, share, 0, [second, *lr_w.sent])]
    if tp == 4:
        line = lax.axis_index("tp")
        inside = (line == 1) | (line == 2)

        def outer(value):
            return lax.ppermute(value, "tp", [(0, 1), (1, 0), (2, 3), (3, 2)])

        def inner(value):
            return lax.ppermute(value, "tp", [(1, 2), (2, 1)])

        def part(share):
            return line_part(second, "tp", jnp.where(line < 2, share, 3 - share))

        near_0, near_1 = outer(mids[0]), inner(mids[0])
        near_0, near_1, second = together(near_0, near_1, second)
        far_1 = outer(jnp.where(inside, near_1, part(3)))
        far_0 = inner(near_0)
        lr_w.third()
        arrived_w = list(lr_w.arrays.values())
        near_0, near_1, far_0, far_1 = together(near_0, near_1, far_0, far_1)
        far_2 = outer(jnp.where(inside, far_0, part(2)))
        sums_0 = inner(add(part(3), far_1))
        begun = lr_in_start(place, gain, [mids[0], near_0, near_1, far_0, far_1], table, in_w, arrived_w)
        begun, sums_0, far_0, far_1, far_2, near_0, near_1 = together(begun, sums_0, far_0, far_1, far_2, near_0, near_1)
        blocks = [mids[0], near_0, near_1, far_0, far_1, far_2]
        arrived = [outer(add(part(jnp.where(inside, 0, 1)), sums_0)), inner(add(part(2), far_2))]
    else:
        blocks = line_gather(mids[0], "tp", 1, None)
        lr_w.third()
        blocks, second, lr_w.arrays = together(blocks, second, lr_w.arrays)
        blocks = line_gather(mids[0], "tp", 2, blocks)
        arrived = line_scatter(second, "tp", 1, None)
        blocks, arrived[:1] = together(blocks, arrived[:1])
        arrived = arrived[:1] * 2 if tp == 4 else arrived
        blocks = line_gather(mids[0], "tp", 3, blocks)
        arrived = line_scatter(second, "tp", 2, arrived)
        begun = lr_in_start(place, gain, near(blocks), table, in_w)
        blocks, arrived, begun = together(blocks, arrived, begun)
        arrived = scatter_all(second, range(3, tp), arrived)
    q, u, send = lr_mix(place, gain, begun, blocks, table, in_w, lr_short, rate)
    arrived, q, u, send = together(arrived, q, u, send)
    mids.append(as_mid(1, line_part(second, "tp", lax.axis_index("tp")), *arrived))
    blocks = line_gather(mids[1], "tp", 1, None)
    across = lax.ppermute(mids[1], "tp", [(0, 3), (3, 0)]) if tp == 4 else None
    sent = lax.all_gather(send, "ctx", axis=0)
    blocks, sent, q, u, across = together(blocks, sent, q, u, across)
    blocks = line_gather(mids[1], "tp", 2, blocks)
    lr_places, lr_weights = lr_w.places(lr_w.arrays), list(lr_w.arrays.values())
    modal_w = (lr_short, rate, res, lr_direct, width, lr_places, lr_weights, tp)
    first = lr_modal(position, q, u, sent, *modal_w)
    blocks, first = together(blocks, first)
    if tp == 4:
        blocks, across, first = together(blocks, across, first)
        share = scattered(first)
        begun = lr_in_start(place, gain, blocks, table, in_w)
        blocks = [*blocks, across]
    else:
        share = scattered(first)
        begun = lr_in_start(place, gain, blocks, table, in_w)
    q, u, send = lr_mix(place, gain, begun, blocks, table, in_w, lr_short, rate)
    sent = lax.all_gather(send, "ctx", axis=0)
    second = lr_modal(position, q, u, sent, *modal_w)
    out = (mids[0].astype(F32) + share.astype(F32)).astype(BF16)
    out, second = together(jnp.stack([out, mids[1]]), second)
    last = (out[1].astype(F32) + scattered(second).astype(F32)).astype(BF16)
    return out.at[1].set(last)


def solution(mesh):
    in_specs = (
        P(None, "ctx", "tp"),
        P(None, "ctx", None, "tp"),
        P(None, None, "tp"),
        P(None, "tp"),
        P("tp"),
        P("tp", "ctx"),
        P(),
        P(None, None, "tp"),
        P(None, None, "tp"),
        P(None, "tp"),
        P(None, "tp"),
        P("tp"),
        P("tp", "ctx"),
    )
    out_specs = P(None, "ctx", "tp")
    return jax.shard_map(local, mesh=mesh, in_specs=in_specs, out_specs=out_specs, check_vma=False)
```

```python
import functools

import jax
import jax.numpy as jnp
from jax import lax
from jax.experimental import pallas as pl
from jax.experimental.pallas import tpu as pltpu
from jax.sharding import PartitionSpec as P

F32 = jnp.float32
BF16 = jnp.bfloat16
LANES = 128
SUB = 8
HALO = 16
STEP = 8
VMEM_MIB = 56


def params(mebibytes, **more):
    return pltpu.CompilerParams(vmem_limit_bytes=mebibytes * 2**20, **more)


def vmem(count):
    return [pl.BlockSpec(memory_space=pltpu.VMEM)] * count


def in_hbm(count):
    return [pl.BlockSpec(memory_space=pltpu.HBM)] * count


def cost(flops, moved):
    return pl.CostEstimate(flops=int(flops), bytes_accessed=int(moved), transcendentals=0)


def tiles(value):
    width = value.shape[-1]
    room = SUB * LANES
    if width < room:
        value = jnp.pad(value, [(0, 0)] * (value.ndim - 1) + [(0, room - width)])
    return value.reshape(value.shape[:-1] + (SUB, LANES)).astype(F32)


def put_rows(flat_ref, first, rows, lane_tile, value):
    flat_ref[pl.ds(first * SUB + lane_tile, rows, stride=SUB), :] = value


def get_rows(flat_ref, first, rows, lane_tile):
    return flat_ref[pl.ds(first * SUB + lane_tile, rows, stride=SUB), :]


def window_sum(filter_ref, source3, base, chunks, totals):
    def chunk(index, totals):
        tap = index * STEP
        window = [source3[base - tap - (STEP - 1) + j] for j in range(2 * STEP - 1)]
        totals = list(totals)
        for k in range(STEP):
            weight = filter_ref[tap + k]
            for t in range(STEP):
                totals[t] = totals[t] + weight * window[t - k + STEP - 1]
        return tuple(totals)

    return lax.fori_loop(*chunks, chunk, tuple(totals))


def mr_local_kernel(x_ref, short_ref, filter_ref, skip_ref, gate_ref, z_ref, q_ref, conv_ref, raw, u, zs):
    _, _, tokens, width = x_ref.shape
    head = q_ref.shape[1]
    taps = filter_ref.shape[0]
    lags = short_ref.shape[0]
    prior = lags - 1
    for tile in range(width // LANES):
        lanes = slice(tile * LANES, (tile + 1) * LANES)
        for p in range(3):
            put_rows(raw.at[p], prior, tokens, tile, x_ref[0, p, :, lanes].astype(F32))
    raw3 = raw.reshape(3, tokens + prior, SUB, LANES)
    u3 = u.reshape(taps + tokens, SUB, LANES)
    zs3 = zs.reshape(tokens, SUB, LANES)
    for p in range(3):
        raw3[p, :prior] = jnp.zeros((prior, SUB, LANES), F32)

    @pl.loop(0, taps // STEP)
    def _(block):
        u3[pl.ds(block * STEP, STEP)] = jnp.zeros((STEP, SUB, LANES), F32)

    def mix(p, first, rows):
        total = short_ref[0, p] * raw3[p, pl.ds(first + prior, rows)]
        for lag in range(1, lags):
            total = total + short_ref[lag, p] * raw3[p, pl.ds(first + prior - lag, rows)]
        return total

    @pl.loop(0, tokens // STEP)
    def _(block):
        first = block * STEP
        product = mix(1, first, STEP) * mix(2, first, STEP)
        u3[pl.ds(taps + first, STEP)] = product.astype(BF16).astype(F32)

    def sums(block):
        first = block * STEP
        totals = [skip_ref[...] * u3[taps + first + t] for t in range(STEP)]
        chunks = (0, lax.min(block + 1, taps // STEP))
        return first, mix(0, first, STEP), window_sum(filter_ref, u3, taps + first, chunks, totals)

    @pl.loop(0, head // STEP)
    def _(block):
        first, queries, totals = sums(block)
        q_ref[0, pl.ds(first, STEP)] = queries
        for t in range(STEP):
            conv_ref[0, first + t] = totals[t]

    @pl.loop(head // STEP, tokens // STEP)
    def _(block):
        first, queries, totals = sums(block)
        for t in range(STEP):
            zs3[first + t] = queries[t] * totals[t]

    for tile in range(width // LANES):
        lanes = slice(tile * LANES, (tile + 1) * LANES)
        z_ref[0, head:, lanes] = get_rows(zs, head, tokens - head, tile).astype(BF16)


def mr_local(x, short_w, taps_w, skip, seq, gate):
    _, _, tokens, width = x.shape
    taps = taps_w.shape[0]
    prior = short_w.shape[0] - 1
    head = taps + HALO
    rows = jax.ShapeDtypeStruct((1, head, SUB, LANES), F32)
    return pl.pallas_call(
        mr_local_kernel,
        grid=(1,),
        out_shape=(jax.ShapeDtypeStruct((1, tokens, width), BF16), rows, rows),
        in_specs=[pl.BlockSpec((1, 3, tokens, width), lambda i: (seq, 0, 0, 0)), *vmem(3), *in_hbm(1)],
        out_specs=(
            pl.BlockSpec((1, tokens, width), lambda i: (0, 0, 0)),
            *(pl.BlockSpec((1, head, SUB, LANES), lambda i: (0, 0, 0, 0)),) * 2,
        ),
        scratch_shapes=[
            pltpu.VMEM((3, (tokens + prior) * SUB, LANES), F32),
            pltpu.VMEM(((taps + tokens) * SUB, LANES), F32),
            pltpu.VMEM((tokens * SUB, LANES), F32),
        ],
        compiler_params=params(VMEM_MIB),
        cost_estimate=cost(1e9, 1e6),
        name="mr_local",
    )(x, short_w, taps_w, skip, gate)


def mr_finish_kernel(x_ref, halo_ref, q_ref, conv_ref, short_ref, filter_ref, skip_ref, gate_ref, z_ref, raw, extra, zs):
    tokens = q_ref.shape[1]
    width = z_ref.shape[1]
    taps = filter_ref.shape[0]
    lags = short_ref.shape[0]
    prior = lags - 1
    for tile in range(width // LANES):
        lanes = slice(tile * LANES, (tile + 1) * LANES)
        put_rows(extra, 0, taps, tile, halo_ref[0, :taps, lanes].astype(F32))
        tail = halo_ref[0, taps : taps + HALO, lanes].astype(F32)
        for p in range(3):
            put_rows(raw.at[p], 0, prior, tile, tail[prior * p : prior * (p + 1)])
            put_rows(raw.at[p], prior, prior, tile, x_ref[0, p, :, lanes].astype(F32)[:prior])
    raw3 = raw.reshape(3, 2 * prior, SUB, LANES)
    extra3 = extra.reshape(taps + 2 * STEP, SUB, LANES)
    zs3 = zs.reshape(tokens, SUB, LANES)

    def mix(p, t, lowest):
        total = short_ref[0, p] * raw3[p, prior + t]
        for lag in range(1, lags):
            if prior + t - lag >= lowest:
                total = total + short_ref[lag, p] * raw3[p, prior + t - lag]
        return total

    extra3[taps:] = jnp.zeros((2 * STEP, SUB, LANES), F32)
    for t in range(prior):
        whole = (mix(1, t, 0) * mix(2, t, 0)).astype(BF16).astype(F32)
        alone = (mix(1, t, prior) * mix(2, t, prior)).astype(BF16).astype(F32)
        extra3[taps + t] = whole - alone

    def sums(block):
        first = block * STEP
        chunks = (lax.max(block - 1, 0), taps // STEP)
        totals = [conv_ref[0, first + t] for t in range(STEP)]
        return first, window_sum(filter_ref, extra3, taps + first, chunks, totals)

    first, totals = sums(0)
    for t in range(STEP):
        if t < prior:
            zs3[t] = mix(0, t, 0) * (totals[t] + skip_ref[...] * extra3[taps + t])
        else:
            zs3[t] = q_ref[0, t] * totals[t]

    @pl.loop(1, taps // STEP + 1)
    def _(block):
        first, totals = sums(block)
        for t in range(STEP):
            zs3[first + t] = q_ref[0, first + t] * totals[t]

    @pl.loop(taps // STEP + 1, tokens // STEP)
    def _(block):
        where = pl.ds(block * STEP, STEP)
        zs3[where] = q_ref[0, where] * conv_ref[0, where]

    for tile in range(width // LANES):
        lanes = slice(tile * LANES, (tile + 1) * LANES)
        z_ref[:, lanes] = get_rows(zs, 0, tokens, tile).astype(BF16)


def mr_finish(x, halo, q, conv, short_w, taps_w, skip, seq, gate):
    width = x.shape[3]
    head = q.shape[1]
    taps = taps_w.shape[0]
    prior = short_w.shape[0] - 1
    rows = pl.BlockSpec((1, head, SUB, LANES), lambda i: (0, 0, 0, 0))
    return pl.pallas_call(
        mr_finish_kernel,
        grid=(1,),
        out_shape=jax.ShapeDtypeStruct((head, width), BF16),
        in_specs=[
            pl.BlockSpec((1, 3, HALO, width), lambda i: (seq, 0, 0, 0)),
            pl.BlockSpec((1, halo.shape[1], width), lambda i: (seq, 0, 0)),
            rows,
            rows,
            *vmem(3),
            *in_hbm(1),
        ],
        out_specs=pl.BlockSpec((head, width), lambda i: (0, 0)),
        scratch_shapes=[
            pltpu.VMEM((3, 2 * prior * SUB, LANES), F32),
            pltpu.VMEM(((taps + 2 * STEP) * SUB, LANES), F32),
            pltpu.VMEM((head * SUB, LANES), F32),
        ],
        compiler_params=params(VMEM_MIB),
        cost_estimate=cost(4e10, 1e6),
        name="mr_finish",
    )(x, halo, q, conv, short_w, taps_w, skip, gate)


def place_blocks(places, position, z, copies, held, result, out_ref, out_sems):
    width = out_ref.shape[2]
    sent = []
    begun = 0
    for k, (offset, begin, whole) in enumerate(places):
        columns = held[k].shape[1]
        start = lax.bitwise_xor(position, offset) * whole + begin
        share = lax.div(start, width)
        lanes = pl.ds(pl.multiple_of(lax.rem(start, width), columns), columns)
        mine = slice(begun, begun + columns)
        begun += columns
        copies.get(k)
        result[:, mine] = jnp.dot(z, held[k][...], preferred_element_type=F32).astype(BF16)
        sent.append(pltpu.make_async_copy(result.at[:, mine], out_ref.at[share, :, lanes], out_sems.at[k]))
        sent[-1].start()
    for copy in sent:
        copy.wait()


class Fetch:
    def __init__(self, copies, ahead=3):
        self.copies, self.ahead = copies, ahead

    def begin(self):
        for copies in self.copies[: self.ahead]:
            for copy in copies:
                copy.start()

    def get(self, k):
        for copy in self.copies[k]:
            copy.wait()
        if k + self.ahead < len(self.copies):
            for copy in self.copies[k + self.ahead]:
                copy.start()


def fetch(sources, held, sems):
    return Fetch([(pltpu.make_async_copy(sources[k], held[k], sems.at[k]),) for k in range(len(held))])


def project_kernel(places, scalar_ref, head_ref, body_ref, *refs):
    count = len(places)
    weights = refs[:count]
    out_ref, z_ref, z_sems, result = refs[-6 - count], refs[-5 - count], refs[-4 - count], refs[-3 - count]
    held, in_sems, out_sems = refs[-2 - count : -2], refs[-2], refs[-1]
    head = head_ref.shape[0]
    rest = z_ref.shape[0] - head
    first = pltpu.make_async_copy(head_ref, z_ref.at[pl.ds(0, head)], z_sems.at[0])
    second = pltpu.make_async_copy(body_ref.at[0, pl.ds(head, rest)], z_ref.at[pl.ds(head, rest)], z_sems.at[1])
    first.start()
    second.start()
    copies = fetch(weights, held, in_sems)
    copies.begin()
    first.wait()
    second.wait()
    place_blocks(places, scalar_ref[0], z_ref[...], copies, held, result, out_ref, out_sems)


def project(z, position, places, weights, shares, given=None):
    head, body = z
    _, tokens, width = body.shape
    total = sum(w.shape[1] for w in weights)
    model = places[0][2] * lax.axis_size("ctx")
    extra = [] if given is None else [given]
    return pl.pallas_call(
        functools.partial(project_kernel, places),
        out_shape=jax.ShapeDtypeStruct((shares, tokens, model // shares), BF16),
        in_specs=[pl.BlockSpec(memory_space=pltpu.SMEM), *in_hbm(2 + len(weights) + len(extra))],
        out_specs=in_hbm(1)[0],
        scratch_shapes=[
            pltpu.VMEM((tokens, width), BF16),
            pltpu.SemaphoreType.DMA((2,)),
            pltpu.VMEM((tokens, total), BF16),
            *[pltpu.VMEM(w.shape, w.dtype) for w in weights],
            pltpu.SemaphoreType.DMA((len(weights),)),
            pltpu.SemaphoreType.DMA((len(weights),)),
        ],
        input_output_aliases={3 + len(weights): 0} if extra else {},
        compiler_params=params(VMEM_MIB),
        cost_estimate=cost(2 * tokens * width * total, 2 * total * (width + tokens)),
        name="project",
    )(position, head, body, *weights, *extra)


def after(value, *others):
    return lax.optimization_barrier((value, *others))[0]


def swap_pairs(axis, bit):
    return [(i, i ^ bit) for i in range(lax.axis_size(axis))]


def together(*values):
    return lax.optimization_barrier(values)


class SwapGather:
    def __init__(self, block, axis):
        count = lax.axis_size(axis)
        self.axis, self.whole = axis, block.shape[1]
        self.far = [1 << k for k in range(count.bit_length() - 1, 0, -1) if 1 << k < count]
        self.arrays = {(0, 0): block}
        self.sent = []

    def swap(self, value, bit):
        return lax.ppermute(value, self.axis, swap_pairs(self.axis, bit))

    def near(self, keys):
        for offset, begin in keys:
            self.arrays[offset ^ 1, begin] = self.swap(self.arrays[offset, begin], 1)

    def first(self):
        block = self.arrays[0, 0]
        for bit in self.far:
            self.arrays[bit, 0] = self.swap(block, bit)
        self.near([(0, 0)])

    def second(self):
        pieces = 1 << max(1, len(self.far)).bit_length() - 1
        columns = self.whole // pieces
        for piece in range(pieces if len(self.far) > 1 else 0):
            begin = piece * columns
            part = {bit: self.arrays[bit, 0][:, begin : begin + columns] for bit in self.far}
            self.sent.append(part[self.far[piece]])
            order = self.far[piece:] + self.far[:piece]
            known = [order[0]]
            for bit in order[1:]:
                for offset in list(known):
                    part[offset ^ bit] = self.swap(part[offset], bit)
                    self.arrays[offset ^ bit, begin] = part[offset ^ bit]
                    known.append(offset ^ bit)
                known.append(bit)
        self.near([(bit, 0) for bit in self.far])

    def third(self):
        self.near([key for key in self.arrays if (key[0] ^ 1, key[1]) not in self.arrays])

    def places(self, keys):
        return tuple((offset, begin, self.whole) for offset, begin in keys)


def add(a, b):
    return (a.astype(F32) + b.astype(F32)).astype(BF16)


def line_part(parts, axis, share):
    return lax.dynamic_index_in_dim(parts, jnp.clip(share, 0, lax.axis_size(axis) - 1), 0, False)


def line_scatter(parts, axis, step, arrived):
    count = lax.axis_size(axis)
    place = lax.axis_index(axis)
    up = [(p, p + 1) for p in range(step)]
    down = [(p, p - 1) for p in range(count - step, count)]
    up_share = count - step + place
    down_share = step - count + place
    if step < count - 1 - step:
        value = line_part(parts, axis, jnp.where(place < step, up_share, down_share))
        if arrived:
            value = add(value, arrived[0])
        return [lax.ppermute(value, axis, up + down)] * 2
    if step <= count - step:
        value = line_part(parts, axis, jnp.where(place < step, up_share, down_share))
        if arrived:
            value = add(value, arrived[0] if arrived[0] is arrived[1] else jnp.where(place < step, *arrived))
        return [lax.ppermute(value, axis, up), lax.ppermute(value, axis, down)]
    low, high = line_part(parts, axis, up_share), line_part(parts, axis, down_share)
    if arrived:
        low, high = add(low, arrived[0]), add(high, arrived[1])
    return [lax.ppermute(low, axis, up), lax.ppermute(high, axis, down)]


def line_gather(value, axis, step, arrays):
    count = lax.axis_size(axis)

    def move(what, *pairs):
        return lax.ppermute(what, axis, pairs)

    if count == 4:
        if step == 1:
            return [value, move(value, (0, 1), (1, 0), (2, 3), (3, 2)), move(value, (1, 2), (2, 1))]
        if step == 2:
            return arrays + [move(arrays[1], (1, 2), (2, 1)), move(arrays[2], (1, 0), (2, 3))]
        return arrays + [move(arrays[3], (1, 0), (2, 3))]
    if step > 1:
        return arrays
    low, high = [value], [value]
    for hop in range(1, count):
        low.append(move(low[-1], *[(p, p + 1) for p in range(hop - 1, count - 1)]))
        high.append(move(high[-1], *[(p, p - 1) for p in range(1, count - hop + 1)]))
    return low + high[1:]


def line_table(count):
    if count == 4:
        return ((0, 1, 4, 5), (1, 0, 2, 3), (3, 2, 0, 1), (5, 4, 1, 0))
    return tuple(
        tuple(place - share if share <= place else count - 1 + share - place for share in range(count))
        for place in range(count)
    )


def lr_in_start_kernel(table, gates, scalar_ref, gain_ref, *refs):
    count = len(table)
    *blocks, w_ref, total_ref, square_ref, scaled, held, total, sems, out_sems = refs[gates:]
    tokens, width = blocks[0].shape
    parts, rows, columns = held.shape
    begin = jnp.where(scalar_ref[0] < count // 2, 0, width)
    copies = []
    for k in range(parts):
        p, first = divmod(k * columns, width)
        source = w_ref.at[p, pl.ds(pl.multiple_of(begin, width), rows), pl.ds(first, columns)]
        copies.append((pltpu.make_async_copy(source, held.at[k], sems.at[k]),))
    copies = Fetch(copies, 3)
    copies.begin()
    for place in range(count):
        shares = [share + (place >= count // 2) for share in range(count - 1)]
        sources = [blocks[table[place][share]] for share in shares]

        @pl.when(scalar_ref[0] == place)
        def _(shares=shares, sources=sources):
            @pl.loop(0, tokens // HALO)
            def _(block):
                where = pl.ds(pl.multiple_of(block * HALO, HALO), HALO)
                squares = jnp.zeros((HALO, LANES), F32)
                for k, source in enumerate(sources):
                    wide = source[where, :].astype(F32)
                    for lane in range(0, width, LANES):
                        squares = squares + wide[:, lane : lane + LANES] * wide[:, lane : lane + LANES]
                    gain = gain_ref[:, shares[k] * width : (shares[k] + 1) * width]
                    scaled[where, k * width : (k + 1) * width] = (wide * gain).astype(BF16)
                square_ref[where, :] = squares

    sent = []
    for k in range(parts):
        p, first = divmod(k * columns, width)
        copies.get(k)
        total[k] = jnp.dot(scaled[...], held[k], preferred_element_type=F32)
        sent.append(pltpu.make_async_copy(total.at[k], total_ref.at[k], out_sems.at[k]))
        sent[-1].start()
    for copy in sent:
        copy.wait()


def lr_in_start(place, gain, blocks, table, weight, gates=()):
    count = len(table)
    tokens, width = blocks[0].shape
    rows = (count - 1) * width
    columns = min(512, width)
    parts = 3 * width // columns
    return pl.pallas_call(
        functools.partial(lr_in_start_kernel, table, len(gates)),
        out_shape=(
            jax.ShapeDtypeStruct((parts, tokens, columns), F32),
            jax.ShapeDtypeStruct((tokens, LANES), F32),
        ),
        in_specs=[pl.BlockSpec(memory_space=pltpu.SMEM), *vmem(1), *in_hbm(len(gates)), *vmem(len(blocks)), *in_hbm(1)],
        out_specs=(*in_hbm(1), *vmem(1)),
        scratch_shapes=[
            pltpu.VMEM((tokens, rows), BF16),
            pltpu.VMEM((parts, rows, columns), BF16),
            pltpu.VMEM((parts, tokens, columns), F32),
            pltpu.SemaphoreType.DMA((parts,)),
            pltpu.SemaphoreType.DMA((parts,)),
        ],
        compiler_params=params(VMEM_MIB),
        cost_estimate=cost(6 * tokens * rows * width, 6 * rows * width),
        name="lr_in_start",
    )(place, gain, *gates, *blocks, weight)


SEGMENTS = 4


def lr_mix_kernel(table, scalar_ref, gain_ref, square_ref, short_ref, rate_ref, total_ref, *refs):
    count = len(table)
    blocks, w_ref, q_out, u_out, send_ref = refs[: len(refs) - 15], *refs[len(refs) - 15 : len(refs) - 11]
    source, scaled, scale, held, begun, raw, q_ref, u_ref, sems, begun_sems, out_sems = refs[len(refs) - 11 :]
    tokens, width = blocks[0].shape
    model = count * width
    parts, _, columns = held.shape
    lags = short_ref.shape[0]
    prior = lags - 1
    poles = rate_ref.shape[0]
    begin = jnp.where(scalar_ref[0] < count // 2, model - width, 0)
    for place in range(count):
        share = count - 1 if place < count // 2 else 0

        @pl.when(scalar_ref[0] == place)
        def _(block=blocks[table[place][share]]):
            pltpu.make_async_copy(block, source, out_sems.at[0, 0]).start()

    copies = []
    for k in range(parts):
        p, first = divmod(k * columns, width)
        weight = w_ref.at[p, pl.ds(pl.multiple_of(begin, width), width), pl.ds(first, columns)]
        both = (
            pltpu.make_async_copy(weight, held.at[k], sems.at[k]),
            pltpu.make_async_copy(total_ref.at[k], begun.at[k], begun_sems.at[k]),
        )
        copies.append(both)
    copies = Fetch(copies)
    copies.begin()
    pltpu.make_async_copy(blocks[0], source, out_sems.at[0, 0]).wait()

    @pl.loop(0, tokens // HALO)
    def _(block):
        where = pl.ds(pl.multiple_of(block * HALO, HALO), HALO)
        wide = source[where, :].astype(F32)
        squares = square_ref[where, :]
        for lane in range(0, width, LANES):
            squares = squares + wide[:, lane : lane + LANES] * wide[:, lane : lane + LANES]
        mean = jnp.sum(squares, axis=-1, keepdims=True) * (1.0 / model)
        scale[where, :] = jnp.broadcast_to(lax.rsqrt(mean + 1e-6), (HALO, LANES))
        gain = gain_ref[:, pl.ds(pl.multiple_of(begin, width), width)]
        scaled[where, :] = (wide * gain).astype(BF16)

    for k in range(parts):
        p, first = divmod(k * columns, width)
        copies.get(k)
        total = jnp.dot(scaled[...], held[k], preferred_element_type=F32)
        for lane in range(0, columns, LANES):
            whole = (total[:, lane : lane + LANES] + begun[k, :, lane : lane + LANES]) * scale[...]
            put_rows(raw.at[p], prior, tokens, (first + lane) // LANES, whole.astype(BF16).astype(F32))

    raw3 = raw.reshape(3, tokens + prior, SUB, LANES)
    for p in range(3):
        raw3[p, :prior] = jnp.zeros((prior, SUB, LANES), F32)
    decay = [jnp.exp(-rate_ref[n]) for n in range(poles)]

    def mix(p, first):
        total = short_ref[0, p] * raw3[p, pl.ds(first + prior, STEP)]
        for lag in range(1, lags):
            total = total + short_ref[lag, p] * raw3[p, pl.ds(first + prior - lag, STEP)]
        return total

    def block(index, states):
        first = index * STEP
        q_ref[pl.ds(first, STEP)] = mix(0, first)
        product = mix(1, first) * mix(2, first)
        u_ref[pl.ds(first, STEP)] = product
        states = list(states)
        for t in range(STEP):
            for n in range(poles):
                states[n] = decay[n] * states[n] + product[t]
        return tuple(states)

    rows = tokens // SEGMENTS

    def moved(segment):
        where = pl.ds(pl.multiple_of(segment * rows, rows), rows)
        return (
            pltpu.make_async_copy(q_ref.at[where], q_out.at[where], out_sems.at[0, segment]),
            pltpu.make_async_copy(u_ref.at[where], u_out.at[where], out_sems.at[1, segment]),
        )

    def segment(index, states):
        steps = rows // STEP
        states = lax.fori_loop(index * steps, (index + 1) * steps, block, states)
        for copy in moved(index):
            copy.start()
        return states

    nothing = jnp.zeros((SUB, LANES), F32)
    states = lax.fori_loop(0, SEGMENTS, segment, (nothing,) * poles)
    lines = [*states]
    lines += [raw3[p, prior + j] for p in (1, 2) for j in range(prior)]
    lines += [raw3[p, tokens + j] for p in range(3) for j in range(prior)]
    for n, line in enumerate(lines):
        send_ref[n] = line.astype(BF16)
    for n in range(len(lines), send_ref.shape[0]):
        send_ref[n] = jnp.zeros((SUB, LANES), BF16)
    for index in range(SEGMENTS):
        for copy in moved(index):
            copy.wait()


def lr_mix(place, gain, begun, blocks, table, weight, short_w, rate):
    tokens, width = blocks[0].shape
    columns = min(512, width)
    parts = 3 * width // columns
    poles = rate.shape[0]
    prior = short_w.shape[0] - 1
    lines = -(-(poles + 5 * prior) // HALO) * HALO
    total, squares = begun
    rows = jax.ShapeDtypeStruct((tokens, SUB, LANES), F32)
    return pl.pallas_call(
        functools.partial(lr_mix_kernel, table),
        out_shape=(rows, rows, jax.ShapeDtypeStruct((lines, SUB, LANES), BF16)),
        in_specs=[pl.BlockSpec(memory_space=pltpu.SMEM), *vmem(4), *in_hbm(2 + len(blocks))],
        out_specs=(*in_hbm(2), *vmem(1)),
        scratch_shapes=[
            pltpu.VMEM((tokens, width), BF16),
            pltpu.VMEM((tokens, width), BF16),
            pltpu.VMEM((tokens, LANES), F32),
            pltpu.VMEM((parts, width, columns), BF16),
            pltpu.VMEM((parts, tokens, columns), F32),
            pltpu.VMEM((3, (tokens + prior) * SUB, LANES), F32),
            pltpu.VMEM((tokens, SUB, LANES), F32),
            pltpu.VMEM((tokens, SUB, LANES), F32),
            pltpu.SemaphoreType.DMA((parts,)),
            pltpu.SemaphoreType.DMA((parts,)),
            pltpu.SemaphoreType.DMA((2, SEGMENTS)),
        ],
        compiler_params=params(VMEM_MIB),
        cost_estimate=cost(6 * tokens * width * width, 6 * width * width),
        name="lr_mix",
    )(place, gain, squares, short_w, rate, total, *blocks, weight)


def lr_modal_kernel(places, scalar_ref, sent_ref, short_ref, rate_ref, res_ref, skip_ref, q_in, u_in, *refs):
    blocks = len(places)
    weights, out_ref, zs, change, z_ref, result = refs[:blocks], *refs[blocks : blocks + 5]
    q_ref, u_ref, row_sems, powers = refs[blocks + 5 : blocks + 9]
    held, in_sems, out_sems = refs[blocks + 9 : -2], refs[-2], refs[-1]
    rows = q_ref.shape[0] // SEGMENTS

    def moved(segment):
        where = pl.ds(pl.multiple_of(segment * rows, rows), rows)
        return (
            pltpu.make_async_copy(q_in.at[where], q_ref.at[where], row_sems.at[0, segment]),
            pltpu.make_async_copy(u_in.at[where], u_ref.at[where], row_sems.at[1, segment]),
        )

    for index in range(SEGMENTS):
        for copy in moved(index):
            copy.start()
    copies = Fetch(fetch(weights, held, in_sems).copies, blocks)
    tokens = q_ref.shape[0]
    width = z_ref.shape[1]
    lags = short_ref.shape[0]
    prior = lags - 1
    poles = rate_ref.shape[0]
    position = scalar_ref[0]
    zs3 = zs.reshape(tokens, SUB, LANES)

    def head(index, p, j):
        return sent_ref[index, poles + (p - 1) * prior + j].astype(F32)

    def tail(index, p, j):
        return sent_ref[index, poles + 2 * prior + p * prior + j].astype(F32)

    def missed(index, p, t):
        total = short_ref[t + 1, p] * tail(index - 1, p, prior - 1)
        for lag in range(t + 2, lags):
            total = total + short_ref[lag, p] * tail(index - 1, p, prior + t - lag)
        return total

    def had(index, p, t):
        total = short_ref[0, p] * head(index, p, t)
        for lag in range(1, t + 1):
            total = total + short_ref[lag, p] * head(index, p, t - lag)
        return total

    def change_of_u(index, t):
        key, value = had(index, 1, t), had(index, 2, t)
        more_key, more_value = missed(index, 1, t), missed(index, 2, t)
        return key * more_value + more_key * value + more_key * more_value

    nothing = jnp.zeros((SUB, LANES), F32)
    change[0] = jnp.zeros((prior, SUB, LANES), F32)

    @pl.loop(1, position + 1)
    def _(index):
        for t in range(prior):
            change[index, t] = change_of_u(index, t)

    decay, weight = [], []
    for n in range(poles):
        rate = rate_ref[n]
        decay.append(jnp.exp(-rate))
        weight.append(res_ref[n] * jnp.sqrt(1.0 - jnp.exp(-2.0 * rate)))
        powers[0, n] = jnp.exp(-rate * tokens)
        for t in range(prior):
            powers[1 + t, n] = jnp.exp(-rate * (tokens - 1 - t))

    def arrive(index, totals):
        totals = list(totals)
        changes = [change[index, t] for t in range(prior)]
        for n in range(poles):
            end = sent_ref[index, n].astype(F32)
            for t in range(prior):
                end = end + powers[1 + t, n] * changes[t]
            totals[n] = powers[0, n] * totals[n] + end
        return tuple(totals)

    enter = lax.fori_loop(0, position, arrive, (nothing,) * poles)

    for copy in moved(0):
        copy.wait()
    copies.begin()
    first_u, first_q = [], []
    for t in range(prior):
        first_u.append(u_ref[t] + change[position, t])
        before = lax.max(position, 1)
        first_q.append(q_ref[t] + jnp.where(position > 0, missed(before, 0, t), 0.0))

    def row(states, value, query):
        total = skip_ref[...] * value
        for n in range(poles):
            states[n] = decay[n] * states[n] + value
            total = total + weight[n] * states[n]
        return query * total

    states = list(enter)
    for t in range(STEP):
        value, query = (first_u[t], first_q[t]) if t < prior else (u_ref[t], q_ref[t])
        zs3[t] = row(states, value, query)

    def block(index, states):
        first = index * STEP
        states = list(states)
        for t in range(STEP):
            zs3[first + t] = row(states, u_ref[first + t], q_ref[first + t])
        return tuple(states)

    steps = rows // STEP
    states = lax.fori_loop(1, steps, block, tuple(states))

    def segment(index, states):
        for copy in moved(index):
            copy.wait()
        return lax.fori_loop(index * steps, (index + 1) * steps, block, states)

    lax.fori_loop(1, SEGMENTS, segment, states)
    for tile in range(width // LANES):
        lanes = slice(tile * LANES, (tile + 1) * LANES)
        z_ref[:, lanes] = get_rows(zs, 0, tokens, tile).astype(BF16)
    place_blocks(places, position, z_ref[...], copies, held, result, out_ref, out_sems)


def lr_modal(position, q, u, sent, short_w, rate, res, skip, width, places, weights, shares):
    tokens = q.shape[0]
    prior = short_w.shape[0] - 1
    total = sum(w.shape[1] for w in weights)
    return pl.pallas_call(
        functools.partial(lr_modal_kernel, places),
        out_shape=jax.ShapeDtypeStruct((shares, tokens, total // shares), BF16),
        in_specs=[pl.BlockSpec(memory_space=pltpu.SMEM), *vmem(5), *in_hbm(2 + len(weights))],
        out_specs=in_hbm(1)[0],
        scratch_shapes=[
            pltpu.VMEM((tokens * SUB, LANES), F32),
            pltpu.VMEM((sent.shape[0], prior, SUB, LANES), F32),
            pltpu.VMEM((tokens, width), BF16),
            pltpu.VMEM((tokens, total), BF16),
            pltpu.VMEM((tokens, SUB, LANES), F32),
            pltpu.VMEM((tokens, SUB, LANES), F32),
            pltpu.SemaphoreType.DMA((2, SEGMENTS)),
            pltpu.VMEM((1 + prior, *rate.shape), F32),
            *[pltpu.VMEM(w.shape, w.dtype) for w in weights],
            pltpu.SemaphoreType.DMA((len(weights),)),
            pltpu.SemaphoreType.DMA((len(weights),)),
        ],
        compiler_params=params(VMEM_MIB),
        cost_estimate=cost(2 * tokens * width * total, 2 * total * (width + tokens)),
        name="lr_modal",
    )(position, sent, short_w, rate, res, skip, q, u, *weights)


def mid_kernel(seq, residual_ref, share_ref, *refs):
    out_ref, residual, share, total, sems = refs[-5:]
    copies = [
        pltpu.make_async_copy(residual_ref.at[seq], residual, sems.at[0]),
        pltpu.make_async_copy(share_ref, share, sems.at[1]),
        pltpu.make_async_copy(total, out_ref, sems.at[2]),
    ]
    copies[0].start()
    copies[1].start()
    copies[0].wait()
    copies[1].wait()

    @pl.loop(0, total.shape[0] // HALO)
    def _(block):
        where = pl.ds(pl.multiple_of(block * HALO, HALO), HALO)
        total[where, :] = (residual[where, :].astype(F32) + share[where, :].astype(F32)).astype(BF16)

    copies[2].start()
    copies[2].wait()


def mid_sum(residual, share, seq, gates):
    tokens, width = share.shape
    rows = pltpu.VMEM((tokens, width), BF16)
    return pl.pallas_call(
        functools.partial(mid_kernel, seq),
        out_shape=jax.ShapeDtypeStruct((tokens, width), BF16),
        in_specs=in_hbm(2 + len(gates)),
        out_specs=in_hbm(1)[0],
        scratch_shapes=[rows, rows, rows, pltpu.SemaphoreType.DMA((3,))],
        compiler_params=params(VMEM_MIB),
        cost_estimate=cost(1e6, 1e6),
        name="mid_sum",
    )(residual, share, *gates)


def local(
    residual_in,
    mr_qkv,
    mr_short_w,
    mr_filter,
    mr_skip,
    mr_out_w,
    lr_gain,
    lr_in_w,
    lr_short_w,
    lr_rate,
    lr_res,
    lr_skip,
    lr_out_w,
):
    sequences, tokens, _, width = mr_qkv.shape
    taps = mr_filter.shape[0]
    prior = mr_short_w.shape[0] - 1
    ctx, tp = lax.axis_size("ctx"), lax.axis_size("tp")
    position = lax.axis_index("ctx").astype(jnp.int32).reshape(1)
    place = lax.axis_index("tp").astype(jnp.int32).reshape(1)
    onward = [(i, i + 1) for i in range(ctx - 1)]

    tail = mr_qkv[:, tokens - taps - prior :].astype(F32)
    mixed = sum(mr_short_w[lag, 1:] * tail[:, prior - lag : prior - lag + taps, 1:] for lag in range(prior + 1))
    tail_u = (mixed[:, :, 0] * mixed[:, :, 1]).astype(BF16)
    last = jnp.swapaxes(mr_qkv[:, tokens - prior :], 1, 2).reshape(sequences, 3 * prior, width)
    last = jnp.pad(last, ((0, 0), (0, HALO - 3 * prior), (0, 0)))
    halo = lax.ppermute(jnp.concatenate([tail_u, last], axis=1), "ctx", onward)

    x = jnp.swapaxes(mr_qkv, 1, 2)
    mr_short, lr_short = tiles(mr_short_w), tiles(lr_short_w)
    mr_taps, mr_direct = tiles(mr_filter), tiles(mr_skip)
    rate, res, lr_direct = tiles(lr_rate), tiles(lr_res), tiles(lr_skip)
    in_w = jnp.swapaxes(lr_in_w, 0, 1)
    gain = lr_gain.reshape(1, -1)

    def scattered(parts):
        return lax.psum_scatter(parts, "tp", scatter_dimension=0)

    def as_mid(s, *terms):
        total = residual_in[s].astype(F32)
        for term in terms:
            total = total + term.astype(F32)
        return lax.optimization_barrier(total.astype(BF16))

    table = line_table(tp)
    assert sequences == 2

    mr_w = SwapGather(mr_out_w, "ctx")
    mr_w.first()
    body, q, conv = mr_local(x, mr_short, mr_taps, mr_direct, 0, x)
    mr_w.arrays, halo = together(mr_w.arrays, halo)

    early = list(mr_w.arrays)
    mr_w.second()
    early = [k for k in mr_w.arrays if k in early or (k[0] ^ 1, k[1]) in early]
    head = mr_finish(x, halo, q, conv, mr_short, mr_taps, mr_direct, 0, conv)
    z = head, body
    first = project(z, position, mr_w.places(early), [mr_w.arrays[k] for k in early], tp)
    mr_w.arrays, first = together(mr_w.arrays, first)

    mr_w.third()
    late = [k for k in mr_w.arrays if k not in early]
    if late:
        first = project(z, position, mr_w.places(late), [mr_w.arrays[k] for k in late], tp, first)
    share = scattered(first)

    lr_w = SwapGather(after(lr_out_w, first), "ctx")
    lr_w.first()
    body, q, conv = mr_local(x, mr_short, mr_taps, mr_direct, 1, first)
    head = mr_finish(x, halo, q, conv, mr_short, mr_taps, mr_direct, 1, first)
    second = project((head, body), position, mr_w.places(mr_w.arrays), list(mr_w.arrays.values()), tp)
    lr_w.arrays, second = together(lr_w.arrays, second)
    lr_w.second()

    def near(blocks):
        return blocks[:5] if tp == 4 else blocks

    def scatter_all(parts, steps, arrived):
        for step in steps:
            arrived = line_scatter(parts, "tp", step, arrived)
        return arrived

    mids = [mid_sum(residual_in, share, 0, [second, *lr_w.sent])]
    if tp == 4:
        line = lax.axis_index("tp")
        inside = (line == 1) | (line == 2)

        def outer(value):
            return lax.ppermute(value, "tp", [(0, 1), (1, 0), (2, 3), (3, 2)])

        def inner(value):
            return lax.ppermute(value, "tp", [(1, 2), (2, 1)])

        def part(share):
            return line_part(second, "tp", jnp.where(line < 2, share, 3 - share))

        near_0, near_1 = outer(mids[0]), inner(mids[0])
        near_0, near_1, second = together(near_0, near_1, second)
        far_1 = outer(jnp.where(inside, near_1, part(3)))
        far_0 = inner(near_0)
        lr_w.third()
        arrived_w = list(lr_w.arrays.values())
        near_0, near_1, far_0, far_1 = together(near_0, near_1, far_0, far_1)
        far_2 = outer(jnp.where(inside, far_0, part(2)))
        sums_0 = inner(add(part(3), far_1))
        begun = lr_in_start(place, gain, [mids[0], near_0, near_1, far_0, far_1], table, in_w, arrived_w)
        begun, sums_0, far_0, far_1, far_2, near_0, near_1 = together(begun, sums_0, far_0, far_1, far_2, near_0, near_1)
        blocks = [mids[0], near_0, near_1, far_0, far_1, far_2]
        arrived = [outer(add(part(jnp.where(inside, 0, 1)), sums_0)), inner(add(part(2), far_2))]
    else:
        blocks = line_gather(mids[0], "tp", 1, None)
        lr_w.third()
        blocks, second, lr_w.arrays = together(blocks, second, lr_w.arrays)
        blocks = line_gather(mids[0], "tp", 2, blocks)
        arrived = line_scatter(second, "tp", 1, None)
        blocks, arrived[:1] = together(blocks, arrived[:1])
        arrived = arrived[:1] * 2 if tp == 4 else arrived
        blocks = line_gather(mids[0], "tp", 3, blocks)
        arrived = line_scatter(second, "tp", 2, arrived)
        begun = lr_in_start(place, gain, near(blocks), table, in_w)
        blocks, arrived, begun = together(blocks, arrived, begun)
        arrived = scatter_all(second, range(3, tp), arrived)
    q, u, send = lr_mix(place, gain, begun, blocks, table, in_w, lr_short, rate)
    arrived, q, u, send = together(arrived, q, u, send)
    mids.append(as_mid(1, line_part(second, "tp", lax.axis_index("tp")), *arrived))
    blocks = line_gather(mids[1], "tp", 1, None)
    across = lax.ppermute(mids[1], "tp", [(0, 3), (3, 0)]) if tp == 4 else None
    sent = lax.all_gather(send, "ctx", axis=0)
    blocks, sent, q, u, across = together(blocks, sent, q, u, across)
    blocks = line_gather(mids[1], "tp", 2, blocks)
    lr_places, lr_weights = lr_w.places(lr_w.arrays), list(lr_w.arrays.values())
    modal_w = (lr_short, rate, res, lr_direct, width, lr_places, lr_weights, tp)
    first = lr_modal(position, q, u, sent, *modal_w)
    blocks, first = together(blocks, first)
    if tp == 4:
        blocks, across, first = together(blocks, across, first)
        share = scattered(first)
        begun = lr_in_start(place, gain, blocks, table, in_w)
        blocks = [*blocks, across]
    else:
        share = scattered(first)
        begun = lr_in_start(place, gain, blocks, table, in_w)
    q, u, send = lr_mix(place, gain, begun, blocks, table, in_w, lr_short, rate)
    sent = lax.all_gather(send, "ctx", axis=0)
    second = lr_modal(position, q, u, sent, *modal_w)
    out = (mids[0].astype(F32) + share.astype(F32)).astype(BF16)
    out, second = together(jnp.stack([out, mids[1]]), second)
    last = (out[1].astype(F32) + scattered(second).astype(F32)).astype(BF16)
    return out.at[1].set(last)


def solution(mesh):
    in_specs = (
        P(None, "ctx", "tp"),
        P(None, "ctx", None, "tp"),
        P(None, None, "tp"),
        P(None, "tp"),
        P("tp"),
        P("tp", "ctx"),
        P(),
        P(None, None, "tp"),
        P(None, None, "tp"),
        P(None, "tp"),
        P(None, "tp"),
        P("tp"),
        P("tp", "ctx"),
    )
    out_specs = P(None, "ctx", "tp")
    return jax.shard_map(local, mesh=mesh, in_specs=in_specs, out_specs=out_specs, check_vma=False)
```
